32 devices in a mesh: dp: 8 (over z, x), rep: 4 (over y, core).
Axes of the slice: x: 2, y: 2, z: 4, core: 2. Of those that a mesh axis runs over, the one named last changes fastest.
Arguments:
- tokens: bfloat16 [512, 256, 384], P(('dp', 'rep')), may hold values from -6 to 6
- conditioning: float32 [512, 384], P(('dp', 'rep')), may hold values from -6 to 6
- ada_weight: bfloat16 [384, 2304], P(None, 'dp'), may hold values from -0.3125 to 0.3125
- ada_bias: bfloat16 [2304], P('dp'), may hold values from -3 to 3
- qkv_weight: bfloat16 [384, 1152], P(None, 'dp'), may hold values from -0.3125 to 0.3125
- qv_bias: bfloat16 [768], P('dp'), may hold values from -3 to 3
- out_weight: bfloat16 [384, 384], P(None, 'dp'), may hold values from -1.25 to 1.25
- out_bias: bfloat16 [384], P('dp'), may hold values from -2 to 2
- up_weight: bfloat16 [384, 1536], P(None, 'dp'), may hold values from -0.3125 to 0.3125
- up_bias: bfloat16 [1536], P('dp'), may hold values from -3 to 3
- down_weight: bfloat16 [1536, 384], P(None, 'dp'), may hold values from -0.15625 to 0.15625
- down_bias: bfloat16 [384], P('dp'), may hold values from -2 to 2
- cotangent: bfloat16 [512, 256, 384], P(('dp', 'rep')), may hold values from -6 to 6
Outputs:
- output: bfloat16 [512, 256, 384], P(('dp', 'rep'))
- tokens_grad: bfloat16 [512, 256, 384], P(('dp', 'rep'))
- conditioning_grad: float32 [512, 384], P(('dp', 'rep'))
- ada_weight_grad: float32 [384, 2304], P(None, 'dp')
- ada_bias_grad: float32 [2304], P('dp')
- qkv_weight_grad: float32 [384, 1152], P(None, 'dp')
- qv_bias_grad: float32 [768], P('dp')
- out_weight_grad: float32 [384, 384], P(None, 'dp')
- out_bias_grad: float32 [384], P('dp')
- up_weight_grad: float32 [384, 1536], P(None, 'dp')
- up_bias_grad: float32 [1536], P('dp')
- down_weight_grad: float32 [1536, 384], P(None, 'dp')
- down_bias_grad: float32 [384], P('dp')
The draws below stay inside these ranges and needn't reach their ends.
All inputs are finite; a program needn't handle non-finite values.
Results may differ from the reference program's by a relative error of at most 0.014.
The reference program's roundings to bfloat16 on the way count: a program that leaves them out, or rounds other values in their place, can miss the bound.
Values may be sent and summed in bfloat16 or wider, within the bound.
No kernel may reach another device: no remote copies, remote signals or barrier semaphores. Data moves between devices by JAX's collectives and lax.ppermute only.
A program may use at most 256 MiB of HBM per device.

```python
import jax
import jax.numpy as jnp
from jax import lax

D = 384
HEAD_DIM = 64
FF = 1536
LEN = 256
SEQ_DEV = 16
SEQS = 512


def raised(entries, stream_key, source, target, shards_of, factor):
    def block_of(position):
        return (jnp.arange(entries.shape[position]) // (entries.shape[position] // shards_of)).reshape((-1,) + (1,) * (entries.ndim - 1 - position))

    near = jax.random.permutation(stream_key, shards_of)[block_of(target)]
    second = (block_of(target) + shards_of // 2) % shards_of
    return jnp.where((block_of(source) == near) | (block_of(source) == second), factor * entries, entries)


def level_of(stream_key, extent, pieces, least, high):
    def one(axis_at, blocks):
        steps = jax.random.uniform(jax.random.fold_in(jax.random.fold_in(stream_key, 6), axis_at), (blocks,), jnp.float32, least / len(pieces), high / len(pieces))
        return jnp.repeat(jnp.exp(steps), extent[axis_at] // blocks).reshape((-1,) + (1,) * (len(extent) - axis_at - 1))

    loudness = one(*pieces[0])
    for cut in pieces[1:]:
        loudness = loudness * one(*cut)
    return loudness


def normal_values(own_key, shape, scale, reach, shards=(), kind=jnp.bfloat16):
    entries = scale * jax.random.normal(own_key, shape, jnp.float32)
    if shards:
        entries = entries * level_of(own_key, shape, shards, -0.22, 0.18)
    return jnp.clip(entries, -reach, reach).astype(kind)


def gaussian_with(stream_key, dims, scale, limit, pieces, heavy, held_as=jnp.bfloat16):
    values = scale * jax.random.normal(stream_key, dims, jnp.float32)
    if pieces:
        values = values * level_of(stream_key, dims, pieces, -0.22, 0.18)
    return jnp.clip(raised(values, jax.random.fold_in(stream_key, 3), *heavy), -limit, limit).astype(held_as)


def setup_inputs(seed: int = 0) -> dict:
    splits = jax.random.split(jax.random.key(seed), 14)
    tokens = normal_values(splits[0], (SEQS, LEN, D), 1.0, 6.0, ((0, 32),))
    conditioning = normal_values(splits[1], (SEQS, D), 1.0, 6.0, ((0, 32),), jnp.float32)
    ada_weight = normal_values(splits[2], (D, 6 * D), D ** -0.5, 0.3125, ((1, 8),))
    ada_bias = normal_values(splits[3], (6 * D,), 0.5, 3.0, ((0, 8),))
    qkv_weight = normal_values(splits[4], (D, 3 * D), D ** -0.5, 0.3125, ((1, 8),))
    qv_bias = normal_values(splits[5], (2 * D,), 0.5, 3.0, ((0, 8),))
    out_weight = normal_values(splits[6], (D, D), (D // 16) ** -0.5, 1.25, ((1, 8),))
    out_bias = normal_values(splits[7], (D,), 0.3, 2.0, ((0, 8),))
    up_weight = normal_values(splits[8], (D, FF), D ** -0.5, 0.3125, ((1, 8),))
    up_bias = normal_values(splits[9], (FF,), 0.5, 3.0, ((0, 8),))
    down_weight = normal_values(splits[10], (FF, D), FF ** -0.5, 0.15625, ((1, 8),))
    down_bias = normal_values(splits[11], (D,), 0.3, 2.0, ((0, 8),))
    cotangent = gaussian_with(splits[12], (SEQS, LEN, D), 1.0, 6.0, ((0, 32),), (0, 2, 32, 2.75))
    return {"tokens": tokens, "conditioning": conditioning, "ada_weight": ada_weight, "ada_bias": ada_bias, "qkv_weight": qkv_weight, "qv_bias": qv_bias, "out_weight": out_weight, "out_bias": out_bias, "up_weight": up_weight, "up_bias": up_bias, "down_weight": down_weight, "down_bias": down_bias, "cotangent": cotangent}


@jax.custom_vjp
def low(v):
    return lax.optimization_barrier(v.astype(jnp.bfloat16)).astype(jnp.float32)

@jax.custom_vjp
def low_back(v):
    return v

def low_keep(v):
    return (low(v), None)

def low_pass(kept, grad):
    return (grad,)

def back_keep(v):
    return (v, None)

def back_low(kept, grad):
    return (low(grad),)
low.defvjp(low_keep, low_pass)
low_back.defvjp(back_keep, back_low)

def modulate(values, shift, scale):
    average = lax.optimization_barrier(jnp.mean(values, axis=-1, keepdims=True))
    centred = values - average
    spread = lax.optimization_barrier(jnp.mean(centred * centred, axis=-1, keepdims=True))
    return centred * lax.rsqrt(spread + 1e-06) * (1.0 + scale[:, None, :]) + shift[:, None, :]

def layer(params, values, condition):
    ada_weight, ada_bias, qkv_weight, qv_bias, out_weight, out_bias, up_weight, up_bias, down_weight, down_bias = params
    highest = lax.Precision.HIGHEST
    groups, length, width = values.shape
    heads = width // HEAD_DIM
    modulation = jnp.dot(low(jax.nn.silu(condition)), ada_weight, precision=highest) + ada_bias
    shift_one, scale_one, gate_one, shift_two, scale_two, gate_two = jnp.split(modulation, 6, axis=-1)
    normed_one = low(modulate(values, shift_one, scale_one))
    full_bias = jnp.concatenate([qv_bias[:width], jnp.zeros((width,), jnp.float32), qv_bias[width:]])
    qkv = low(low_back(jnp.einsum('gld,de->gle', normed_one, qkv_weight, precision=highest) + full_bias))
    queries = qkv[..., :width].reshape(groups, length, heads, HEAD_DIM)
    keys_in = qkv[..., width:2 * width].reshape(groups, length, heads, HEAD_DIM)
    values_in = qkv[..., 2 * width:].reshape(groups, length, heads, HEAD_DIM)
    scores = low_back(jnp.einsum('gqhe,gkhe->ghqk', queries, keys_in, precision=highest) * HEAD_DIM ** (-0.5))
    shifted = jnp.exp(scores - lax.optimization_barrier(jnp.max(scores, axis=-1, keepdims=True)))
    probs = low(shifted / lax.optimization_barrier(jnp.sum(shifted, axis=-1, keepdims=True)))
    attended = low(low_back(jnp.einsum('ghqk,gkhe->gqhe', probs, values_in, precision=highest)))
    attended = attended.reshape(groups, length, width)
    branch = low_back(jnp.einsum('gld,de->gle', attended, out_weight, precision=highest) + out_bias)
    middle = values + gate_one[:, None, :] * branch
    normed_two = low(modulate(middle, shift_two, scale_two))
    hidden = low_back(jnp.einsum('gld,di->gli', normed_two, up_weight, precision=highest) + up_bias)
    active = low(jax.nn.gelu(hidden, approximate=True))
    feed = low_back(jnp.einsum('gli,id->gld', active, down_weight, precision=highest) + down_bias)
    return middle + gate_two[:, None, :] * feed

def reference(tokens, conditioning, ada_weight, ada_bias, qkv_weight, qv_bias, out_weight, out_bias, up_weight, up_bias, down_weight, down_bias, cotangent):
    params = (ada_weight.astype(jnp.float32), ada_bias.astype(jnp.float32), qkv_weight.astype(jnp.float32), qv_bias.astype(jnp.float32), out_weight.astype(jnp.float32), out_bias.astype(jnp.float32), up_weight.astype(jnp.float32), up_bias.astype(jnp.float32), down_weight.astype(jnp.float32), down_bias.astype(jnp.float32))
    seqs_all, length, width = tokens.shape
    blocks = seqs_all // SEQ_DEV
    values = tokens.astype(jnp.float32).reshape(blocks, SEQ_DEV, length, width)
    incoming = cotangent.astype(jnp.float32).reshape(blocks, SEQ_DEV, length, width)
    condition = conditioning.astype(jnp.float32).reshape(blocks, SEQ_DEV, width)

    def step(totals, item):
        block_values, block_condition, block_incoming = item
        result, pull = jax.vjp(layer, params, block_values, block_condition)
        grad_params, grad_values, grad_condition = pull(block_incoming)
        totals = tuple((left + right for left, right in zip(totals, grad_params)))
        return (totals, (result, grad_values, grad_condition))
    start = tuple((jnp.zeros_like(param) for param in params))
    totals, (results, grad_values, grad_condition) = lax.scan(step, start, (values, condition, incoming))
    return (results.reshape(seqs_all, length, width).astype(jnp.bfloat16), grad_values.reshape(seqs_all, length, width).astype(jnp.bfloat16), grad_condition.reshape(seqs_all, width), totals[0], totals[1], totals[2], totals[3], totals[4], totals[5], totals[6], totals[7], totals[8], totals[9])
```

```python
import functools

import jax
import jax.numpy as jnp
from jax import lax
from jax.experimental import pallas as pl
from jax.experimental.pallas import tpu as pltpu
from jax.sharding import PartitionSpec as P

HEAD_DIM = 64
EPS = 1e-06
GELU_C = 0.7978845608028654
VMEM_LIMIT = 56 * 1024 * 1024
F32 = jnp.float32
BF16 = jnp.bfloat16


def dot_nn(left, right):
    return lax.dot_general(left, right, (((1,), (0,)), ((), ())), preferred_element_type=F32)


def dot_nt(left, right):
    return lax.dot_general(left, right, (((1,), (1,)), ((), ())), preferred_element_type=F32)


def dot_tn(left, right):
    return lax.dot_general(left, right, (((0,), (0,)), ((), ())), preferred_element_type=F32)


def normalise(values):
    average = jnp.mean(values, axis=-1, keepdims=True)
    centred = values - average
    spread = jnp.mean(centred * centred, axis=-1, keepdims=True)
    inverse = lax.rsqrt(spread + EPS)
    return centred * inverse, inverse


def normalise_back(upstream, normal, inverse):
    first = jnp.mean(upstream, axis=-1, keepdims=True)
    second = jnp.mean(upstream * normal, axis=-1, keepdims=True)
    return inverse * (upstream - first - normal * second)


def lane_low(shape):
    return lax.broadcasted_iota(jnp.int32, shape, 1) < HEAD_DIM


def attention_forward_kernel(
    tokens_ref, mod_ref, weight_ref, bias_ref, normed_ref, qkv_ref, lse_ref, attended_ref
):
    latents, length, width = tokens_ref.shape
    pairs = width // (2 * HEAD_DIM)
    mask = lane_low((length, 2 * HEAD_DIM))
    for latent in range(latents):
        normal, _ = normalise(tokens_ref[latent].astype(F32))
        normed = normal * (1.0 + mod_ref[latent, 1:2, :]) + mod_ref[latent, 0:1, :]
        normed = normed.astype(BF16)
        normed_ref[latent] = normed
        qkv = (dot_nt(normed, weight_ref[...]) + bias_ref[...]).astype(BF16)
        qkv_ref[latent] = qkv
        for pair in range(pairs):
            low = pair * 2 * HEAD_DIM
            high = low + 2 * HEAD_DIM
            queries = qkv[:, low:high]
            keys_in = qkv[:, width + low : width + high]
            values_in = qkv[:, 2 * width + low : 2 * width + high]
            halves = []
            for side in range(2):
                keep = mask if side == 0 else jnp.logical_not(mask)
                keys_side = jnp.where(keep, keys_in, jnp.zeros_like(keys_in))
                scores = dot_nt(keys_side, queries) * HEAD_DIM ** (-0.5)
                highest = jnp.max(scores, axis=0, keepdims=True)
                shifted = jnp.exp(scores - highest)
                total = jnp.sum(shifted, axis=0, keepdims=True)
                probs = (shifted * (1.0 / total)).astype(BF16)
                lse_ref[latent, 2 * pair + side : 2 * pair + side + 1, :] = highest + jnp.log(total)
                halves.append(dot_tn(probs, values_in))
            attended_ref[latent, :, low:high] = jnp.where(mask, halves[0], halves[1]).astype(BF16)


def feed_kernel(
    tokens_ref,
    cotangent_ref,
    attended_ref,
    mod_ref,
    out_weight_ref,
    out_bias_ref,
    up_weight_ref,
    up_bias_ref,
    down_weight_ref,
    down_bias_ref,
    output_ref,
    grad_middle_ref,
    grad_attended_ref,
    grad_mod_ref,
    out_grad_ref,
    up_grad_ref,
    down_grad_ref,
    bias_grad_ref,
    out_acc,
    up_acc,
    down_acc,
    bias_acc,
    *,
    chunk,
):
    step = pl.program_id(0)
    length, width = tokens_ref.shape[1:]
    hidden_width = up_weight_ref.shape[0]

    @pl.when(step == 0)
    def _():
        out_acc[...] = jnp.zeros_like(out_acc)
        up_acc[...] = jnp.zeros_like(up_acc)
        down_acc[...] = jnp.zeros_like(down_acc)
        bias_acc[...] = jnp.zeros_like(bias_acc)

    gate_one = mod_ref[0, 2:3, :]
    shift_two = mod_ref[0, 3:4, :]
    scale_two = 1.0 + mod_ref[0, 4:5, :]
    gate_two = mod_ref[0, 5:6, :]
    attended = attended_ref[0]
    branch = dot_nt(attended, out_weight_ref[...]) + out_bias_ref[...]
    middle = tokens_ref[0].astype(F32) + gate_one * branch
    normal, inverse = normalise(middle)
    normed = (normal * scale_two + shift_two).astype(BF16)
    incoming = cotangent_ref[0].astype(F32)
    grad_feed = (incoming * gate_two).astype(BF16)
    bias_acc[0:1, :width] += jnp.sum(grad_feed.astype(F32), axis=0, keepdims=True)

    feed = jnp.zeros((length, width), F32)
    grad_normed = jnp.zeros((length, width), F32)
    for low in range(0, hidden_width, chunk):
        high = low + chunk
        hidden = dot_nt(normed, up_weight_ref[low:high, :]) + up_bias_ref[:, low:high]
        square = hidden * hidden
        bent = jnp.tanh(hidden * (GELU_C + (GELU_C * 0.044715) * square))
        half = 0.5 + 0.5 * bent
        active = (hidden * half).astype(BF16)
        slope = half + hidden * (0.5 - 0.5 * (bent * bent)) * (
            GELU_C + (3.0 * GELU_C * 0.044715) * square
        )
        feed += dot_nt(active, down_weight_ref[:, low:high])
        grad_active = dot_nn(grad_feed, down_weight_ref[:, low:high])
        grad_hidden_wide = grad_active * slope
        grad_hidden = grad_hidden_wide.astype(BF16)
        bias_acc[2:3, low:high] += jnp.sum(grad_hidden.astype(F32), axis=0, keepdims=True)
        grad_normed += dot_nn(grad_hidden, up_weight_ref[low:high, :])
        up_acc[:, low:high] += dot_tn(normed, grad_hidden)
        down_acc[:, low:high] += dot_tn(grad_feed, active)

    feed = feed + down_bias_ref[...]
    output_ref[0] = (middle + gate_two * feed).astype(BF16)
    grad_mod_ref[0, 3:4, :] = jnp.sum(incoming * feed, axis=0, keepdims=True)
    grad_mod_ref[0, 1:2, :] = jnp.sum(grad_normed, axis=0, keepdims=True)
    grad_mod_ref[0, 2:3, :] = jnp.sum(grad_normed * normal, axis=0, keepdims=True)
    grad_middle = incoming + normalise_back(grad_normed * scale_two, normal, inverse)
    grad_middle_ref[0] = grad_middle
    grad_branch = (grad_middle * gate_one).astype(BF16)
    grad_mod_ref[0, 0:1, :] = jnp.sum(grad_middle * branch, axis=0, keepdims=True)
    bias_acc[1:2, :width] += jnp.sum(grad_branch.astype(F32), axis=0, keepdims=True)
    grad_attended_ref[0] = dot_nn(grad_branch, out_weight_ref[...]).astype(BF16)
    out_acc[...] += dot_tn(grad_branch, attended)

    @pl.when(step == pl.num_programs(0) - 1)
    def _():
        out_grad_ref[...] = out_acc[...].astype(BF16)
        up_grad_ref[...] = up_acc[...].T.astype(BF16)
        down_grad_ref[...] = down_acc[...].astype(BF16)
        bias_grad_ref[...] = bias_acc[...]


def attention_backward_kernel(
    qkv_ref,
    lse_ref,
    grad_attended_ref,
    normed_ref,
    grad_qkv_ref,
    weight_grad_ref,
    bias_grad_ref,
    acc,
    bias_acc,
):
    step = pl.program_id(0)
    length, width = grad_attended_ref.shape[1:]
    pairs = width // (2 * HEAD_DIM)
    mask = lane_low((length, 2 * HEAD_DIM))

    @pl.when(step == 0)
    def _():
        acc[...] = jnp.zeros_like(acc)
        bias_acc[...] = jnp.zeros_like(bias_acc)

    for pair in range(pairs):
        low = pair * 2 * HEAD_DIM
        high = low + 2 * HEAD_DIM
        queries = qkv_ref[0, :, low:high]
        keys_in = qkv_ref[0, :, width + low : width + high]
        values_in = qkv_ref[0, :, 2 * width + low : 2 * width + high]
        grad_out = grad_attended_ref[0, :, low:high]
        sides_q = []
        sides_k = []
        sides_v = []
        for side in range(2):
            keep = mask if side == 0 else jnp.logical_not(mask)
            keys_side = jnp.where(keep, keys_in, jnp.zeros_like(keys_in))
            values_side = jnp.where(keep, values_in, jnp.zeros_like(values_in))
            scores = dot_nt(keys_side, queries) * HEAD_DIM ** (-0.5)
            probs = jnp.exp(scores - lse_ref[0, 2 * pair + side : 2 * pair + side + 1, :])
            grad_probs = dot_nt(values_side, grad_out)
            row_terms = jnp.sum(probs * grad_probs, axis=0, keepdims=True)
            grad_scores = (probs * (grad_probs - row_terms)).astype(BF16)
            sides_v.append(dot_nn(probs.astype(BF16), grad_out))
            sides_k.append(dot_nn(grad_scores, queries))
            sides_q.append(dot_tn(grad_scores, keys_in))
        grad_qkv_ref[0, :, low:high] = (
            jnp.where(mask, sides_q[0], sides_q[1]) * HEAD_DIM ** (-0.5)
        ).astype(BF16)
        grad_qkv_ref[0, :, width + low : width + high] = (
            jnp.where(mask, sides_k[0], sides_k[1]) * HEAD_DIM ** (-0.5)
        ).astype(BF16)
        grad_qkv_ref[0, :, 2 * width + low : 2 * width + high] = jnp.where(
            mask, sides_v[0], sides_v[1]
        ).astype(BF16)
    grad_qkv = grad_qkv_ref[0]
    bias_acc[0:1, :] += jnp.sum(grad_qkv.astype(F32), axis=0, keepdims=True)
    acc[...] += dot_tn(normed_ref[0], grad_qkv)

    @pl.when(step == pl.num_programs(0) - 1)
    def _():
        weight_grad_ref[...] = acc[...].T.astype(BF16)
        bias_grad_ref[...] = bias_acc[...]


def first_norm_kernel(
    grad_qkv_ref, tokens_ref, grad_middle_ref, mod_ref, weight_ref, tokens_grad_ref, grad_mod_ref
):
    normal, inverse = normalise(tokens_ref[0].astype(F32))
    grad_normed = dot_nn(grad_qkv_ref[0], weight_ref[...])
    grad_mod_ref[0, 0:1, :] = jnp.sum(grad_normed, axis=0, keepdims=True)
    grad_mod_ref[0, 1:2, :] = jnp.sum(grad_normed * normal, axis=0, keepdims=True)
    upstream = grad_normed * (1.0 + mod_ref[0, 1:2, :])
    tokens_grad_ref[0] = (grad_middle_ref[0] + normalise_back(upstream, normal, inverse)).astype(
        BF16
    )


def each(shape):
    zeros = (0,) * (len(shape) - 1)
    return pl.BlockSpec((1,) + tuple(shape[1:]), lambda step: (step,) + zeros)


def whole(shape):
    zeros = (0,) * len(shape)
    return pl.BlockSpec(tuple(shape), lambda step: zeros)


def run_kernel(kernel, steps, streamed, fixed, streamed_out, fixed_out, scratch, order, cost):
    operands = [item for kind, item in order]
    in_specs = [each(item.shape) if kind == "s" else whole(item.shape) for kind, item in order]
    del streamed, fixed
    outs = list(streamed_out) + list(fixed_out)
    out_specs = [each(item.shape) for item in streamed_out] + [
        whole(item.shape) for item in fixed_out
    ]
    return pl.pallas_call(
        kernel,
        grid=(steps,),
        in_specs=in_specs,
        out_specs=out_specs,
        out_shape=outs,
        scratch_shapes=scratch,
        compiler_params=pltpu.CompilerParams(
            dimension_semantics=("arbitrary",), vmem_limit_bytes=VMEM_LIMIT
        ),
        cost_estimate=cost,
    )(*operands)


def shape_of(dims, kind):
    return jax.ShapeDtypeStruct(tuple(dims), kind)


def pair_shift(n_dp, n_rep, hop):
    return [
        (d * n_rep + r, ((d + hop) % n_dp) * n_rep + r) for d in range(n_dp) for r in range(n_rep)
    ]


def rep_shift(n_dp, n_rep, hop):
    return [(d * n_rep + r, d * n_rep + (r ^ hop)) for d in range(n_dp) for r in range(n_rep)]


AXES = ("dp", "rep")


def by_source(pieces, position):
    count = len(pieces)
    backwards = jnp.stack(pieces[::-1])
    twice = jnp.concatenate([backwards, backwards])
    return lax.dynamic_slice_in_dim(twice, count - 1 - position, count, axis=0)


def gather_halves(shard, n_dp, n_rep, axis):
    position = lax.axis_index("dp")
    core = lax.axis_index("rep") % 2
    half = shard.shape[axis] // 2
    mine = lax.dynamic_slice_in_dim(shard, core * half, half, axis=axis)
    pieces = [mine]
    for hop in range(1, n_dp):
        pieces.append(lax.ppermute(mine, AXES, pair_shift(n_dp, n_rep, hop)))
    stacked = by_source(pieces, position)
    other = lax.ppermute(stacked, AXES, rep_shift(n_dp, n_rep, 1))
    first = jnp.where(core == 0, stacked, other)
    second = jnp.where(core == 0, other, stacked)
    return jnp.concatenate([first, second], axis=axis + 1)


def exchange(blocks, n_dp, n_rep):
    position = lax.axis_index("dp")
    pieces = [lax.dynamic_index_in_dim(blocks, position, keepdims=False)]
    for hop in range(1, n_dp):
        target = (position + hop) % n_dp
        block = lax.dynamic_index_in_dim(blocks, target, keepdims=False)
        pieces.append(lax.ppermute(block, AXES, pair_shift(n_dp, n_rep, hop)))
    return by_source(pieces, position)


def spread_rep(value, n_dp, n_rep):
    place = lax.axis_index("rep")
    pieces = [value]
    for hop in range(1, n_rep):
        pieces.append(lax.ppermute(value, AXES, rep_shift(n_dp, n_rep, hop)))
    return jnp.stack([select_piece(pieces, place ^ r) for r in range(n_rep)])


def select_piece(pieces, index):
    chosen = pieces[0]
    for hop in range(1, len(pieces)):
        chosen = jnp.where(index == hop, pieces[hop], chosen)
    return chosen


def reduce_to_owner(blocks, n_dp, n_rep):
    place = lax.axis_index("rep")
    position = lax.axis_index("dp")
    total = lax.dynamic_index_in_dim(blocks, place, axis=1, keepdims=False).astype(F32)
    for hop in range(1, n_rep):
        block = lax.dynamic_index_in_dim(blocks, place ^ hop, axis=1, keepdims=False)
        total = total + lax.ppermute(block, AXES, rep_shift(n_dp, n_rep, hop)).astype(F32)
    total_low = total.astype(BF16)
    result = lax.dynamic_index_in_dim(total, position, keepdims=False)
    for hop in range(1, n_dp):
        block = lax.dynamic_index_in_dim(total_low, (position + hop) % n_dp, keepdims=False)
        result = result + lax.ppermute(block, AXES, pair_shift(n_dp, n_rep, hop)).astype(F32)
    return result


def quarters(grad, n_dp, n_rep):
    blocks = grad.reshape(n_dp, -1, grad.shape[-1])
    blocks = jnp.pad(blocks, ((0, 0), (0, -blocks.shape[1] % n_rep), (0, 0)))
    return blocks.reshape(n_dp, n_rep, -1, grad.shape[-1])


def body(
    n_dp,
    n_rep,
    tokens,
    conditioning,
    ada_weight,
    ada_bias,
    qkv_weight,
    qv_bias,
    out_weight,
    out_bias,
    up_weight,
    up_bias,
    down_weight,
    down_bias,
    cotangent,
):
    latents, length, width = tokens.shape
    hidden_width = up_weight.shape[1] * n_dp
    heads = width // HEAD_DIM
    rows = latents * length

    silu_low = jax.nn.silu(conditioning).astype(BF16)
    silu_group = exchange(jnp.broadcast_to(silu_low, (n_dp,) + silu_low.shape), n_dp, n_rep)
    mod_columns = jnp.dot(
        silu_group.reshape(n_dp * latents, width), ada_weight, preferred_element_type=F32
    ) + ada_bias.astype(F32)
    mod_parts = exchange(mod_columns.reshape(n_dp, latents, -1), n_dp, n_rep)
    modulation = mod_parts.transpose(1, 0, 2).reshape(latents, 6, width)

    bias_shard = jnp.concatenate([qv_bias, out_bias, up_bias, down_bias])
    bias_all = exchange(
        jnp.broadcast_to(bias_shard, (n_dp,) + bias_shard.shape), n_dp, n_rep
    ).astype(F32)
    cuts = [0]
    for part in (qv_bias, out_bias, up_bias, down_bias):
        cuts.append(cuts[-1] + part.shape[0])
    qv_full, out_full, up_full, down_full = (
        bias_all[:, low:high].reshape(1, -1) for low, high in zip(cuts[:-1], cuts[1:])
    )
    qkv_bias = jnp.concatenate(
        [qv_full[:, :width], jnp.zeros((1, width), F32), qv_full[:, width:]], axis=1
    )

    qkv_full = gather_halves(qkv_weight.T, n_dp, n_rep, 0).reshape(3 * width, width)
    out_wide, up_shard, down_shard, _ = lax.optimization_barrier(
        (out_weight.T, up_weight.T, down_weight.T, qkv_full)
    )
    out_all = gather_halves(out_wide, n_dp, n_rep, 0).reshape(width, width)
    up_all = gather_halves(up_shard, n_dp, n_rep, 0).reshape(hidden_width, width)
    down_all = gather_halves(down_shard, n_dp, n_rep, 1).reshape(width, hidden_width)

    normed, qkv, lse, attended = run_kernel(
        attention_forward_kernel,
        latents,
        None,
        None,
        [
            shape_of((latents, length, width), BF16),
            shape_of((latents, length, 3 * width), BF16),
            shape_of((latents, 8 * ((heads + 7) // 8), length), F32),
            shape_of((latents, length, width), BF16),
        ],
        [],
        [],
        [("s", tokens), ("s", modulation), ("f", qkv_full), ("f", qkv_bias)],
        pl.CostEstimate(
            flops=2 * rows * width * (3 * width + 2 * length),
            bytes_accessed=rows * width * 12,
            transcendentals=rows * heads * length,
        ),
    )

    (
        output,
        grad_middle,
        grad_attended,
        grad_mod_two,
        out_grad,
        up_grad,
        down_grad,
        bias_grad,
    ) = run_kernel(
        functools.partial(feed_kernel, chunk=512),
        latents,
        None,
        None,
        [
            shape_of((latents, length, width), BF16),
            shape_of((latents, length, width), F32),
            shape_of((latents, length, width), BF16),
            shape_of((latents, 4, width), F32),
        ],
        [
            shape_of((width, width), BF16),
            shape_of((hidden_width, width), BF16),
            shape_of((width, hidden_width), BF16),
            shape_of((8, hidden_width), F32),
        ],
        [
            pltpu.VMEM((width, width), F32),
            pltpu.VMEM((width, hidden_width), F32),
            pltpu.VMEM((width, hidden_width), F32),
            pltpu.VMEM((8, hidden_width), F32),
        ],
        [
            ("s", tokens),
            ("s", cotangent),
            ("s", attended),
            ("s", modulation),
            ("f", out_all),
            ("f", out_full),
            ("f", up_all),
            ("f", up_full),
            ("f", down_all),
            ("f", down_full),
        ],
        pl.CostEstimate(
            flops=6 * rows * width * (width + 2 * hidden_width),
            bytes_accessed=rows * width * 14,
            transcendentals=rows * hidden_width,
        ),
    )

    out_rows = width // n_dp
    up_rows = hidden_width // n_dp
    up_quarter = -(-up_rows // n_rep)
    down_quarter = hidden_width // n_rep
    up_blocks = quarters(up_grad, n_dp, n_rep)
    down_blocks = down_grad.reshape(n_dp, out_rows, n_rep, down_quarter).transpose(0, 2, 1, 3)
    out_blocks = quarters(out_grad, n_dp, n_rep)
    up_sum = reduce_to_owner(
        jnp.concatenate([up_blocks, out_blocks], axis=2), n_dp, n_rep
    )
    down_sum = reduce_to_owner(down_blocks, n_dp, n_rep)

    grad_qkv, qkv_grad, qkv_bias_grad = run_kernel(
        attention_backward_kernel,
        latents,
        None,
        None,
        [shape_of((latents, length, 3 * width), BF16)],
        [shape_of((3 * width, width), BF16), shape_of((8, 3 * width), F32)],
        [pltpu.VMEM((width, 3 * width), F32), pltpu.VMEM((8, 3 * width), F32)],
        [("s", qkv), ("s", lse), ("s", grad_attended), ("s", normed)],
        pl.CostEstimate(
            flops=2 * rows * width * (3 * width + 5 * length),
            bytes_accessed=rows * width * 16,
            transcendentals=rows * heads * length,
        ),
    )
    qkv_rows = 3 * width // n_dp
    qkv_sum = reduce_to_owner(quarters(qkv_grad, n_dp, n_rep), n_dp, n_rep)

    tokens_grad, grad_mod_one = run_kernel(
        first_norm_kernel,
        latents,
        None,
        None,
        [shape_of((latents, length, width), BF16), shape_of((latents, 2, width), F32)],
        [],
        [],
        [
            ("s", grad_qkv),
            ("s", tokens),
            ("s", grad_middle),
            ("s", modulation),
            ("f", qkv_full),
        ],
        pl.CostEstimate(
            flops=6 * rows * width * width, bytes_accessed=rows * width * 14, transcendentals=0
        ),
    )

    grad_modulation = jnp.concatenate([grad_mod_one, grad_mod_two], axis=1).reshape(
        latents, 6 * width
    )
    highest = lax.Precision.HIGHEST
    grad_columns = exchange(
        grad_modulation.reshape(latents, n_dp, -1).transpose(1, 0, 2), n_dp, n_rep
    ).reshape(n_dp * latents, -1)
    silu_wide = silu_group.reshape(n_dp * latents, width).astype(F32)
    ada_part = lax.dot_general(
        grad_columns, silu_wide, (((0,), (0,)), ((), ())), precision=highest
    )
    ada_bias_part = jnp.sum(grad_columns, axis=0)
    silu_part = lax.dot_general(
        grad_columns, ada_weight.astype(F32), (((1,), (1,)), ((), ())), precision=highest
    )
    grad_silu = jnp.sum(exchange(silu_part.reshape(n_dp, latents, width), n_dp, n_rep), axis=0)
    _, silu_pull = jax.vjp(jax.nn.silu, conditioning)
    condition_grad = silu_pull(grad_silu)[0]

    qkv_columns = qkv_bias_grad[0]
    qv_columns = jnp.concatenate([qkv_columns[:width], qkv_columns[2 * width :]])
    bias_blocks = jnp.concatenate(
        [
            qv_columns.reshape(n_dp, -1),
            bias_grad[1, :width].reshape(n_dp, -1),
            bias_grad[2].reshape(n_dp, -1),
            bias_grad[0, :width].reshape(n_dp, -1),
        ],
        axis=1,
    )
    bias_part = jnp.sum(exchange(bias_blocks, n_dp, n_rep), axis=0)

    ada_sum = jnp.sum(spread_rep(ada_part.astype(BF16), n_dp, n_rep).astype(F32), axis=0)
    small = jnp.concatenate([bias_part, ada_bias_part])
    small_sum = jnp.sum(spread_rep(small, n_dp, n_rep), axis=0)
    up_out = spread_rep(up_sum.astype(BF16), n_dp, n_rep).astype(F32)
    up_owned = up_out[:, :up_quarter].reshape(-1, width)[:up_rows]
    out_owned = up_out[:, up_quarter:].reshape(-1, width)[:out_rows]
    down_owned = (
        spread_rep(down_sum.astype(BF16), n_dp, n_rep)
        .astype(F32)
        .transpose(1, 0, 2)
        .reshape(out_rows, hidden_width)
    )
    qkv_owned = spread_rep(qkv_sum.astype(BF16), n_dp, n_rep).astype(F32)
    qkv_owned = qkv_owned.reshape(-1, width)[:qkv_rows]
    ends = list(cuts) + [cuts[-1] + ada_bias_part.shape[0]]
    qv_sum, out_bias_sum, up_bias_sum, down_bias_sum, ada_bias_sum = (
        small_sum[low:high] for low, high in zip(ends[:-1], ends[1:])
    )
    return (
        output,
        tokens_grad,
        condition_grad,
        ada_sum.T,
        ada_bias_sum,
        qkv_owned.T,
        qv_sum,
        out_owned.T,
        out_bias_sum,
        up_owned.T,
        up_bias_sum,
        down_owned.T,
        down_bias_sum,
    )


def solution(mesh):
    return jax.shard_map(
        functools.partial(body, mesh.shape["dp"], mesh.shape["rep"]),
        mesh=mesh,
        in_specs=(
            P(("dp", "rep"), None, None),
            P(("dp", "rep"), None),
            P(None, "dp"),
            P("dp"),
            P(None, "dp"),
            P("dp"),
            P(None, "dp"),
            P("dp"),
            P(None, "dp"),
            P("dp"),
            P(None, "dp"),
            P("dp"),
            P(("dp", "rep"), None, None),
        ),
        out_specs=(
            P(("dp", "rep"), None, None),
            P(("dp", "rep"), None, None),
            P(("dp", "rep"), None),
            P(None, "dp"),
            P("dp"),
            P(None, "dp"),
            P("dp"),
            P(None, "dp"),
            P("dp"),
            P(None, "dp"),
            P("dp"),
            P(None, "dp"),
            P("dp"),
        ),
        check_vma=False,
    )
```

```python
import functools

import jax
import jax.numpy as jnp
from jax import lax
from jax.experimental import pallas as pl
from jax.experimental.pallas import tpu as pltpu
from jax.sharding import PartitionSpec as P

HEAD_DIM = 64
EPS = 1e-06
GELU_C = 0.7978845608028654
VMEM_LIMIT = 56 * 1024 * 1024
F32 = jnp.float32
BF16 = jnp.bfloat16


def dot_nn(left, right):
    return lax.dot_general(left, right, (((1,), (0,)), ((), ())), preferred_element_type=F32)


def dot_nt(left, right):
    return lax.dot_general(left, right, (((1,), (1,)), ((), ())), preferred_element_type=F32)


def dot_tn(left, right):
    return lax.dot_general(left, right, (((0,), (0,)), ((), ())), preferred_element_type=F32)


def normalise(values):
    average = jnp.mean(values, axis=-1, keepdims=True)
    centred = values - average
    spread = jnp.mean(centred * centred, axis=-1, keepdims=True)
    inverse = lax.rsqrt(spread + EPS)
    return centred * inverse, inverse


def normalise_back(upstream, normal, inverse):
    first = jnp.mean(upstream, axis=-1, keepdims=True)
    second = jnp.mean(upstream * normal, axis=-1, keepdims=True)
    return inverse * (upstream - first - normal * second)


def lane_low(shape):
    return lax.broadcasted_iota(jnp.int32, shape, 1) < HEAD_DIM


def attention_forward_kernel(
    tokens_ref, mod_ref, weight_ref, bias_ref, normed_ref, qkv_ref, lse_ref, attended_ref
):
    latents, length, width = tokens_ref.shape
    pairs = width // (2 * HEAD_DIM)
    mask = lane_low((length, 2 * HEAD_DIM))
    for latent in range(latents):
        normal, _ = normalise(tokens_ref[latent].astype(F32))
        normed = normal * (1.0 + mod_ref[latent, 1:2, :]) + mod_ref[latent, 0:1, :]
        normed = normed.astype(BF16)
        normed_ref[latent] = normed
        qkv = (dot_nt(normed, weight_ref[...]) + bias_ref[...]).astype(BF16)
        qkv_ref[latent] = qkv
        for pair in range(pairs):
            low = pair * 2 * HEAD_DIM
            high = low + 2 * HEAD_DIM
            queries = qkv[:, low:high]
            keys_in = qkv[:, width + low : width + high]
            values_in = qkv[:, 2 * width + low : 2 * width + high]
            halves = []
            for side in range(2):
                keep = mask if side == 0 else jnp.logical_not(mask)
                keys_side = jnp.where(keep, keys_in, jnp.zeros_like(keys_in))
                scores = dot_nt(keys_side, queries) * HEAD_DIM ** (-0.5)
                highest = jnp.max(scores, axis=0, keepdims=True)
                shifted = jnp.exp(scores - highest)
                total = jnp.sum(shifted, axis=0, keepdims=True)
                probs = (shifted * (1.0 / total)).astype(BF16)
                lse_ref[latent, 2 * pair + side : 2 * pair + side + 1, :] = highest + jnp.log(total)
                halves.append(dot_tn(probs, values_in))
            attended_ref[latent, :, low:high] = jnp.where(mask, halves[0], halves[1]).astype(BF16)


def feed_kernel(
    tokens_ref,
    cotangent_ref,
    attended_ref,
    mod_ref,
    out_weight_ref,
    out_bias_ref,
    up_weight_ref,
    up_bias_ref,
    down_weight_ref,
    down_bias_ref,
    output_ref,
    grad_middle_ref,
    grad_attended_ref,
    grad_mod_ref,
    out_grad_ref,
    up_grad_ref,
    down_grad_ref,
    bias_grad_ref,
    out_acc,
    up_acc,
    down_acc,
    bias_acc,
    *,
    chunk,
):
    step = pl.program_id(0)
    latents, length, width = tokens_ref.shape
    rows = latents * length
    hidden_width = up_weight_ref.shape[0]

    @pl.when(step == 0)
    def _():
        out_acc[...] = jnp.zeros_like(out_acc)
        up_acc[...] = jnp.zeros_like(up_acc)
        down_acc[...] = jnp.zeros_like(down_acc)
        bias_acc[...] = jnp.zeros_like(bias_acc)

    def flat(values):
        return values.reshape(rows, width)

    def deep(values):
        return values.reshape(latents, length, width)

    gate_one = mod_ref[:, 2:3, :]
    shift_two = mod_ref[:, 3:4, :]
    scale_two = 1.0 + mod_ref[:, 4:5, :]
    gate_two = mod_ref[:, 5:6, :]
    attended = flat(attended_ref[...])
    branch = deep(dot_nt(attended, out_weight_ref[...]) + out_bias_ref[...])
    middle = tokens_ref[...].astype(F32) + gate_one * branch
    normal, inverse = normalise(middle)
    normed = flat((normal * scale_two + shift_two).astype(BF16))
    incoming = cotangent_ref[...].astype(F32)
    grad_feed = flat((incoming * gate_two).astype(BF16))
    bias_acc[0:1, :width] += jnp.sum(grad_feed.astype(F32), axis=0, keepdims=True)

    feed = jnp.zeros((rows, width), F32)
    grad_normed = jnp.zeros((rows, width), F32)
    for low in range(0, hidden_width, chunk):
        high = low + chunk
        hidden = dot_nt(normed, up_weight_ref[low:high, :]) + up_bias_ref[:, low:high]
        square = hidden * hidden
        bent = jnp.tanh(hidden * (GELU_C + (GELU_C * 0.044715) * square))
        half = 0.5 + 0.5 * bent
        active = (hidden * half).astype(BF16)
        slope = half + hidden * (0.5 - 0.5 * (bent * bent)) * (
            GELU_C + (3.0 * GELU_C * 0.044715) * square
        )
        feed += dot_nt(active, down_weight_ref[:, low:high])
        grad_active = dot_nn(grad_feed, down_weight_ref[:, low:high])
        grad_hidden = (grad_active * slope).astype(BF16)
        bias_acc[2:3, low:high] += jnp.sum(grad_hidden.astype(F32), axis=0, keepdims=True)
        grad_normed += dot_nn(grad_hidden, up_weight_ref[low:high, :])
        up_acc[:, low:high] += dot_tn(normed, grad_hidden)
        down_acc[:, low:high] += dot_tn(grad_feed, active)

    feed = deep(feed + down_bias_ref[...])
    grad_normed = deep(grad_normed)
    output_ref[...] = (middle + gate_two * feed).astype(BF16)
    grad_mod_ref[:, 3:4, :] = jnp.sum(incoming * feed, axis=1, keepdims=True)
    grad_mod_ref[:, 1:2, :] = jnp.sum(grad_normed, axis=1, keepdims=True)
    grad_mod_ref[:, 2:3, :] = jnp.sum(grad_normed * normal, axis=1, keepdims=True)
    grad_middle = incoming + normalise_back(grad_normed * scale_two, normal, inverse)
    grad_middle_ref[...] = grad_middle
    grad_branch = flat((grad_middle * gate_one).astype(BF16))
    grad_mod_ref[:, 0:1, :] = jnp.sum(grad_middle * branch, axis=1, keepdims=True)
    bias_acc[1:2, :width] += jnp.sum(grad_branch.astype(F32), axis=0, keepdims=True)
    grad_attended_ref[...] = deep(dot_nn(grad_branch, out_weight_ref[...]).astype(BF16))
    out_acc[...] += dot_tn(grad_branch, attended)

    @pl.when(step == pl.num_programs(0) - 1)
    def _():
        out_grad_ref[...] = out_acc[...].astype(BF16)
        up_grad_ref[...] = up_acc[...].T.astype(BF16)
        down_grad_ref[...] = down_acc[...].astype(BF16)
        bias_grad_ref[...] = bias_acc[...]


def attention_backward_kernel(
    qkv_ref,
    lse_ref,
    grad_attended_ref,
    normed_ref,
    grad_qkv_ref,
    weight_grad_ref,
    bias_grad_ref,
    acc,
    bias_acc,
):
    step = pl.program_id(0)
    latents, length, width = grad_attended_ref.shape
    pairs = width // (2 * HEAD_DIM)
    mask = lane_low((length, 2 * HEAD_DIM))

    @pl.when(step == 0)
    def _():
        acc[...] = jnp.zeros_like(acc)
        bias_acc[...] = jnp.zeros_like(bias_acc)

    for latent in range(latents):
        for pair in range(pairs):
            low = pair * 2 * HEAD_DIM
            high = low + 2 * HEAD_DIM
            queries = qkv_ref[latent, :, low:high]
            keys_in = qkv_ref[latent, :, width + low : width + high]
            values_in = qkv_ref[latent, :, 2 * width + low : 2 * width + high]
            grad_out = grad_attended_ref[latent, :, low:high]
            sides_q = []
            sides_k = []
            sides_v = []
            for side in range(2):
                keep = mask if side == 0 else jnp.logical_not(mask)
                keys_side = jnp.where(keep, keys_in, jnp.zeros_like(keys_in))
                values_side = jnp.where(keep, values_in, jnp.zeros_like(values_in))
                scores = dot_nt(keys_side, queries) * HEAD_DIM ** (-0.5)
                head = 2 * pair + side
                probs = jnp.exp(scores - lse_ref[latent, head : head + 1, :])
                grad_probs = dot_nt(values_side, grad_out)
                row_terms = jnp.sum(probs * grad_probs, axis=0, keepdims=True)
                grad_scores = (probs * (grad_probs - row_terms)).astype(BF16)
                sides_v.append(dot_nn(probs.astype(BF16), grad_out))
                sides_k.append(dot_nn(grad_scores, queries))
                sides_q.append(dot_tn(grad_scores, keys_in))
            grad_qkv_ref[latent, :, low:high] = (
                jnp.where(mask, sides_q[0], sides_q[1]) * HEAD_DIM ** (-0.5)
            ).astype(BF16)
            grad_qkv_ref[latent, :, width + low : width + high] = (
                jnp.where(mask, sides_k[0], sides_k[1]) * HEAD_DIM ** (-0.5)
            ).astype(BF16)
            grad_qkv_ref[latent, :, 2 * width + low : 2 * width + high] = jnp.where(
                mask, sides_v[0], sides_v[1]
            ).astype(BF16)
    grad_qkv = grad_qkv_ref[...].reshape(latents * length, 3 * width)
    bias_acc[0:1, :] += jnp.sum(grad_qkv.astype(F32), axis=0, keepdims=True)
    acc[...] += dot_tn(normed_ref[...].reshape(latents * length, width), grad_qkv)

    @pl.when(step == pl.num_programs(0) - 1)
    def _():
        weight_grad_ref[...] = acc[...].T.astype(BF16)
        bias_grad_ref[...] = bias_acc[...]


def first_norm_kernel(
    grad_qkv_ref, tokens_ref, grad_middle_ref, mod_ref, weight_ref, tokens_grad_ref, grad_mod_ref
):
    latents, length, width = tokens_ref.shape
    grad_qkv = grad_qkv_ref[...].reshape(latents * length, 3 * width)
    grad_normed_all = dot_nn(grad_qkv, weight_ref[...])
    for latent in range(latents):
        normal, inverse = normalise(tokens_ref[latent].astype(F32))
        grad_normed = grad_normed_all[latent * length : (latent + 1) * length]
        grad_mod_ref[latent, 0:1, :] = jnp.sum(grad_normed, axis=0, keepdims=True)
        grad_mod_ref[latent, 1:2, :] = jnp.sum(grad_normed * normal, axis=0, keepdims=True)
        upstream = grad_normed * (1.0 + mod_ref[latent, 1:2, :])
        tokens_grad_ref[latent] = (
            grad_middle_ref[latent] + normalise_back(upstream, normal, inverse)
        ).astype(BF16)


def each(shape, count):
    zeros = (0,) * (len(shape) - 1)
    return pl.BlockSpec((count,) + tuple(shape[1:]), lambda step: (step,) + zeros)


def whole(shape):
    zeros = (0,) * len(shape)
    return pl.BlockSpec(tuple(shape), lambda step: zeros)


def run_kernel(kernel, count, streamed_out, fixed_out, scratch, streamed, fixed, cost):
    return pl.pallas_call(
        kernel,
        grid=(streamed[0].shape[0] // count,),
        in_specs=[each(item.shape, count) for item in streamed]
        + [whole(item.shape) for item in fixed],
        out_specs=[each(item.shape, count) for item in streamed_out]
        + [whole(item.shape) for item in fixed_out],
        out_shape=list(streamed_out) + list(fixed_out),
        scratch_shapes=scratch,
        compiler_params=pltpu.CompilerParams(
            dimension_semantics=("arbitrary",), vmem_limit_bytes=VMEM_LIMIT
        ),
        cost_estimate=cost,
    )(*streamed, *fixed)


def shape_of(dims, kind):
    return jax.ShapeDtypeStruct(tuple(dims), kind)


AXES = ("dp", "rep")


class Hops:
    def __init__(self, n_dp, n_rep):
        self.sizes = {"dp": n_dp, "rep": n_rep}
        self.place = {name: lax.axis_index(name) for name in AXES}

    def bits(self, name):
        return [1 << shift for shift in range(self.sizes[name].bit_length() - 1)]

    def mine(self, name, bit):
        return (self.place[name] // bit) % 2

    def swap(self, value, name, bit):
        n_dp, n_rep = self.sizes["dp"], self.sizes["rep"]
        flip_dp, flip_rep = (bit, 0) if name == "dp" else (0, bit)
        pairs = [
            (d * n_rep + r, (d ^ flip_dp) * n_rep + (r ^ flip_rep))
            for d in range(n_dp)
            for r in range(n_rep)
        ]
        return lax.ppermute(value, AXES, pairs)

    def both(self, kept, came, name, bit, axis):
        upper = self.mine(name, bit) == 1
        return jnp.stack(
            [jnp.where(upper, came, kept), jnp.where(upper, kept, came)], axis=axis
        )

    def cut(self, value, name, bit, axis):
        here = self.mine(name, bit)
        return (
            lax.dynamic_index_in_dim(value, here, axis, keepdims=False),
            lax.dynamic_index_in_dim(value, 1 - here, axis, keepdims=False),
        )


def pad_rows(values, count):
    return jnp.pad(values, ((0, 0),) * (values.ndim - 2) + ((0, count - values.shape[-2]), (0, 0)))


def up_to(count, multiple):
    return -(-count // multiple) * multiple


def body(
    n_dp,
    n_rep,
    tokens,
    conditioning,
    ada_weight,
    ada_bias,
    qkv_weight,
    qv_bias,
    out_weight,
    out_bias,
    up_weight,
    up_bias,
    down_weight,
    down_bias,
    cotangent,
):
    latents, length, width = tokens.shape
    hidden_width = up_weight.shape[1] * n_dp
    heads = width // HEAD_DIM
    rows = latents * length
    hops = Hops(n_dp, n_rep)
    dp_bits = hops.bits("dp")
    folds = hidden_width // width

    up_rows, out_rows = up_weight.shape[1], out_weight.shape[1]
    down_shard = down_weight.T.reshape(out_rows, folds, width).transpose(1, 0, 2)
    late_shard = jnp.concatenate(
        [up_weight.T, down_shard.reshape(folds * out_rows, width), out_weight.T]
    )
    late = lax.all_gather(late_shard, "dp", axis=0)
    up_all = late[:, :up_rows].reshape(hidden_width, width)
    down_all = late[:, up_rows : up_rows + folds * out_rows]
    down_all = down_all.reshape(n_dp, folds, out_rows, width).transpose(0, 2, 1, 3)
    down_all = down_all.reshape(width, hidden_width)
    out_all = late[:, up_rows + folds * out_rows :].reshape(width, width)
    silu_low = jax.nn.silu(conditioning).astype(BF16)
    ada_shard, silu_shard, _ = lax.optimization_barrier((ada_weight.T, silu_low, late))
    ada_all = lax.all_gather(ada_shard, "dp", axis=0, tiled=True)
    silu_all = lax.all_gather(silu_shard, AXES, axis=0, tiled=True)

    qkv_rows = qkv_weight.shape[1]
    half_rows = qkv_rows // 2
    core = hops.mine("rep", 1)
    bias_shard = jnp.concatenate([qv_bias, out_bias, up_bias, down_bias])
    bias_rows = up_to(bias_shard.shape[0], width) // width
    bias_block = jnp.pad(bias_shard, (0, bias_rows * width - bias_shard.shape[0]))
    front = jnp.concatenate(
        [
            lax.dynamic_slice_in_dim(qkv_weight.T, core * half_rows, half_rows, axis=0),
            silu_low,
            bias_block.reshape(bias_rows, width),
        ]
    )
    front = pad_rows(front, up_to(front.shape[0], 8))
    for done, bit in enumerate(dp_bits[::-1]):
        front = hops.both(front, hops.swap(front, "dp", bit), "dp", bit, done)
    front = front.reshape(n_dp, -1, width)
    halves = front[:, :half_rows]
    halves = hops.both(halves, hops.swap(halves, "rep", 1), "rep", 1, 1)
    qkv_full = halves.reshape(3 * width, width)
    silu_group = front[:, half_rows : half_rows + latents].reshape(n_dp * latents, width)

    bias_all = front[:, half_rows + latents : half_rows + latents + bias_rows]
    bias_all = bias_all.reshape(n_dp, -1).astype(F32)
    cuts = [0]
    for part in (qv_bias, out_bias, up_bias, down_bias):
        cuts.append(cuts[-1] + part.shape[0])
    qv_full, out_full, up_full, down_full = (
        bias_all[:, low:high].reshape(1, -1) for low, high in zip(cuts[:-1], cuts[1:])
    )
    qkv_bias = jnp.concatenate(
        [qv_full[:, :width], jnp.zeros((1, width), F32), qv_full[:, width:]], axis=1
    )

    mod = jnp.dot(silu_group, ada_weight, preferred_element_type=F32) + ada_bias.astype(F32)
    mod = mod.reshape((2,) * len(dp_bits) + (latents, -1))
    for done, bit in enumerate(dp_bits[::-1]):
        kept, sent = hops.cut(mod, "dp", bit, done)
        mod = hops.both(kept, hops.swap(sent, "dp", bit), "dp", bit, done)
    modulation = mod.reshape(n_dp, latents, -1).transpose(1, 0, 2).reshape(latents, 6, width)

    normed, qkv, lse, attended = run_kernel(
        attention_forward_kernel,
        2,
        [
            shape_of((latents, length, width), BF16),
            shape_of((latents, length, 3 * width), BF16),
            shape_of((latents, 8 * ((heads + 7) // 8), length), F32),
            shape_of((latents, length, width), BF16),
        ],
        [],
        [],
        [tokens, modulation],
        [qkv_full, qkv_bias],
        pl.CostEstimate(
            flops=2 * rows * width * (3 * width + 2 * length),
            bytes_accessed=rows * width * 12,
            transcendentals=rows * heads * length,
        ),
    )

    (
        output,
        grad_middle,
        grad_attended,
        grad_mod_two,
        out_grad,
        up_grad,
        down_grad,
        bias_grad,
    ) = run_kernel(
        functools.partial(feed_kernel, chunk=512),
        2,
        [
            shape_of((latents, length, width), BF16),
            shape_of((latents, length, width), F32),
            shape_of((latents, length, width), BF16),
            shape_of((latents, 4, width), F32),
        ],
        [
            shape_of((width, width), BF16),
            shape_of((hidden_width, width), BF16),
            shape_of((width, hidden_width), BF16),
            shape_of((8, hidden_width), F32),
        ],
        [
            pltpu.VMEM((width, width), F32),
            pltpu.VMEM((width, hidden_width), F32),
            pltpu.VMEM((width, hidden_width), F32),
            pltpu.VMEM((8, hidden_width), F32),
        ],
        [tokens, cotangent, attended, modulation],
        [out_all, out_full, up_all, up_full, down_all, down_full],
        pl.CostEstimate(
            flops=6 * rows * width * (width + 2 * hidden_width),
            bytes_accessed=rows * width * 14,
            transcendentals=rows * hidden_width,
        ),
    )

    late_grad = jnp.concatenate(
        [
            up_grad.reshape(n_dp, up_rows, width),
            down_grad.reshape(n_dp, out_rows, folds, width)
            .transpose(0, 2, 1, 3)
            .reshape(n_dp, folds * out_rows, width),
            out_grad.reshape(n_dp, out_rows, width),
        ],
        axis=1,
    )
    late_sum = lax.psum_scatter(late_grad, "dp", scatter_dimension=0, tiled=True)
    late_sum = lax.psum(late_sum, "rep").astype(F32).reshape(-1, width)
    up_owned = late_sum[:up_rows]
    down_owned = late_sum[up_rows : up_rows + folds * out_rows]
    down_owned = down_owned.reshape(folds, out_rows, width).transpose(1, 0, 2)
    down_owned = down_owned.reshape(out_rows, hidden_width)
    out_owned = late_sum[up_rows + folds * out_rows :]

    grad_qkv, qkv_grad, qkv_bias_grad = run_kernel(
        attention_backward_kernel,
        2,
        [shape_of((latents, length, 3 * width), BF16)],
        [shape_of((3 * width, width), BF16), shape_of((8, 3 * width), F32)],
        [pltpu.VMEM((width, 3 * width), F32), pltpu.VMEM((8, 3 * width), F32)],
        [qkv, lse, grad_attended, normed],
        [],
        pl.CostEstimate(
            flops=2 * rows * width * (3 * width + 5 * length),
            bytes_accessed=rows * width * 16,
            transcendentals=rows * heads * length,
        ),
    )

    qkv_columns = qkv_bias_grad[0]
    bias_blocks = jnp.concatenate(
        [
            jnp.concatenate([qkv_columns[:width], qkv_columns[2 * width :]]).reshape(n_dp, -1),
            bias_grad[1, :width].reshape(n_dp, -1),
            bias_grad[2].reshape(n_dp, -1),
            bias_grad[0, :width].reshape(n_dp, -1),
        ],
        axis=1,
    ).astype(BF16)
    bias_part = up_to(cuts[-1], n_rep) // n_rep
    bias_blocks = jnp.pad(bias_blocks, ((0, 0), (0, bias_part * n_rep - cuts[-1])))
    bias_blocks = bias_blocks.reshape(n_dp, n_rep, 1, bias_part)
    bias_blocks = jnp.pad(bias_blocks, ((0, 0), (0, 0), (0, 0), (0, width - bias_part)))
    quarter = up_to(qkv_rows, n_rep) // n_rep
    tail_rows = up_to(quarter + 1, 8)
    blocks = pad_rows(qkv_grad.reshape(n_dp, qkv_rows, width), quarter * n_rep)
    blocks = jnp.concatenate([blocks.reshape(n_dp, n_rep, quarter, width), bias_blocks], axis=2)
    blocks = pad_rows(blocks, tail_rows)
    rep_bits = hops.bits("rep")
    total = blocks.reshape((n_dp,) + (2,) * len(rep_bits) + (tail_rows, width))
    for bit in rep_bits:
        kept, sent = hops.cut(total, "rep", bit, total.ndim - 3)
        total = kept.astype(F32) + hops.swap(sent.astype(BF16), "rep", bit).astype(F32)

    tokens_grad, grad_mod_one = run_kernel(
        first_norm_kernel,
        2,
        [shape_of((latents, length, width), BF16), shape_of((latents, 2, width), F32)],
        [],
        [],
        [grad_qkv, tokens, grad_middle, modulation],
        [qkv_full],
        pl.CostEstimate(
            flops=6 * rows * width * width, bytes_accessed=rows * width * 14, transcendentals=0
        ),
    )
    grad_modulation = jnp.concatenate([grad_mod_one, grad_mod_two], axis=1).reshape(
        latents, 6 * width
    )

    own = 6 * width // n_dp
    columns = grad_modulation.reshape(latents, n_dp, own).transpose(1, 0, 2).astype(BF16)
    columns = columns.reshape((2,) * len(dp_bits) + (latents * own,))
    total = total.reshape((2,) * len(dp_bits) + (tail_rows * width,))
    axis = len(dp_bits) - 1
    for bit in dp_bits:
        kept, sent = hops.cut(total, "dp", bit, axis)
        column_kept, column_sent = hops.cut(columns, "dp", bit, axis)
        lead = sent.shape[:axis]
        column_flat = column_sent.reshape(lead + (-1,))
        came = hops.swap(
            jnp.concatenate([sent.astype(BF16), column_flat], axis=-1), "dp", bit
        )
        total = kept.astype(F32) + came[..., : tail_rows * width].astype(F32)
        column_came = came[..., tail_rows * width :].reshape(column_kept.shape)
        columns = hops.both(column_kept, column_came, "dp", bit, axis)
        columns = jnp.moveaxis(columns, axis, columns.ndim - 2)
        axis -= 1
    order = tuple(range(len(dp_bits)))[::-1]
    columns = columns.transpose(order + (len(dp_bits),)).reshape(-1)
    final = jnp.concatenate([total.astype(BF16), columns])
    for done, bit in enumerate(rep_bits):
        final = hops.both(final, hops.swap(final, "rep", bit), "rep", bit, 0)
    final = final.reshape(n_rep, -1)
    summed = final[:, : tail_rows * width].reshape(n_rep, tail_rows, width).astype(F32)
    qkv_owned = summed[:, :quarter].reshape(-1, width)[:qkv_rows]
    bias_owned = summed[:, quarter, :bias_part].reshape(-1)
    columns = final[:, tail_rows * width :].reshape(n_rep, n_dp, latents, own)
    columns = columns.transpose(1, 0, 2, 3).reshape(n_dp * n_rep * latents, own)
    ada_grad = dot_tn(columns, silu_all)
    ada_bias_grad = jnp.sum(columns.astype(F32), axis=0)

    grad_silu = lax.dot_general(
        grad_modulation,
        ada_all.astype(F32),
        (((1,), (0,)), ((), ())),
        precision=lax.Precision.HIGHEST,
    )
    _, silu_pull = jax.vjp(jax.nn.silu, conditioning)
    condition_grad = silu_pull(grad_silu)[0]

    qv_sum, out_bias_sum, up_bias_sum, down_bias_sum = (
        bias_owned[low:high] for low, high in zip(cuts[:-1], cuts[1:])
    )
    return (
        output,
        tokens_grad,
        condition_grad,
        ada_grad.T,
        ada_bias_grad,
        qkv_owned.T,
        qv_sum,
        out_owned.T,
        out_bias_sum,
        up_owned.T,
        up_bias_sum,
        down_owned.T,
        down_bias_sum,
    )


def solution(mesh):
    return jax.shard_map(
        functools.partial(body, mesh.shape["dp"], mesh.shape["rep"]),
        mesh=mesh,
        in_specs=(
            P(("dp", "rep"), None, None),
            P(("dp", "rep"), None),
            P(None, "dp"),
            P("dp"),
            P(None, "dp"),
            P("dp"),
            P(None, "dp"),
            P("dp"),
            P(None, "dp"),
            P("dp"),
            P(None, "dp"),
            P("dp"),
            P(("dp", "rep"), None, None),
        ),
        out_specs=(
            P(("dp", "rep"), None, None),
            P(("dp", "rep"), None, None),
            P(("dp", "rep"), None),
            P(None, "dp"),
            P("dp"),
            P(None, "dp"),
            P("dp"),
            P(None, "dp"),
            P("dp"),
            P(None, "dp"),
            P("dp"),
            P(None, "dp"),
            P("dp"),
        ),
        check_vma=False,
    )
```

```python
import functools

import jax
import jax.numpy as jnp
from jax import lax
from jax.experimental import pallas as pl
from jax.experimental.pallas import tpu as pltpu
from jax.sharding import PartitionSpec as P

HEAD_DIM = 64
EPS = 1e-06
GELU_C = 0.7978845608028654
VMEM_LIMIT = 56 * 1024 * 1024
F32 = jnp.float32
BF16 = jnp.bfloat16


def dot_nn(left, right):
    return lax.dot_general(left, right, (((1,), (0,)), ((), ())), preferred_element_type=F32)


def dot_nt(left, right):
    return lax.dot_general(left, right, (((1,), (1,)), ((), ())), preferred_element_type=F32)


def dot_tn(left, right):
    return lax.dot_general(left, right, (((0,), (0,)), ((), ())), preferred_element_type=F32)


def normalise(values):
    average = jnp.mean(values, axis=-1, keepdims=True)
    centred = values - average
    spread = jnp.mean(centred * centred, axis=-1, keepdims=True)
    inverse = lax.rsqrt(spread + EPS)
    return centred * inverse, inverse


def normalise_back(upstream, normal, inverse):
    first = jnp.mean(upstream, axis=-1, keepdims=True)
    second = jnp.mean(upstream * normal, axis=-1, keepdims=True)
    return inverse * (upstream - first - normal * second)


def beside(left, right):
    return jnp.concatenate([left, right], axis=1)


def attention_forward_kernel(
    tokens_ref, mod_ref, weight_ref, bias_ref, normed_ref, qkv_ref, lse_ref, attended_ref
):
    latents, length, width = tokens_ref.shape
    bias = beside(bias_ref[...], bias_ref[...])
    blank = jnp.zeros((HEAD_DIM, length), BF16)
    for latent in range(latents):
        normal, _ = normalise(tokens_ref[latent].astype(F32))
        normed = normal * (1.0 + mod_ref[latent, 1:2, :]) + mod_ref[latent, 0:1, :]
        normed = normed.astype(BF16)
        normed_ref[latent] = normed
        qkv = (dot_nt(weight_ref[...], normed) + bias).astype(BF16)
        qkv_ref[latent] = qkv
        keys_in = qkv[width : 2 * width].T
        for head in range(width // HEAD_DIM):
            low = head * HEAD_DIM
            high = low + HEAD_DIM
            pair = low - low % (2 * HEAD_DIM)
            queries = qkv[low:high]
            queries = jnp.concatenate([blank, queries] if low > pair else [queries, blank])
            scores = dot_nn(keys_in[:, pair : pair + 2 * HEAD_DIM], queries) * HEAD_DIM ** (-0.5)
            highest = jnp.max(scores, axis=0, keepdims=True)
            shifted = jnp.exp(scores - highest)
            total = jnp.sum(shifted, axis=0, keepdims=True)
            probs = (shifted * (1.0 / total)).astype(BF16)
            lse_ref[latent, head : head + 1, :] = highest + jnp.log(total)
            values_in = qkv[2 * width + low : 2 * width + high]
            attended_ref[latent, low:high, :] = dot_nn(values_in, probs).astype(BF16)


def feed_kernel(
    tokens_ref,
    cotangent_ref,
    attended_ref,
    mod_ref,
    out_weight_ref,
    out_bias_ref,
    up_weight_ref,
    up_bias_ref,
    down_weight_ref,
    down_bias_ref,
    output_ref,
    grad_middle_ref,
    grad_attended_ref,
    grad_mod_ref,
    out_grad_ref,
    up_grad_ref,
    down_grad_ref,
    out_bias_grad_ref,
    up_bias_grad_ref,
    down_bias_grad_ref,
    out_acc,
    up_acc,
    down_acc,
    bias_acc,
    out_back,
    up_back,
    down_back,
    active_all,
    grad_hidden_all,
    *,
    chunk,
):
    step = pl.program_id(0)
    latents, length, width = tokens_ref.shape
    hidden_width = up_weight_ref.shape[0]

    @pl.when(step == 0)
    def _():
        out_acc[...] = jnp.zeros_like(out_acc)
        up_acc[...] = jnp.zeros_like(up_acc)
        down_acc[...] = jnp.zeros_like(down_acc)
        bias_acc[...] = jnp.zeros_like(bias_acc)
        out_back[...] = out_weight_ref[...].T
        up_back[...] = up_weight_ref[...].T
        down_back[...] = down_weight_ref[...].T

    kept = []
    for latent in range(latents):
        gate_one = mod_ref[latent, 2:3, :]
        shift_two = mod_ref[latent, 3:4, :]
        scale_two = 1.0 + mod_ref[latent, 4:5, :]
        gate_two = mod_ref[latent, 5:6, :]
        branch = dot_nn(out_weight_ref[...], attended_ref[latent]).T + out_bias_ref[...]
        middle = tokens_ref[latent].astype(F32) + gate_one * branch
        normal, inverse = normalise(middle)
        normed = (normal * scale_two + shift_two).astype(BF16)
        incoming = cotangent_ref[latent].astype(F32)
        grad_feed = (incoming * gate_two).astype(BF16)
        bias_acc[0:1, :] += jnp.sum(grad_feed.astype(F32), axis=0, keepdims=True)
        kept.append((gate_one, scale_two, gate_two, branch, middle, normal, inverse, normed, incoming, grad_feed))

    for latent in range(latents):
        normed, grad_feed = kept[latent][7], kept[latent][9]
        here = slice(latent * length, (latent + 1) * length)
        for low in range(0, hidden_width, chunk):
            high = low + chunk
            bias = up_bias_ref[low:high, :]
            hidden = dot_nt(up_weight_ref[low:high, :], normed) + beside(bias, bias)
            grad_active = dot_nt(down_back[low:high, :], grad_feed)
            square = hidden * hidden
            bent = jnp.tanh(hidden * (GELU_C + (GELU_C * 0.044715) * square))
            half = 0.5 + 0.5 * bent
            active_all[low:high, here] = (hidden * half).astype(BF16)
            slope = half + hidden * (0.5 - 0.5 * (bent * bent)) * (
                GELU_C + (3.0 * GELU_C * 0.044715) * square
            )
            grad_hidden_all[low:high, here] = (grad_active * slope).astype(BF16)

    grad_branches = []
    for latent in range(latents):
        gate_one, scale_two, gate_two, branch, middle, normal, inverse, _, incoming, _ = kept[latent]
        here = slice(latent * length, (latent + 1) * length)
        feed = dot_nn(down_weight_ref[...], active_all[:, here]).T + down_bias_ref[...]
        grad_normed = dot_nn(up_back[...], grad_hidden_all[:, here]).T
        output_ref[latent] = (middle + gate_two * feed).astype(BF16)
        grad_mod_ref[latent, 3:4, :] = jnp.sum(incoming * feed, axis=0, keepdims=True)
        grad_mod_ref[latent, 1:2, :] = jnp.sum(grad_normed, axis=0, keepdims=True)
        grad_mod_ref[latent, 2:3, :] = jnp.sum(grad_normed * normal, axis=0, keepdims=True)
        grad_middle = incoming + normalise_back(grad_normed * scale_two, normal, inverse)
        grad_middle_ref[latent] = grad_middle
        grad_branch = (grad_middle * gate_one).astype(BF16)
        grad_branches.append(grad_branch)
        grad_mod_ref[latent, 0:1, :] = jnp.sum(grad_middle * branch, axis=0, keepdims=True)
        bias_acc[1:2, :] += jnp.sum(grad_branch.astype(F32), axis=0, keepdims=True)
        grad_attended_ref[latent] = dot_nt(out_back[...], grad_branch).astype(BF16)

    normed_all = jnp.concatenate([entry[7] for entry in kept])
    ones = jnp.ones((latents * length, 128), BF16)
    grad_feed_all = jnp.concatenate([entry[9] for entry in kept])
    attended_all = jnp.concatenate([attended_ref[latent] for latent in range(latents)], axis=1)
    up_acc[...] += dot_nn(grad_hidden_all[...], beside(normed_all, ones))
    down_acc[...] += dot_nn(active_all[...], grad_feed_all)
    out_acc[...] += dot_nn(attended_all, jnp.concatenate(grad_branches))

    @pl.when(step == pl.num_programs(0) - 1)
    def _():
        out_grad_ref[...] = out_acc[...].T.astype(BF16)
        up_grad_ref[...] = up_acc[:, :width].astype(BF16)
        down_grad_ref[...] = down_acc[...].T.astype(BF16)
        up_bias_grad_ref[...] = up_acc[:, width:]
        down_bias_grad_ref[...] = bias_acc[0:1, :]
        out_bias_grad_ref[...] = bias_acc[1:2, :]


def attention_backward_kernel(
    qkv_ref,
    lse_ref,
    grad_attended_ref,
    normed_ref,
    grad_qkv_ref,
    weight_grad_ref,
    bias_grad_ref,
    acc,
):
    step = pl.program_id(0)
    latents, length, width = normed_ref.shape
    blank = jnp.zeros((HEAD_DIM, length), BF16)

    @pl.when(step == 0)
    def _():
        acc[...] = jnp.zeros_like(acc)

    for latent in range(latents):
        keys_all = qkv_ref[latent, width : 2 * width, :].T
        values_all = qkv_ref[latent, 2 * width : 3 * width, :].T
        for head in range(width // HEAD_DIM):
            low = head * HEAD_DIM
            high = low + HEAD_DIM
            pair = low - low % (2 * HEAD_DIM)
            queries = qkv_ref[latent, low:high, :]
            keys_in = qkv_ref[latent, width + low : width + high, :]
            grad_out = grad_attended_ref[latent, low:high, :]
            first = low == pair
            queries_wide = jnp.concatenate([queries, blank] if first else [blank, queries])
            grad_out_wide = jnp.concatenate([grad_out, blank] if first else [blank, grad_out])
            scores = dot_nn(keys_all[:, pair : pair + 2 * HEAD_DIM], queries_wide)
            grad_probs = dot_nn(values_all[:, pair : pair + 2 * HEAD_DIM], grad_out_wide)
            probs = jnp.exp(scores * HEAD_DIM ** (-0.5) - lse_ref[latent, head : head + 1, :])
            row_terms = jnp.sum(probs * grad_probs, axis=0, keepdims=True)
            grad_scores = (probs * (grad_probs - row_terms)).astype(BF16)
            grad_qkv_ref[latent, low:high, :] = (
                dot_nn(keys_in, grad_scores) * HEAD_DIM ** (-0.5)
            ).astype(BF16)
            grad_qkv_ref[latent, width + low : width + high, :] = (
                dot_nt(queries, grad_scores) * HEAD_DIM ** (-0.5)
            ).astype(BF16)
            grad_qkv_ref[latent, 2 * width + low : 2 * width + high, :] = dot_nt(
                grad_out, probs.astype(BF16)
            ).astype(BF16)
    grad_qkv = jnp.concatenate([grad_qkv_ref[latent] for latent in range(latents)], axis=1)
    normed = normed_ref[...].reshape(latents * length, width)
    acc[...] += dot_nn(grad_qkv, beside(normed, jnp.ones((latents * length, 128), BF16)))

    @pl.when(step == pl.num_programs(0) - 1)
    def _():
        weight_grad_ref[...] = acc[:, :width].astype(BF16)
        bias_grad_ref[...] = acc[:, width:]


def first_norm_kernel(
    grad_qkv_ref,
    tokens_ref,
    grad_middle_ref,
    mod_ref,
    weight_ref,
    tokens_grad_ref,
    grad_mod_ref,
    weight_back,
):
    latents = tokens_ref.shape[0]

    @pl.when(pl.program_id(0) == 0)
    def _():
        weight_back[...] = weight_ref[...].T

    for latent in range(latents):
        normal, inverse = normalise(tokens_ref[latent].astype(F32))
        grad_normed = dot_nn(weight_back[...], grad_qkv_ref[latent]).T
        grad_mod_ref[latent, 0:1, :] = jnp.sum(grad_normed, axis=0, keepdims=True)
        grad_mod_ref[latent, 1:2, :] = jnp.sum(grad_normed * normal, axis=0, keepdims=True)
        upstream = grad_normed * (1.0 + mod_ref[latent, 1:2, :])
        tokens_grad_ref[latent] = (
            grad_middle_ref[latent] + normalise_back(upstream, normal, inverse)
        ).astype(BF16)


def each(shape, count):
    zeros = (0,) * (len(shape) - 1)
    return pl.BlockSpec((count,) + tuple(shape[1:]), lambda step: (step,) + zeros)


def whole(shape):
    zeros = (0,) * len(shape)
    return pl.BlockSpec(tuple(shape), lambda step: zeros)


def run_kernel(kernel, count, streamed_out, fixed_out, scratch, streamed, fixed, cost):
    return pl.pallas_call(
        kernel,
        grid=(streamed[0].shape[0] // count,),
        in_specs=[each(item.shape, count) for item in streamed]
        + [whole(item.shape) for item in fixed],
        out_specs=[each(item.shape, count) for item in streamed_out]
        + [whole(item.shape) for item in fixed_out],
        out_shape=list(streamed_out) + list(fixed_out),
        scratch_shapes=scratch,
        compiler_params=pltpu.CompilerParams(
            dimension_semantics=("arbitrary",), vmem_limit_bytes=VMEM_LIMIT
        ),
        cost_estimate=cost,
    )(*streamed, *fixed)


def shape_of(dims, kind):
    return jax.ShapeDtypeStruct(tuple(dims), kind)


AXES = ("dp", "rep")


class Hops:
    def __init__(self, n_dp, n_rep):
        self.sizes = {"dp": n_dp, "rep": n_rep}
        self.place = {name: lax.axis_index(name) for name in AXES}

    def bits(self, name):
        return [1 << shift for shift in range(self.sizes[name].bit_length() - 1)]

    def mine(self, name, bit):
        return (self.place[name] // bit) % 2

    def swap(self, value, name, bit):
        n_dp, n_rep = self.sizes["dp"], self.sizes["rep"]
        flip_dp, flip_rep = (bit, 0) if name == "dp" else (0, bit)
        pairs = [
            (d * n_rep + r, (d ^ flip_dp) * n_rep + (r ^ flip_rep))
            for d in range(n_dp)
            for r in range(n_rep)
        ]
        return lax.ppermute(value, AXES, pairs)

    def both(self, kept, came, name, bit, axis):
        upper = self.mine(name, bit) == 1
        return jnp.stack(
            [jnp.where(upper, came, kept), jnp.where(upper, kept, came)], axis=axis
        )

    def cut(self, value, name, bit, axis):
        here = self.mine(name, bit)
        return (
            lax.dynamic_index_in_dim(value, here, axis, keepdims=False),
            lax.dynamic_index_in_dim(value, 1 - here, axis, keepdims=False),
        )


def pad_rows(values, count):
    return jnp.pad(values, ((0, 0),) * (values.ndim - 2) + ((0, count - values.shape[-2]), (0, 0)))


def up_to(count, multiple):
    return -(-count // multiple) * multiple


def body(
    n_dp,
    n_rep,
    tokens,
    conditioning,
    ada_weight,
    ada_bias,
    qkv_weight,
    qv_bias,
    out_weight,
    out_bias,
    up_weight,
    up_bias,
    down_weight,
    down_bias,
    cotangent,
):
    latents, length, width = tokens.shape
    hidden_width = up_weight.shape[1] * n_dp
    heads = width // HEAD_DIM
    rows = latents * length
    hops = Hops(n_dp, n_rep)
    dp_bits = hops.bits("dp")
    folds = hidden_width // width

    up_rows, out_rows = up_weight.shape[1], out_weight.shape[1]
    down_shard = down_weight.T.reshape(out_rows, folds, width).transpose(1, 0, 2)
    late_shard = jnp.concatenate(
        [up_weight.T, down_shard.reshape(folds * out_rows, width), out_weight.T]
    )
    late = lax.all_gather(late_shard, "dp", axis=0)
    up_all = late[:, :up_rows].reshape(hidden_width, width)
    down_all = late[:, up_rows : up_rows + folds * out_rows]
    down_all = down_all.reshape(n_dp, folds, out_rows, width).transpose(0, 2, 1, 3)
    down_all = down_all.reshape(width, hidden_width)
    out_all = late[:, up_rows + folds * out_rows :].reshape(width, width)
    silu_low = jax.nn.silu(conditioning).astype(BF16)
    ada_shard, _ = lax.optimization_barrier((ada_weight.T, late))
    ada_all = lax.all_gather(ada_shard, "dp", axis=0, tiled=True)

    qkv_rows = qkv_weight.shape[1]
    half_rows = qkv_rows // 2
    core = hops.mine("rep", 1)
    bias_shard = jnp.concatenate([qv_bias, out_bias, up_bias, down_bias])
    bias_rows = up_to(bias_shard.shape[0], width) // width
    bias_block = jnp.pad(bias_shard, (0, bias_rows * width - bias_shard.shape[0]))
    front = jnp.concatenate(
        [
            lax.dynamic_slice_in_dim(qkv_weight.T, core * half_rows, half_rows, axis=0),
            silu_low,
            bias_block.reshape(bias_rows, width),
        ]
    )
    front = pad_rows(front, up_to(front.shape[0], 8))
    for done, bit in enumerate(dp_bits[::-1]):
        front = hops.both(front, hops.swap(front, "dp", bit), "dp", bit, done)
    front = front.reshape(n_dp, -1, width)
    front = front[:, : half_rows + latents + bias_rows]
    silu_group = front[:, half_rows : half_rows + latents].reshape(n_dp * latents, width)
    halves = front[:, : half_rows + latents]
    halves = hops.both(halves, hops.swap(halves, "rep", 1), "rep", 1, 0)
    qkv_full = halves[:, :, :half_rows].transpose(1, 0, 2, 3).reshape(3 * width, width)
    silu_all = halves[:, :, half_rows:]
    for bit in hops.bits("rep")[1:]:
        silu_all = hops.both(silu_all, hops.swap(silu_all, "rep", bit), "rep", bit, 0)
    silu_all = silu_all.reshape(n_rep, n_dp, latents, width).reshape(-1, width)

    bias_all = front[:, half_rows + latents : half_rows + latents + bias_rows]
    bias_all = bias_all.reshape(n_dp, -1).astype(F32)
    cuts = [0]
    for part in (qv_bias, out_bias, up_bias, down_bias):
        cuts.append(cuts[-1] + part.shape[0])
    qv_full, out_full, up_full, down_full = (
        bias_all[:, low:high].reshape(1, -1) for low, high in zip(cuts[:-1], cuts[1:])
    )
    qkv_bias = jnp.concatenate(
        [qv_full[:, :width], jnp.zeros((1, width), F32), qv_full[:, width:]], axis=1
    )
    qkv_bias = jnp.broadcast_to(qkv_bias.reshape(-1, 1), (3 * width, 128))
    up_full = jnp.broadcast_to(up_full.reshape(-1, 1), (hidden_width, 128))

    mod = jnp.dot(silu_group, ada_weight, preferred_element_type=F32) + ada_bias.astype(F32)
    mod = mod.reshape((2,) * len(dp_bits) + (latents, -1))
    for done, bit in enumerate(dp_bits[::-1]):
        kept, sent = hops.cut(mod, "dp", bit, done)
        mod = hops.both(kept, hops.swap(sent, "dp", bit), "dp", bit, done)
    modulation = mod.reshape(n_dp, latents, -1).transpose(1, 0, 2).reshape(latents, 6, width)

    normed, qkv, lse, attended = run_kernel(
        attention_forward_kernel,
        2,
        [
            shape_of((latents, length, width), BF16),
            shape_of((latents, 3 * width, length), BF16),
            shape_of((latents, 8 * ((heads + 7) // 8), length), F32),
            shape_of((latents, width, length), BF16),
        ],
        [],
        [],
        [tokens, modulation],
        [qkv_full, qkv_bias],
        pl.CostEstimate(
            flops=2 * rows * width * (3 * width + 2 * length),
            bytes_accessed=rows * width * 12,
            transcendentals=rows * heads * length,
        ),
    )

    (
        output,
        grad_middle,
        grad_attended,
        grad_mod_two,
        out_grad,
        up_grad,
        down_grad,
        out_bias_grad,
        up_bias_grad,
        down_bias_grad,
    ) = run_kernel(
        functools.partial(feed_kernel, chunk=512),
        2,
        [
            shape_of((latents, length, width), BF16),
            shape_of((latents, length, width), F32),
            shape_of((latents, width, length), BF16),
            shape_of((latents, 4, width), F32),
        ],
        [
            shape_of((width, width), BF16),
            shape_of((hidden_width, width), BF16),
            shape_of((width, hidden_width), BF16),
            shape_of((1, width), F32),
            shape_of((hidden_width, 128), F32),
            shape_of((1, width), F32),
        ],
        [
            pltpu.VMEM((width, width), F32),
            pltpu.VMEM((hidden_width, width + 128), F32),
            pltpu.VMEM((hidden_width, width), F32),
            pltpu.VMEM((8, width), F32),
            pltpu.VMEM((width, width), BF16),
            pltpu.VMEM((width, hidden_width), BF16),
            pltpu.VMEM((hidden_width, width), BF16),
            pltpu.VMEM((hidden_width, 2 * length), BF16),
            pltpu.VMEM((hidden_width, 2 * length), BF16),
        ],
        [tokens, cotangent, attended, modulation],
        [out_all, out_full, up_all, up_full, down_all, down_full],
        pl.CostEstimate(
            flops=6 * rows * width * (width + 2 * hidden_width),
            bytes_accessed=rows * width * 14,
            transcendentals=rows * hidden_width,
        ),
    )

    late_grad = jnp.concatenate(
        [
            up_grad.reshape(n_dp, up_rows, width),
            down_grad.reshape(n_dp, out_rows, folds, width)
            .transpose(0, 2, 1, 3)
            .reshape(n_dp, folds * out_rows, width),
            out_grad.reshape(n_dp, out_rows, width),
        ],
        axis=1,
    )
    late_sum = lax.psum_scatter(late_grad, "dp", scatter_dimension=0, tiled=True)
    late_sum = late_sum.reshape(-1, width)

    normed, ada_all = lax.optimization_barrier((normed, ada_all))
    grad_qkv, qkv_grad, qkv_bias_grad = run_kernel(
        attention_backward_kernel,
        2,
        [shape_of((latents, 3 * width, length), BF16)],
        [shape_of((3 * width, width), BF16), shape_of((3 * width, 128), F32)],
        [pltpu.VMEM((3 * width, width + 128), F32)],
        [qkv, lse, grad_attended, normed],
        [],
        pl.CostEstimate(flops=1, bytes_accessed=1, transcendentals=0),
    )

    qkv_columns = qkv_bias_grad[:, 0]
    bias_blocks = jnp.concatenate(
        [
            jnp.concatenate([qkv_columns[:width], qkv_columns[2 * width :]]).reshape(n_dp, -1),
            out_bias_grad.reshape(n_dp, -1),
            up_bias_grad[:, 0].reshape(n_dp, -1),
            down_bias_grad.reshape(n_dp, -1),
        ],
        axis=1,
    ).astype(BF16)
    bias_part = cuts[-1] // 2
    bias_blocks = bias_blocks.reshape(n_dp, 2, 1, bias_part)
    tail_rows = up_to(half_rows + 1, 8)
    bias_blocks = jnp.pad(
        bias_blocks,
        ((0, 0), (0, 0), (0, tail_rows - half_rows - 1), (0, width - bias_part)),
    )
    blocks = jnp.concatenate([qkv_grad.reshape(n_dp, 2, half_rows, width), bias_blocks], axis=2)
    kept, sent = hops.cut(blocks, "rep", 1, 1)
    total = kept.astype(F32) + hops.swap(sent, "rep", 1).astype(F32)

    tokens_grad, grad_mod_one = run_kernel(
        first_norm_kernel,
        2,
        [shape_of((latents, length, width), BF16), shape_of((latents, 2, width), F32)],
        [],
        [pltpu.VMEM((width, 3 * width), BF16)],
        [grad_qkv, tokens, grad_middle, modulation],
        [qkv_full],
        pl.CostEstimate(flops=1, bytes_accessed=1, transcendentals=0),
    )
    grad_modulation = jnp.concatenate([grad_mod_one, grad_mod_two], axis=1).reshape(
        latents, 6 * width
    )

    own = 6 * width // n_dp
    columns = grad_modulation.reshape(latents, n_dp, own).transpose(1, 0, 2).astype(BF16)
    columns = jnp.pad(columns, ((0, 0), (0, 0), (0, up_to(own, width) - own)))
    columns = columns.reshape((2,) * len(dp_bits) + (latents, width))
    total = total.reshape((2,) * len(dp_bits) + (tail_rows, width))
    axis = len(dp_bits) - 1
    for bit in dp_bits:
        kept, sent = hops.cut(total, "dp", bit, axis)
        column_kept, column_sent = hops.cut(columns, "dp", bit, axis)
        lead = sent.shape[:axis]
        sources = column_sent.shape[axis:-2]
        came = hops.swap(
            jnp.concatenate(
                [sent.astype(BF16), column_sent.reshape(lead + (-1, width))], axis=-2
            ),
            "dp",
            bit,
        )
        total = kept.astype(F32) + came[..., :tail_rows, :].astype(F32)
        column_came = came[..., tail_rows:, :].reshape(lead + sources + (latents, width))
        columns = hops.both(column_kept, column_came, "dp", bit, axis)
        axis -= 1
    columns = columns.reshape(n_dp * latents, width)

    qkv_total = total.astype(BF16)
    end = tail_rows + late_sum.shape[0]
    for bit in hops.bits("rep")[1:]:
        sums = jnp.concatenate([qkv_total, late_sum])
        came = hops.swap(jnp.concatenate([sums, columns]), "rep", bit)
        sums = (sums.astype(F32) + came[:end].astype(F32)).astype(BF16)
        qkv_total, late_sum = sums[:tail_rows], sums[tail_rows:]
        columns = hops.both(columns, came[end:], "rep", bit, 0).reshape(-1, width)
    came = hops.swap(jnp.concatenate([qkv_total, late_sum, columns]), "rep", 1)
    qkv_total = hops.both(qkv_total, came[:tail_rows], "rep", 1, 0).astype(F32)
    late_sum = late_sum.astype(F32) + came[tail_rows:end].astype(F32)
    columns = hops.both(columns, came[end:], "rep", 1, 0)
    columns = columns.reshape(2, n_rep // 2, n_dp * latents, width)[..., :own]
    columns = columns.transpose(1, 0, 2, 3).reshape(-1, own)
    qkv_owned = qkv_total[:, :half_rows].reshape(qkv_rows, width)
    bias_owned = qkv_total[:, half_rows, :bias_part].reshape(-1)
    up_owned = late_sum[:up_rows]
    down_owned = late_sum[up_rows : up_rows + folds * out_rows]
    down_owned = down_owned.reshape(folds, out_rows, width).transpose(1, 0, 2)
    down_owned = down_owned.reshape(out_rows, hidden_width)
    out_owned = late_sum[up_rows + folds * out_rows :]
    ada_grad = dot_tn(columns, silu_all)
    ada_bias_grad = jnp.sum(columns.astype(F32), axis=0)

    grad_silu = lax.dot_general(
        grad_modulation,
        ada_all.astype(F32),
        (((1,), (0,)), ((), ())),
        precision=lax.Precision.HIGHEST,
    )
    _, silu_pull = jax.vjp(jax.nn.silu, conditioning)
    condition_grad = silu_pull(grad_silu)[0]

    qv_sum, out_bias_sum, up_bias_sum, down_bias_sum = (
        bias_owned[low:high] for low, high in zip(cuts[:-1], cuts[1:])
    )
    return (
        output,
        tokens_grad,
        condition_grad,
        ada_grad.T,
        ada_bias_grad,
        qkv_owned.T,
        qv_sum,
        out_owned.T,
        out_bias_sum,
        up_owned.T,
        up_bias_sum,
        down_owned.T,
        down_bias_sum,
    )


def solution(mesh):
    return jax.shard_map(
        functools.partial(body, mesh.shape["dp"], mesh.shape["rep"]),
        mesh=mesh,
        in_specs=(
            P(("dp", "rep"), None, None),
            P(("dp", "rep"), None),
            P(None, "dp"),
            P("dp"),
            P(None, "dp"),
            P("dp"),
            P(None, "dp"),
            P("dp"),
            P(None, "dp"),
            P("dp"),
            P(None, "dp"),
            P("dp"),
            P(("dp", "rep"), None, None),
        ),
        out_specs=(
            P(("dp", "rep"), None, None),
            P(("dp", "rep"), None, None),
            P(("dp", "rep"), None),
            P(None, "dp"),
            P("dp"),
            P(None, "dp"),
            P("dp"),
            P(None, "dp"),
            P("dp"),
            P(None, "dp"),
            P("dp"),
            P(None, "dp"),
            P("dp"),
        ),
        check_vma=False,
    )
```

```python
import functools

import jax
import jax.numpy as jnp
from jax import lax
from jax.experimental import pallas as pl
from jax.experimental.pallas import tpu as pltpu
from jax.sharding import PartitionSpec as P

HEAD_DIM = 64
EPS = 1e-06
GELU_C = 0.7978845608028654
VMEM_LIMIT = 56 * 1024 * 1024
F32 = jnp.float32
BF16 = jnp.bfloat16


def dot_nn(left, right):
    return lax.dot_general(left, right, (((1,), (0,)), ((), ())), preferred_element_type=F32)


def dot_nt(left, right):
    return lax.dot_general(left, right, (((1,), (1,)), ((), ())), preferred_element_type=F32)


def dot_tn(left, right):
    return lax.dot_general(left, right, (((0,), (0,)), ((), ())), preferred_element_type=F32)


def normalise(values):
    average = jnp.mean(values, axis=-1, keepdims=True)
    centred = values - average
    spread = jnp.mean(centred * centred, axis=-1, keepdims=True)
    inverse = lax.rsqrt(spread + EPS)
    return centred * inverse, inverse


def normalise_back(upstream, normal, inverse):
    first = jnp.mean(upstream, axis=-1, keepdims=True)
    second = jnp.mean(upstream * normal, axis=-1, keepdims=True)
    return inverse * (upstream - first - normal * second)


STRIP = 64
GROUP = 3


def beside(*parts):
    return jnp.concatenate(parts, axis=1)


def above(*parts):
    return jnp.concatenate(parts, axis=0)


def strips(extent, size):
    return [slice(low, low + size) for low in range(0, extent, size)]


def head_slices(head):
    low = head * HEAD_DIM
    pair = low - low % (2 * HEAD_DIM)
    return slice(low, low + HEAD_DIM), slice(pair, pair + 2 * HEAD_DIM), low == pair


def in_groups(items, size):
    return [items[low : low + size] for low in range(0, len(items), size)]


def attention_forward_kernel(
    tokens_ref, mod_ref, weight_ref, bias_ref, normed_ref, qkv_ref, lse_ref, attended_ref
):
    latents, length, width = tokens_ref.shape
    blank = jnp.zeros((HEAD_DIM, length), BF16)
    for latent in range(latents):
        for rows in strips(length, STRIP):
            normal, _ = normalise(tokens_ref[latent, rows, :].astype(F32))
            normed = normal * (1.0 + mod_ref[latent, 1:2, :]) + mod_ref[latent, 0:1, :]
            normed_ref[latent, rows, :] = normed.astype(BF16)
    normed = normed_ref[...].reshape(latents * length, width)
    for part in strips(3 * width, 2 * HEAD_DIM):
        bias = bias_ref[part, :]
        qkv = dot_nt(weight_ref[part, :], normed) + beside(*([bias] * (latents * length // 128)))
        qkv = qkv.astype(BF16)
        for latent in range(latents):
            qkv_ref[latent, part, :] = qkv[:, latent * length : (latent + 1) * length]
    keys_all = [qkv_ref[latent, width : 2 * width, :].T for latent in range(latents)]

    def scores_of(latent, head):
        own, pair, first = head_slices(head)
        queries = qkv_ref[latent, own, :]
        queries = above(queries, blank) if first else above(blank, queries)
        return dot_nn(keys_all[latent][:, pair], queries)

    def probs_of(latent, head, scores):
        parts = []
        for columns in strips(length, 128):
            strip = scores[:, columns] * HEAD_DIM ** (-0.5)
            highest = jnp.max(strip, axis=0, keepdims=True)
            shifted = jnp.exp(strip - highest)
            total = jnp.sum(shifted, axis=0, keepdims=True)
            parts.append((shifted * (1.0 / total)).astype(BF16))
            lse_ref[latent, head : head + 1, columns] = highest + jnp.log(total)
        return beside(*parts)

    def attend(latent, head, probs):
        own, _, _ = head_slices(head)
        values_in = qkv_ref[latent, 2 * width + own.start : 2 * width + own.stop, :]
        attended_ref[latent, own, :] = dot_nn(values_in, probs).astype(BF16)

    items = [(latent, head) for latent in range(latents) for head in range(width // HEAD_DIM)]
    groups = in_groups(items, GROUP)
    scores = [scores_of(*item) for item in groups[0]]
    previous = []
    for place, group in enumerate(groups):
        later = groups[place + 1] if place + 1 < len(groups) else []
        next_scores = [scores_of(*item) for item in later]
        probs = [probs_of(*item, value) for item, value in zip(group, scores)]
        for item, value in previous:
            attend(*item, value)
        previous = list(zip(group, probs))
        scores = next_scores
    for item, value in previous:
        attend(*item, value)


def feed_kernel(
    tokens_ref,
    cotangent_ref,
    attended_ref,
    mod_ref,
    out_weight_ref,
    out_bias_ref,
    up_weight_ref,
    up_bias_ref,
    down_weight_ref,
    down_bias_ref,
    output_ref,
    grad_middle_ref,
    grad_attended_ref,
    grad_mod_ref,
    out_grad_ref,
    up_grad_ref,
    down_grad_ref,
    out_bias_grad_ref,
    up_bias_grad_ref,
    down_bias_grad_ref,
    out_acc,
    up_acc,
    down_acc,
    bias_acc,
    out_back,
    up_back,
    down_back,
    active_all,
    grad_hidden_all,
    middle_all,
    normal_all,
    branch_all,
    *,
    chunk,
):
    step = pl.program_id(0)
    latents, length, width = tokens_ref.shape
    hidden_width = up_weight_ref.shape[0]
    tokens_all = latents * length

    @pl.when(step == 0)
    def _():
        out_acc[...] = jnp.zeros_like(out_acc)
        up_acc[...] = jnp.zeros_like(up_acc)
        down_acc[...] = jnp.zeros_like(down_acc)
        bias_acc[...] = jnp.zeros_like(bias_acc)
        out_back[...] = out_weight_ref[...].T
        up_back[...] = up_weight_ref[...].T
        down_back[...] = down_weight_ref[...].T

    attended = beside(*[attended_ref[latent] for latent in range(latents)])
    branch_wide = dot_nn(out_weight_ref[...], attended)
    normed_parts = []
    grad_feed_parts = []
    inverses = []
    down_sum = jnp.zeros((1, width), F32)
    for latent in range(latents):
        gate_one = mod_ref[latent, 2:3, :]
        shift_two = mod_ref[latent, 3:4, :]
        scale_two = 1.0 + mod_ref[latent, 4:5, :]
        gate_two = mod_ref[latent, 5:6, :]
        branch_tall = branch_wide[:, latent * length : (latent + 1) * length].T
        for rows in strips(length, STRIP):
            there = slice(latent * length + rows.start, latent * length + rows.stop)
            branch = branch_tall[rows] + out_bias_ref[...]
            branch_all[there, :] = branch
            middle = tokens_ref[latent, rows, :].astype(F32) + gate_one * branch
            middle_all[there, :] = middle
            normal, inverse = normalise(middle)
            normal_all[there, :] = normal
            inverses.append(inverse)
            normed_parts.append((normal * scale_two + shift_two).astype(BF16))
            grad_feed = (cotangent_ref[latent, rows, :].astype(F32) * gate_two).astype(BF16)
            grad_feed_parts.append(grad_feed)
            down_sum += jnp.sum(grad_feed.astype(F32), axis=0, keepdims=True)
    bias_acc[0:1, :] += down_sum
    normed_all = above(*normed_parts)
    grad_feed_all = above(*grad_feed_parts)

    def products(rows):
        return (
            dot_nt(up_weight_ref[rows, :], normed_all),
            dot_nt(down_back[rows, :], grad_feed_all),
        )

    parts = strips(hidden_width, chunk)
    ahead = products(parts[0])
    for place, part in enumerate(parts):
        hidden_wide, grad_wide = ahead
        if place + 1 < len(parts):
            ahead = products(parts[place + 1])
        for rows in strips(chunk, STRIP):
            there = slice(part.start + rows.start, part.start + rows.stop)
            bias = up_bias_ref[there, :]
            bias = beside(bias, bias)
            for columns in strips(tokens_all, 256):
                hidden = hidden_wide[rows, columns] + bias
                square = hidden * hidden
                bent = jnp.tanh(hidden * (GELU_C + (GELU_C * 0.044715) * square))
                half = 0.5 + 0.5 * bent
                active_all[there, columns] = (hidden * half).astype(BF16)
                slope = half + hidden * (0.5 - 0.5 * (bent * bent)) * (
                    GELU_C + (3.0 * GELU_C * 0.044715) * square
                )
                grad_hidden_all[there, columns] = (grad_wide[rows, columns] * slope).astype(BF16)

    feed_wide = dot_nn(down_weight_ref[...], active_all[...])
    grad_normed_wide = dot_nn(up_back[...], grad_hidden_all[...])
    ones = jnp.ones((tokens_all, 128), BF16)
    up_acc[...] += dot_nn(grad_hidden_all[...], beside(normed_all, ones))
    down_acc[...] += dot_nn(active_all[...], grad_feed_all)

    grad_branch_parts = []
    out_sum = jnp.zeros((1, width), F32)
    for latent in range(latents):
        gate_one = mod_ref[latent, 2:3, :]
        scale_two = 1.0 + mod_ref[latent, 4:5, :]
        gate_two = mod_ref[latent, 5:6, :]
        here = slice(latent * length, (latent + 1) * length)
        feed_tall = feed_wide[:, here].T
        grad_normed_tall = grad_normed_wide[:, here].T
        sums = [jnp.zeros((1, width), F32) for _ in range(4)]
        for rows in strips(length, STRIP):
            there = slice(here.start + rows.start, here.start + rows.stop)
            feed = feed_tall[rows] + down_bias_ref[...]
            grad_normed = grad_normed_tall[rows]
            incoming = cotangent_ref[latent, rows, :].astype(F32)
            normal = normal_all[there, :]
            output_ref[latent, rows, :] = (middle_all[there, :] + gate_two * feed).astype(BF16)
            grad_middle = incoming + normalise_back(
                grad_normed * scale_two, normal, inverses[there.start // STRIP]
            )
            grad_middle_ref[latent, rows, :] = grad_middle
            grad_branch = (grad_middle * gate_one).astype(BF16)
            grad_branch_parts.append(grad_branch)
            terms = (
                grad_middle * branch_all[there, :],
                grad_normed,
                grad_normed * normal,
                incoming * feed,
            )
            for place, term in enumerate(terms):
                sums[place] += jnp.sum(term, axis=0, keepdims=True)
            out_sum += jnp.sum(grad_branch.astype(F32), axis=0, keepdims=True)
        grad_mod_ref[latent] = above(*sums)
    bias_acc[1:2, :] += out_sum
    grad_branch_all = above(*grad_branch_parts)
    grad_attended = dot_nt(out_back[...], grad_branch_all).astype(BF16)
    for latent in range(latents):
        grad_attended_ref[latent] = grad_attended[:, latent * length : (latent + 1) * length]
    out_acc[...] += dot_nn(attended, grad_branch_all)

    @pl.when(step == pl.num_programs(0) - 1)
    def _():
        out_grad_ref[...] = out_acc[...].T.astype(BF16)
        up_grad_ref[...] = up_acc[:, :width].astype(BF16)
        down_grad_ref[...] = down_acc[...].T.astype(BF16)
        up_bias_grad_ref[...] = up_acc[:, width:]
        down_bias_grad_ref[...] = bias_acc[0:1, :]
        out_bias_grad_ref[...] = bias_acc[1:2, :]


def attention_backward_kernel(
    qkv_ref,
    lse_ref,
    grad_attended_ref,
    normed_ref,
    grad_qkv_ref,
    weight_grad_ref,
    bias_grad_ref,
    acc,
):
    step = pl.program_id(0)
    latents, length, width = normed_ref.shape
    blank = jnp.zeros((HEAD_DIM, length), BF16)

    @pl.when(step == 0)
    def _():
        acc[...] = jnp.zeros_like(acc)

    keys_all = [qkv_ref[latent, width : 2 * width, :].T for latent in range(latents)]
    values_all = [qkv_ref[latent, 2 * width : 3 * width, :].T for latent in range(latents)]

    def products(latent, head):
        own, pair, first = head_slices(head)
        queries = qkv_ref[latent, own, :]
        grad_out = grad_attended_ref[latent, own, :]
        queries = above(queries, blank) if first else above(blank, queries)
        grad_out = above(grad_out, blank) if first else above(blank, grad_out)
        return (
            dot_nn(keys_all[latent][:, pair], queries),
            dot_nn(values_all[latent][:, pair], grad_out),
        )

    def middle_of(latent, head, scores, grad_probs):
        low_parts = []
        grad_parts = []
        for columns in strips(length, 128):
            total = lse_ref[latent, head : head + 1, columns]
            probs = jnp.exp(scores[:, columns] * HEAD_DIM ** (-0.5) - total)
            terms = probs * grad_probs[:, columns]
            row_terms = jnp.sum(terms, axis=0, keepdims=True)
            grad_parts.append((probs * (grad_probs[:, columns] - row_terms)).astype(BF16))
            low_parts.append(probs.astype(BF16))
        return beside(*low_parts), beside(*grad_parts)

    def finish(latent, head, probs, grad_scores):
        own, _, _ = head_slices(head)
        low, high = own.start, own.stop
        queries = qkv_ref[latent, own, :]
        keys_in = qkv_ref[latent, width + low : width + high, :]
        grad_out = grad_attended_ref[latent, own, :]
        scale = HEAD_DIM ** (-0.5)
        grad_qkv_ref[latent, own, :] = (dot_nn(keys_in, grad_scores) * scale).astype(BF16)
        grad_qkv_ref[latent, width + low : width + high, :] = (
            dot_nt(queries, grad_scores) * scale
        ).astype(BF16)
        grad_qkv_ref[latent, 2 * width + low : 2 * width + high, :] = dot_nt(
            grad_out, probs
        ).astype(BF16)

    items = [(latent, head) for latent in range(latents) for head in range(width // HEAD_DIM)]
    groups = in_groups(items, GROUP)
    values = [products(*item) for item in groups[0]]
    previous = []
    for place, group in enumerate(groups):
        later = groups[place + 1] if place + 1 < len(groups) else []
        next_values = [products(*item) for item in later]
        middles = [middle_of(*item, *value) for item, value in zip(group, values)]
        for item, value in previous:
            finish(*item, *value)
        previous = list(zip(group, middles))
        values = next_values
    for item, value in previous:
        finish(*item, *value)

    grad_qkv = beside(*[grad_qkv_ref[latent] for latent in range(latents)])
    normed = normed_ref[...].reshape(latents * length, width)
    acc[...] += dot_nn(grad_qkv, beside(normed, jnp.ones((latents * length, 128), BF16)))

    @pl.when(step == pl.num_programs(0) - 1)
    def _():
        weight_grad_ref[...] = acc[:, :width].astype(BF16)
        bias_grad_ref[...] = acc[:, width:]


def first_norm_kernel(
    grad_qkv_ref,
    tokens_ref,
    grad_middle_ref,
    mod_ref,
    weight_ref,
    tokens_grad_ref,
    grad_mod_ref,
    weight_back,
):
    latents, length, width = tokens_ref.shape

    @pl.when(pl.program_id(0) == 0)
    def _():
        weight_back[...] = weight_ref[...].T

    grad_qkv = beside(*[grad_qkv_ref[latent] for latent in range(latents)])
    grad_normed_wide = dot_nn(weight_back[...], grad_qkv)
    for latent in range(latents):
        grad_normed_tall = grad_normed_wide[:, latent * length : (latent + 1) * length].T
        scale_one = 1.0 + mod_ref[latent, 1:2, :]
        first = jnp.zeros((1, width), F32)
        second = jnp.zeros((1, width), F32)
        for rows in strips(length, STRIP):
            normal, inverse = normalise(tokens_ref[latent, rows, :].astype(F32))
            grad_normed = grad_normed_tall[rows]
            first += jnp.sum(grad_normed, axis=0, keepdims=True)
            second += jnp.sum(grad_normed * normal, axis=0, keepdims=True)
            back = normalise_back(grad_normed * scale_one, normal, inverse)
            tokens_grad_ref[latent, rows, :] = (grad_middle_ref[latent, rows, :] + back).astype(
                BF16
            )
        grad_mod_ref[latent] = above(first, second)


def each(shape, count):
    zeros = (0,) * (len(shape) - 1)
    return pl.BlockSpec((count,) + tuple(shape[1:]), lambda step: (step,) + zeros)


def whole(shape):
    zeros = (0,) * len(shape)
    return pl.BlockSpec(tuple(shape), lambda step: zeros)


def run_kernel(kernel, count, streamed_out, fixed_out, scratch, streamed, fixed, cost):
    return pl.pallas_call(
        kernel,
        grid=(streamed[0].shape[0] // count,),
        in_specs=[each(item.shape, count) for item in streamed]
        + [whole(item.shape) for item in fixed],
        out_specs=[each(item.shape, count) for item in streamed_out]
        + [whole(item.shape) for item in fixed_out],
        out_shape=list(streamed_out) + list(fixed_out),
        scratch_shapes=scratch,
        compiler_params=pltpu.CompilerParams(
            dimension_semantics=("arbitrary",), vmem_limit_bytes=VMEM_LIMIT
        ),
        cost_estimate=cost,
    )(*streamed, *fixed)


def shape_of(dims, kind):
    return jax.ShapeDtypeStruct(tuple(dims), kind)


AXES = ("dp", "rep")


class Hops:
    def __init__(self, n_dp, n_rep):
        self.sizes = {"dp": n_dp, "rep": n_rep}
        self.place = {name: lax.axis_index(name) for name in AXES}

    def bits(self, name):
        return [1 << shift for shift in range(self.sizes[name].bit_length() - 1)]

    def mine(self, name, bit):
        return (self.place[name] // bit) % 2

    def swap(self, value, name, bit):
        n_dp, n_rep = self.sizes["dp"], self.sizes["rep"]
        flip_dp, flip_rep = (bit, 0) if name == "dp" else (0, bit)
        pairs = [
            (d * n_rep + r, (d ^ flip_dp) * n_rep + (r ^ flip_rep))
            for d in range(n_dp)
            for r in range(n_rep)
        ]
        return lax.ppermute(value, AXES, pairs)

    def both(self, kept, came, name, bit, axis):
        upper = self.mine(name, bit) == 1
        return jnp.stack(
            [jnp.where(upper, came, kept), jnp.where(upper, kept, came)], axis=axis
        )

    def cut(self, value, name, bit, axis):
        here = self.mine(name, bit)
        return (
            lax.dynamic_index_in_dim(value, here, axis, keepdims=False),
            lax.dynamic_index_in_dim(value, 1 - here, axis, keepdims=False),
        )


def pad_rows(values, count):
    return jnp.pad(values, ((0, 0),) * (values.ndim - 2) + ((0, count - values.shape[-2]), (0, 0)))


def up_to(count, multiple):
    return -(-count // multiple) * multiple


def body(
    n_dp,
    n_rep,
    tokens,
    conditioning,
    ada_weight,
    ada_bias,
    qkv_weight,
    qv_bias,
    out_weight,
    out_bias,
    up_weight,
    up_bias,
    down_weight,
    down_bias,
    cotangent,
):
    latents, length, width = tokens.shape
    hidden_width = up_weight.shape[1] * n_dp
    heads = width // HEAD_DIM
    rows = latents * length
    hops = Hops(n_dp, n_rep)
    dp_bits = hops.bits("dp")
    folds = hidden_width // width

    up_rows, out_rows = up_weight.shape[1], out_weight.shape[1]
    down_shard = down_weight.T.reshape(out_rows, folds, width).transpose(1, 0, 2)
    late_shard = jnp.concatenate(
        [up_weight.T, down_shard.reshape(folds * out_rows, width), out_weight.T]
    )
    late = lax.all_gather(late_shard, "dp", axis=0)
    up_all = late[:, :up_rows].reshape(hidden_width, width)
    down_all = late[:, up_rows : up_rows + folds * out_rows]
    down_all = down_all.reshape(n_dp, folds, out_rows, width).transpose(0, 2, 1, 3)
    down_all = down_all.reshape(width, hidden_width)
    out_all = late[:, up_rows + folds * out_rows :].reshape(width, width)
    silu_low = jax.nn.silu(conditioning).astype(BF16)
    ada_shard, _ = lax.optimization_barrier((ada_weight.T, late))
    ada_all = lax.all_gather(ada_shard, "dp", axis=0, tiled=True)

    qkv_rows = qkv_weight.shape[1]
    half_rows = qkv_rows // 2
    core = hops.mine("rep", 1)
    bias_shard = jnp.concatenate([qv_bias, out_bias, up_bias, down_bias])
    bias_rows = up_to(bias_shard.shape[0], width) // width
    bias_block = jnp.pad(bias_shard, (0, bias_rows * width - bias_shard.shape[0]))
    front = jnp.concatenate(
        [
            lax.dynamic_slice_in_dim(qkv_weight.T, core * half_rows, half_rows, axis=0),
            silu_low,
            bias_block.reshape(bias_rows, width),
        ]
    )
    front = pad_rows(front, up_to(front.shape[0], 8))
    for done, bit in enumerate(dp_bits[::-1]):
        front = hops.both(front, hops.swap(front, "dp", bit), "dp", bit, done)
    front = front.reshape(n_dp, -1, width)
    front = front[:, : half_rows + latents + bias_rows]
    silu_group = front[:, half_rows : half_rows + latents].reshape(n_dp * latents, width)
    halves = front[:, : half_rows + latents]
    halves = hops.both(halves, hops.swap(halves, "rep", 1), "rep", 1, 0)
    qkv_full = halves[:, :, :half_rows].transpose(1, 0, 2, 3).reshape(3 * width, width)
    silu_all = halves[:, :, half_rows:]
    for bit in hops.bits("rep")[1:]:
        silu_all = hops.both(silu_all, hops.swap(silu_all, "rep", bit), "rep", bit, 0)
    silu_all = silu_all.reshape(n_rep, n_dp, latents, width).reshape(-1, width)

    bias_all = front[:, half_rows + latents : half_rows + latents + bias_rows]
    bias_all = bias_all.reshape(n_dp, -1).astype(F32)
    cuts = [0]
    for part in (qv_bias, out_bias, up_bias, down_bias):
        cuts.append(cuts[-1] + part.shape[0])
    qv_full, out_full, up_full, down_full = (
        bias_all[:, low:high].reshape(1, -1) for low, high in zip(cuts[:-1], cuts[1:])
    )
    qkv_bias = jnp.concatenate(
        [qv_full[:, :width], jnp.zeros((1, width), F32), qv_full[:, width:]], axis=1
    )
    qkv_bias = jnp.broadcast_to(qkv_bias.reshape(-1, 1), (3 * width, 128))
    up_full = jnp.broadcast_to(up_full.reshape(-1, 1), (hidden_width, 128))

    mod = jnp.dot(silu_group, ada_weight, preferred_element_type=F32) + ada_bias.astype(F32)
    mod = mod.reshape((2,) * len(dp_bits) + (latents, -1))
    for done, bit in enumerate(dp_bits[::-1]):
        kept, sent = hops.cut(mod, "dp", bit, done)
        mod = hops.both(kept, hops.swap(sent, "dp", bit), "dp", bit, done)
    modulation = mod.reshape(n_dp, latents, -1).transpose(1, 0, 2).reshape(latents, 6, width)

    normed, qkv, lse, attended = run_kernel(
        attention_forward_kernel,
        4,
        [
            shape_of((latents, length, width), BF16),
            shape_of((latents, 3 * width, length), BF16),
            shape_of((latents, 8 * ((heads + 7) // 8), length), F32),
            shape_of((latents, width, length), BF16),
        ],
        [],
        [],
        [tokens, modulation],
        [qkv_full, qkv_bias],
        pl.CostEstimate(
            flops=2 * rows * width * (3 * width + 2 * length),
            bytes_accessed=rows * width * 12,
            transcendentals=rows * heads * length,
        ),
    )

    attended, silu_all = lax.optimization_barrier((attended, silu_all))
    (
        output,
        grad_middle,
        grad_attended,
        grad_mod_two,
        out_grad,
        up_grad,
        down_grad,
        out_bias_grad,
        up_bias_grad,
        down_bias_grad,
    ) = run_kernel(
        functools.partial(feed_kernel, chunk=256),
        4,
        [
            shape_of((latents, length, width), BF16),
            shape_of((latents, length, width), F32),
            shape_of((latents, width, length), BF16),
            shape_of((latents, 4, width), F32),
        ],
        [
            shape_of((width, width), BF16),
            shape_of((hidden_width, width), BF16),
            shape_of((width, hidden_width), BF16),
            shape_of((1, width), F32),
            shape_of((hidden_width, 128), F32),
            shape_of((1, width), F32),
        ],
        [
            pltpu.VMEM((width, width), F32),
            pltpu.VMEM((hidden_width, width + 128), F32),
            pltpu.VMEM((hidden_width, width), F32),
            pltpu.VMEM((8, width), F32),
            pltpu.VMEM((width, width), BF16),
            pltpu.VMEM((width, hidden_width), BF16),
            pltpu.VMEM((hidden_width, width), BF16),
            pltpu.VMEM((hidden_width, 4 * length), BF16),
            pltpu.VMEM((hidden_width, 4 * length), BF16),
            pltpu.VMEM((4 * length, width), F32),
            pltpu.VMEM((4 * length, width), F32),
            pltpu.VMEM((4 * length, width), F32),
        ],
        [tokens, cotangent, attended, modulation],
        [out_all, out_full, up_all, up_full, down_all, down_full],
        pl.CostEstimate(
            flops=6 * rows * width * (width + 2 * hidden_width),
            bytes_accessed=rows * width * 14,
            transcendentals=rows * hidden_width,
        ),
    )

    late_grad = jnp.concatenate(
        [
            up_grad.reshape(n_dp, up_rows, width),
            down_grad.reshape(n_dp, out_rows, folds, width)
            .transpose(0, 2, 1, 3)
            .reshape(n_dp, folds * out_rows, width),
            out_grad.reshape(n_dp, out_rows, width),
        ],
        axis=1,
    )
    late_sum = lax.psum_scatter(late_grad, "dp", scatter_dimension=0, tiled=True)
    late_sum = late_sum.reshape(-1, width)

    normed, ada_all = lax.optimization_barrier((normed, ada_all))
    grad_qkv, qkv_grad, qkv_bias_grad = run_kernel(
        attention_backward_kernel,
        2,
        [shape_of((latents, 3 * width, length), BF16)],
        [shape_of((3 * width, width), BF16), shape_of((3 * width, 128), F32)],
        [pltpu.VMEM((3 * width, width + 128), F32)],
        [qkv, lse, grad_attended, normed],
        [],
        pl.CostEstimate(flops=1, bytes_accessed=1, transcendentals=0),
    )

    qkv_columns = qkv_bias_grad[:, 0]
    bias_blocks = jnp.concatenate(
        [
            jnp.concatenate([qkv_columns[:width], qkv_columns[2 * width :]]).reshape(n_dp, -1),
            out_bias_grad.reshape(n_dp, -1),
            up_bias_grad[:, 0].reshape(n_dp, -1),
            down_bias_grad.reshape(n_dp, -1),
        ],
        axis=1,
    ).astype(BF16)
    bias_part = cuts[-1] // 2
    bias_blocks = bias_blocks.reshape(n_dp, 2, 1, bias_part)
    tail_rows = up_to(half_rows + 1, 8)
    bias_blocks = jnp.pad(
        bias_blocks,
        ((0, 0), (0, 0), (0, tail_rows - half_rows - 1), (0, width - bias_part)),
    )
    blocks = jnp.concatenate([qkv_grad.reshape(n_dp, 2, half_rows, width), bias_blocks], axis=2)
    kept, sent = hops.cut(blocks, "rep", 1, 1)
    total = kept.astype(F32) + hops.swap(sent, "rep", 1).astype(F32)

    tokens_grad, grad_mod_one = run_kernel(
        first_norm_kernel,
        4,
        [shape_of((latents, length, width), BF16), shape_of((latents, 2, width), F32)],
        [],
        [pltpu.VMEM((width, 3 * width), BF16)],
        [grad_qkv, tokens, grad_middle, modulation],
        [qkv_full],
        pl.CostEstimate(flops=1, bytes_accessed=1, transcendentals=0),
    )
    grad_modulation = jnp.concatenate([grad_mod_one, grad_mod_two], axis=1).reshape(
        latents, 6 * width
    )

    own = 6 * width // n_dp
    columns = grad_modulation.reshape(latents, n_dp, own).transpose(1, 0, 2).astype(BF16)
    columns = jnp.pad(columns, ((0, 0), (0, 0), (0, up_to(own, width) - own)))
    columns = columns.reshape((2,) * len(dp_bits) + (latents, width))
    total = total.reshape((2,) * len(dp_bits) + (tail_rows, width))
    axis = len(dp_bits) - 1
    for bit in dp_bits:
        kept, sent = hops.cut(total, "dp", bit, axis)
        column_kept, column_sent = hops.cut(columns, "dp", bit, axis)
        lead = sent.shape[:axis]
        sources = column_sent.shape[axis:-2]
        came = hops.swap(
            jnp.concatenate(
                [sent.astype(BF16), column_sent.reshape(lead + (-1, width))], axis=-2
            ),
            "dp",
            bit,
        )
        total = kept.astype(F32) + came[..., :tail_rows, :].astype(F32)
        column_came = came[..., tail_rows:, :].reshape(lead + sources + (latents, width))
        columns = hops.both(column_kept, column_came, "dp", bit, axis)
        axis -= 1
    columns = columns.reshape(n_dp * latents, width)

    qkv_total = total.astype(BF16)
    end = tail_rows + late_sum.shape[0]
    for bit in hops.bits("rep")[1:]:
        sums = jnp.concatenate([qkv_total, late_sum])
        came = hops.swap(jnp.concatenate([sums, columns]), "rep", bit)
        sums = (sums.astype(F32) + came[:end].astype(F32)).astype(BF16)
        qkv_total, late_sum = sums[:tail_rows], sums[tail_rows:]
        columns = hops.both(columns, came[end:], "rep", bit, 0).reshape(-1, width)
    came = hops.swap(jnp.concatenate([qkv_total, late_sum, columns]), "rep", 1)
    qkv_total = hops.both(qkv_total, came[:tail_rows], "rep", 1, 0).astype(F32)
    late_sum = late_sum.astype(F32) + came[tail_rows:end].astype(F32)
    columns = hops.both(columns, came[end:], "rep", 1, 0)
    columns = columns.reshape(2, n_rep // 2, n_dp * latents, width)[..., :own]
    columns = columns.transpose(1, 0, 2, 3).reshape(-1, own)
    qkv_owned = qkv_total[:, :half_rows].reshape(qkv_rows, width)
    bias_owned = qkv_total[:, half_rows, :bias_part].reshape(-1)
    up_owned = late_sum[:up_rows]
    down_owned = late_sum[up_rows : up_rows + folds * out_rows]
    down_owned = down_owned.reshape(folds, out_rows, width).transpose(1, 0, 2)
    down_owned = down_owned.reshape(out_rows, hidden_width)
    out_owned = late_sum[up_rows + folds * out_rows :]
    ada_grad = dot_tn(columns, silu_all)
    ada_bias_grad = jnp.sum(columns.astype(F32), axis=0)

    grad_silu = lax.dot_general(
        grad_modulation,
        ada_all.astype(F32),
        (((1,), (0,)), ((), ())),
        precision=lax.Precision.HIGHEST,
    )
    _, silu_pull = jax.vjp(jax.nn.silu, conditioning)
    condition_grad = silu_pull(grad_silu)[0]

    qv_sum, out_bias_sum, up_bias_sum, down_bias_sum = (
        bias_owned[low:high] for low, high in zip(cuts[:-1], cuts[1:])
    )
    return (
        output,
        tokens_grad,
        condition_grad,
        ada_grad.T,
        ada_bias_grad,
        qkv_owned.T,
        qv_sum,
        out_owned.T,
        out_bias_sum,
        up_owned.T,
        up_bias_sum,
        down_owned.T,
        down_bias_sum,
    )


def solution(mesh):
    return jax.shard_map(
        functools.partial(body, mesh.shape["dp"], mesh.shape["rep"]),
        mesh=mesh,
        in_specs=(
            P(("dp", "rep"), None, None),
            P(("dp", "rep"), None),
            P(None, "dp"),
            P("dp"),
            P(None, "dp"),
            P("dp"),
            P(None, "dp"),
            P("dp"),
            P(None, "dp"),
            P("dp"),
            P(None, "dp"),
            P("dp"),
            P(("dp", "rep"), None, None),
        ),
        out_specs=(
            P(("dp", "rep"), None, None),
            P(("dp", "rep"), None, None),
            P(("dp", "rep"), None),
            P(None, "dp"),
            P("dp"),
            P(None, "dp"),
            P("dp"),
            P(None, "dp"),
            P("dp"),
            P(None, "dp"),
            P("dp"),
            P(None, "dp"),
            P("dp"),
        ),
        check_vma=False,
    )
```

```python
import functools

import jax
import jax.numpy as jnp
from jax import lax
from jax.experimental import pallas as pl
from jax.experimental.pallas import tpu as pltpu
from jax.sharding import PartitionSpec as P

HEAD_DIM = 64
EPS = 1e-06
GELU_C = 0.7978845608028654
VMEM_LIMIT = 56 * 1024 * 1024
F32 = jnp.float32
BF16 = jnp.bfloat16


def dot_nn(left, right):
    return lax.dot_general(left, right, (((1,), (0,)), ((), ())), preferred_element_type=F32)


def dot_nt(left, right):
    return lax.dot_general(left, right, (((1,), (1,)), ((), ())), preferred_element_type=F32)


def dot_tn(left, right):
    return lax.dot_general(left, right, (((0,), (0,)), ((), ())), preferred_element_type=F32)


def normalise(values):
    average = jnp.mean(values, axis=-1, keepdims=True)
    centred = values - average
    spread = jnp.mean(centred * centred, axis=-1, keepdims=True)
    inverse = lax.rsqrt(spread + EPS)
    return centred * inverse, inverse


def normalise_back(upstream, normal, inverse):
    first = jnp.mean(upstream, axis=-1, keepdims=True)
    second = jnp.mean(upstream * normal, axis=-1, keepdims=True)
    return inverse * (upstream - first - normal * second)


STRIP = 64
GROUP = 3


def beside(*parts):
    return jnp.concatenate(parts, axis=1)


def above(*parts):
    return jnp.concatenate(parts, axis=0)


def strips(extent, size):
    return [slice(low, low + size) for low in range(0, extent, size)]


def head_slices(head):
    low = head * HEAD_DIM
    pair = low - low % (2 * HEAD_DIM)
    return slice(low, low + HEAD_DIM), slice(pair, pair + 2 * HEAD_DIM), low == pair


def in_groups(items, size):
    return [items[low : low + size] for low in range(0, len(items), size)]


def attention_forward_kernel(
    tokens_ref, mod_ref, weight_ref, bias_ref, normed_ref, qkv_ref, lse_ref, attended_ref
):
    latents, length, width = tokens_ref.shape
    blank = jnp.zeros((HEAD_DIM, length), BF16)
    for latent in range(latents):
        for rows in strips(length, STRIP):
            normal, _ = normalise(tokens_ref[latent, rows, :].astype(F32))
            normed = normal * (1.0 + mod_ref[latent, 1:2, :]) + mod_ref[latent, 0:1, :]
            normed_ref[latent, rows, :] = normed.astype(BF16)
    normed = normed_ref[...].reshape(latents * length, width)
    for part in strips(3 * width, 2 * HEAD_DIM):
        bias = bias_ref[part, :]
        qkv = dot_nt(weight_ref[part, :], normed) + beside(*([bias] * (latents * length // 128)))
        qkv = qkv.astype(BF16)
        for latent in range(latents):
            qkv_ref[latent, part, :] = qkv[:, latent * length : (latent + 1) * length]
    keys_all = [qkv_ref[latent, width : 2 * width, :].T for latent in range(latents)]

    def scores_of(latent, head):
        own, pair, first = head_slices(head)
        queries = qkv_ref[latent, own, :]
        queries = above(queries, blank) if first else above(blank, queries)
        return dot_nn(keys_all[latent][:, pair], queries)

    def probs_of(latent, head, scores):
        parts = []
        for columns in strips(length, 128):
            strip = scores[:, columns] * HEAD_DIM ** (-0.5)
            highest = jnp.max(strip, axis=0, keepdims=True)
            shifted = jnp.exp(strip - highest)
            total = jnp.sum(shifted, axis=0, keepdims=True)
            parts.append((shifted * (1.0 / total)).astype(BF16))
            lse_ref[latent, head : head + 1, columns] = highest + jnp.log(total)
        return beside(*parts)

    def attend(latent, head, probs):
        own, _, _ = head_slices(head)
        values_in = qkv_ref[latent, 2 * width + own.start : 2 * width + own.stop, :]
        attended_ref[latent, own, :] = dot_nn(values_in, probs).astype(BF16)

    items = [(latent, head) for latent in range(latents) for head in range(width // HEAD_DIM)]
    groups = in_groups(items, GROUP)
    scores = [scores_of(*item) for item in groups[0]]
    previous = []
    for place, group in enumerate(groups):
        later = groups[place + 1] if place + 1 < len(groups) else []
        next_scores = [scores_of(*item) for item in later]
        probs = [probs_of(*item, value) for item, value in zip(group, scores)]
        for item, value in previous:
            attend(*item, value)
        previous = list(zip(group, probs))
        scores = next_scores
    for item, value in previous:
        attend(*item, value)


def feed_kernel(
    tokens_ref,
    cotangent_ref,
    attended_ref,
    mod_ref,
    late_ref,
    out_bias_ref,
    up_bias_row_ref,
    down_bias_ref,
    output_ref,
    grad_middle_ref,
    grad_attended_ref,
    grad_mod_ref,
    late_grad_ref,
    out_bias_grad_ref,
    up_bias_grad_ref,
    down_bias_grad_ref,
    out_acc,
    up_acc,
    down_acc,
    bias_acc,
    out_weight_ref,
    up_weight_ref,
    down_weight_ref,
    up_bias_ref,
    out_back,
    up_back,
    down_back,
    active_all,
    grad_hidden_all,
    middle_all,
    normal_all,
    branch_all,
    *,
    chunk,
):
    step = pl.program_id(0)
    n_dp = late_ref.shape[0]
    latents, length, width = tokens_ref.shape
    hidden_width = up_weight_ref.shape[0]
    tokens_all = latents * length
    up_rows, out_rows = hidden_width // n_dp, width // n_dp
    out_low = up_rows + out_rows * (hidden_width // width)

    @pl.when(step == 0)
    def _():
        out_acc[...] = jnp.zeros_like(out_acc)
        up_acc[...] = jnp.zeros_like(up_acc)
        down_acc[...] = jnp.zeros_like(down_acc)
        bias_acc[...] = jnp.zeros_like(bias_acc)
        for owner in range(n_dp):
            up_weight_ref[owner * up_rows : (owner + 1) * up_rows, :] = late_ref[owner, :up_rows, :]
            outs = slice(owner * out_rows, (owner + 1) * out_rows)
            for fold in range(hidden_width // width):
                low = up_rows + fold * out_rows
                down_weight_ref[outs, fold * width : (fold + 1) * width] = late_ref[
                    owner, low : low + out_rows, :
                ]
            out_weight_ref[outs, :] = late_ref[owner, out_low:, :]
        out_back[...] = out_weight_ref[...].T
        up_back[...] = up_weight_ref[...].T
        down_back[...] = down_weight_ref[...].T
        up_bias_ref[...] = jnp.broadcast_to(up_bias_row_ref[...], (128, hidden_width)).T

    attended = beside(*[attended_ref[latent] for latent in range(latents)])
    branch_wide = dot_nn(out_weight_ref[...], attended)
    normed_parts = []
    grad_feed_parts = []
    inverses = []
    down_sum = jnp.zeros((1, width), F32)
    for latent in range(latents):
        gate_one = mod_ref[latent, 2:3, :]
        shift_two = mod_ref[latent, 3:4, :]
        scale_two = 1.0 + mod_ref[latent, 4:5, :]
        gate_two = mod_ref[latent, 5:6, :]
        branch_tall = branch_wide[:, latent * length : (latent + 1) * length].T
        for rows in strips(length, STRIP):
            there = slice(latent * length + rows.start, latent * length + rows.stop)
            branch = branch_tall[rows] + out_bias_ref[...]
            branch_all[there, :] = branch
            middle = tokens_ref[latent, rows, :].astype(F32) + gate_one * branch
            middle_all[there, :] = middle
            normal, inverse = normalise(middle)
            normal_all[there, :] = normal
            inverses.append(inverse)
            normed_parts.append((normal * scale_two + shift_two).astype(BF16))
            grad_feed = (cotangent_ref[latent, rows, :].astype(F32) * gate_two).astype(BF16)
            grad_feed_parts.append(grad_feed)
            down_sum += jnp.sum(grad_feed.astype(F32), axis=0, keepdims=True)
    bias_acc[0:1, :] += down_sum
    normed_all = above(*normed_parts)
    grad_feed_all = above(*grad_feed_parts)

    def products(rows):
        return (
            dot_nt(up_weight_ref[rows, :], normed_all),
            dot_nt(down_back[rows, :], grad_feed_all),
        )

    parts = strips(hidden_width, chunk)
    ahead = products(parts[0])
    for place, part in enumerate(parts):
        hidden_wide, grad_wide = ahead
        if place + 1 < len(parts):
            ahead = products(parts[place + 1])
        for rows in strips(chunk, STRIP):
            there = slice(part.start + rows.start, part.start + rows.stop)
            bias = up_bias_ref[there, :]
            bias = beside(bias, bias)
            for columns in strips(tokens_all, 256):
                hidden = hidden_wide[rows, columns] + bias
                square = hidden * hidden
                bent = jnp.tanh(hidden * (GELU_C + (GELU_C * 0.044715) * square))
                half = 0.5 + 0.5 * bent
                active_all[there, columns] = (hidden * half).astype(BF16)
                slope = half + hidden * (0.5 - 0.5 * (bent * bent)) * (
                    GELU_C + (3.0 * GELU_C * 0.044715) * square
                )
                grad_hidden_all[there, columns] = (grad_wide[rows, columns] * slope).astype(BF16)

    feed_wide = dot_nn(down_weight_ref[...], active_all[...])
    grad_normed_wide = dot_nn(up_back[...], grad_hidden_all[...])
    ones = jnp.ones((tokens_all, 128), BF16)
    up_acc[...] += dot_nn(grad_hidden_all[...], beside(normed_all, ones))
    down_acc[...] += dot_nn(active_all[...], grad_feed_all)

    grad_branch_parts = []
    out_sum = jnp.zeros((1, width), F32)
    for latent in range(latents):
        gate_one = mod_ref[latent, 2:3, :]
        scale_two = 1.0 + mod_ref[latent, 4:5, :]
        gate_two = mod_ref[latent, 5:6, :]
        here = slice(latent * length, (latent + 1) * length)
        feed_tall = feed_wide[:, here].T
        grad_normed_tall = grad_normed_wide[:, here].T
        sums = [jnp.zeros((1, width), F32) for _ in range(4)]
        for rows in strips(length, STRIP):
            there = slice(here.start + rows.start, here.start + rows.stop)
            feed = feed_tall[rows] + down_bias_ref[...]
            grad_normed = grad_normed_tall[rows]
            incoming = cotangent_ref[latent, rows, :].astype(F32)
            normal = normal_all[there, :]
            output_ref[latent, rows, :] = (middle_all[there, :] + gate_two * feed).astype(BF16)
            grad_middle = incoming + normalise_back(
                grad_normed * scale_two, normal, inverses[there.start // STRIP]
            )
            grad_middle_ref[latent, rows, :] = grad_middle
            grad_branch = (grad_middle * gate_one).astype(BF16)
            grad_branch_parts.append(grad_branch)
            terms = (
                grad_middle * branch_all[there, :],
                grad_normed,
                grad_normed * normal,
                incoming * feed,
            )
            for place, term in enumerate(terms):
                sums[place] += jnp.sum(term, axis=0, keepdims=True)
            out_sum += jnp.sum(grad_branch.astype(F32), axis=0, keepdims=True)
        grad_mod_ref[latent] = above(*sums)
    bias_acc[1:2, :] += out_sum
    grad_branch_all = above(*grad_branch_parts)
    grad_attended = dot_nt(out_back[...], grad_branch_all).astype(BF16)
    for latent in range(latents):
        grad_attended_ref[latent] = grad_attended[:, latent * length : (latent + 1) * length]
    out_acc[...] += dot_nn(attended, grad_branch_all)

    @pl.when(step == pl.num_programs(0) - 1)
    def _():
        out_back[...] = out_acc[...].T.astype(BF16)
        up_back[...] = down_acc[...].T.astype(BF16)
        for owner in range(n_dp):
            ups = slice(owner * up_rows, (owner + 1) * up_rows)
            late_grad_ref[owner, :up_rows, :] = up_acc[ups, :width].astype(BF16)
            outs = slice(owner * out_rows, (owner + 1) * out_rows)
            for fold in range(hidden_width // width):
                low = up_rows + fold * out_rows
                late_grad_ref[owner, low : low + out_rows, :] = up_back[
                    outs, fold * width : (fold + 1) * width
                ]
            late_grad_ref[owner, out_low:, :] = out_back[outs, :]
        up_bias_grad_ref[...] = up_acc[:, width:]
        down_bias_grad_ref[...] = bias_acc[0:1, :]
        out_bias_grad_ref[...] = bias_acc[1:2, :]


def attention_backward_kernel(
    qkv_ref,
    lse_ref,
    grad_attended_ref,
    normed_ref,
    tokens_ref,
    grad_middle_ref,
    mod_ref,
    weight_ref,
    tokens_grad_ref,
    grad_mod_ref,
    weight_grad_ref,
    bias_grad_ref,
    acc,
    weight_back,
    grad_qkv_ref,
):
    step = pl.program_id(0)
    latents, length, width = normed_ref.shape
    blank = jnp.zeros((HEAD_DIM, length), BF16)

    @pl.when(step == 0)
    def _():
        acc[...] = jnp.zeros_like(acc)
        weight_back[...] = weight_ref[...].T

    keys_all = [qkv_ref[latent, width : 2 * width, :].T for latent in range(latents)]
    values_all = [qkv_ref[latent, 2 * width : 3 * width, :].T for latent in range(latents)]

    def products(latent, head):
        own, pair, first = head_slices(head)
        queries = qkv_ref[latent, own, :]
        grad_out = grad_attended_ref[latent, own, :]
        queries = above(queries, blank) if first else above(blank, queries)
        grad_out = above(grad_out, blank) if first else above(blank, grad_out)
        return (
            dot_nn(keys_all[latent][:, pair], queries),
            dot_nn(values_all[latent][:, pair], grad_out),
        )

    def middle_of(latent, head, scores, grad_probs):
        low_parts = []
        grad_parts = []
        for columns in strips(length, 128):
            total = lse_ref[latent, head : head + 1, columns]
            probs = jnp.exp(scores[:, columns] * HEAD_DIM ** (-0.5) - total)
            terms = probs * grad_probs[:, columns]
            row_terms = jnp.sum(terms, axis=0, keepdims=True)
            grad_parts.append((probs * (grad_probs[:, columns] - row_terms)).astype(BF16))
            low_parts.append(probs.astype(BF16))
        return beside(*low_parts), beside(*grad_parts)

    def finish(latent, head, probs, grad_scores):
        own, _, _ = head_slices(head)
        low, high = own.start, own.stop
        queries = qkv_ref[latent, own, :]
        keys_in = qkv_ref[latent, width + low : width + high, :]
        grad_out = grad_attended_ref[latent, own, :]
        scale = HEAD_DIM ** (-0.5)
        grad_qkv_ref[latent, own, :] = (dot_nn(keys_in, grad_scores) * scale).astype(BF16)
        grad_qkv_ref[latent, width + low : width + high, :] = (
            dot_nt(queries, grad_scores) * scale
        ).astype(BF16)
        grad_qkv_ref[latent, 2 * width + low : 2 * width + high, :] = dot_nt(
            grad_out, probs
        ).astype(BF16)

    items = [(latent, head) for latent in range(latents) for head in range(width // HEAD_DIM)]
    groups = in_groups(items, GROUP)
    values = [products(*item) for item in groups[0]]
    previous = []
    for place, group in enumerate(groups):
        later = groups[place + 1] if place + 1 < len(groups) else []
        next_values = [products(*item) for item in later]
        middles = [middle_of(*item, *value) for item, value in zip(group, values)]
        for item, value in previous:
            finish(*item, *value)
        previous = list(zip(group, middles))
        values = next_values
    for item, value in previous:
        finish(*item, *value)

    grad_qkv = beside(*[grad_qkv_ref[latent] for latent in range(latents)])
    normed = normed_ref[...].reshape(latents * length, width)
    grad_normed_wide = dot_nn(weight_back[...], grad_qkv)
    acc[...] += dot_nn(grad_qkv, beside(normed, jnp.ones((latents * length, 128), BF16)))
    for latent in range(latents):
        grad_normed_tall = grad_normed_wide[:, latent * length : (latent + 1) * length].T
        scale_one = 1.0 + mod_ref[latent, 1:2, :]
        first = jnp.zeros((1, width), F32)
        second = jnp.zeros((1, width), F32)
        for rows in strips(length, STRIP):
            normal, inverse = normalise(tokens_ref[latent, rows, :].astype(F32))
            grad_normed = grad_normed_tall[rows]
            first += jnp.sum(grad_normed, axis=0, keepdims=True)
            second += jnp.sum(grad_normed * normal, axis=0, keepdims=True)
            back = normalise_back(grad_normed * scale_one, normal, inverse)
            tokens_grad_ref[latent, rows, :] = (grad_middle_ref[latent, rows, :] + back).astype(
                BF16
            )
        grad_mod_ref[latent] = above(first, second)

    @pl.when(step == pl.num_programs(0) - 1)
    def _():
        weight_grad_ref[...] = acc[:, :width].astype(BF16)
        bias_grad_ref[...] = acc[:, width:]


def finish_kernel(
    core_ref,
    mine_ref,
    came_ref,
    silu_ref,
    ada_ref,
    ada_bias_ref,
    qkv_ref,
    up_ref,
    down_ref,
    out_ref,
    bias_ref,
    *,
    tail_rows,
):
    first = core_ref[0] == 0
    own = ada_ref.shape[0]
    half_rows = qkv_ref.shape[0] // 2
    up_rows, out_rows = up_ref.shape[0], out_ref.shape[0]
    width = out_ref.shape[1]
    out_low = tail_rows + up_rows + down_ref.shape[1] // width * out_rows
    end = out_low + out_rows
    mine = mine_ref[:tail_rows, :].astype(F32)
    came = came_ref[:tail_rows, :].astype(F32)
    lower = jnp.where(first, mine, came)
    upper = jnp.where(first, came, mine)
    qkv_ref[:half_rows, :] = lower[:half_rows]
    qkv_ref[half_rows:, :] = upper[:half_rows]
    bias_ref[0:1, :] = lower[half_rows : half_rows + 1]
    bias_ref[1:2, :] = upper[half_rows : half_rows + 1]
    sums = mine_ref[tail_rows:end, :].astype(F32) + came_ref[tail_rows:end, :].astype(F32)
    up_ref[...] = sums[:up_rows]
    for fold in range(down_ref.shape[1] // width):
        low = up_rows + fold * out_rows
        down_ref[:, fold * width : (fold + 1) * width] = sums[low : low + out_rows]
    out_ref[...] = sums[out_low - tail_rows :]
    mine = mine_ref[end:, :]
    came = came_ref[end:, :]
    columns = above(jnp.where(first, mine, came), jnp.where(first, came, mine))
    ada_ref[...] = dot_tn(columns, silu_ref[...])[:own]
    ada_bias_ref[...] = jnp.sum(columns.astype(F32), axis=0, keepdims=True)


def each(shape, count):
    zeros = (0,) * (len(shape) - 1)
    return pl.BlockSpec((count,) + tuple(shape[1:]), lambda step: (step,) + zeros)


def whole(shape):
    zeros = (0,) * len(shape)
    return pl.BlockSpec(tuple(shape), lambda step: zeros)


def run_kernel(kernel, count, streamed_out, fixed_out, scratch, streamed, fixed, cost):
    return pl.pallas_call(
        kernel,
        grid=(streamed[0].shape[0] // count,),
        in_specs=[each(item.shape, count) for item in streamed]
        + [whole(item.shape) for item in fixed],
        out_specs=[each(item.shape, count) for item in streamed_out]
        + [whole(item.shape) for item in fixed_out],
        out_shape=list(streamed_out) + list(fixed_out),
        scratch_shapes=scratch,
        compiler_params=pltpu.CompilerParams(
            dimension_semantics=("arbitrary",), vmem_limit_bytes=VMEM_LIMIT
        ),
        cost_estimate=cost,
    )(*streamed, *fixed)


def shape_of(dims, kind):
    return jax.ShapeDtypeStruct(tuple(dims), kind)


AXES = ("dp", "rep")


class Hops:
    def __init__(self, n_dp, n_rep):
        self.sizes = {"dp": n_dp, "rep": n_rep}
        self.place = {name: lax.axis_index(name) for name in AXES}

    def bits(self, name):
        return [1 << shift for shift in range(self.sizes[name].bit_length() - 1)]

    def mine(self, name, bit):
        return (self.place[name] // bit) % 2

    def swap(self, value, name, bit):
        n_dp, n_rep = self.sizes["dp"], self.sizes["rep"]
        flip_dp, flip_rep = (bit, 0) if name == "dp" else (0, bit)
        pairs = [
            (d * n_rep + r, (d ^ flip_dp) * n_rep + (r ^ flip_rep))
            for d in range(n_dp)
            for r in range(n_rep)
        ]
        return lax.ppermute(value, AXES, pairs)

    def both(self, kept, came, name, bit, axis):
        upper = self.mine(name, bit) == 1
        return jnp.stack(
            [jnp.where(upper, came, kept), jnp.where(upper, kept, came)], axis=axis
        )

    def cut(self, value, name, bit, axis):
        here = self.mine(name, bit)
        return (
            lax.dynamic_index_in_dim(value, here, axis, keepdims=False),
            lax.dynamic_index_in_dim(value, 1 - here, axis, keepdims=False),
        )


def pad_rows(values, count):
    return jnp.pad(values, ((0, 0),) * (values.ndim - 2) + ((0, count - values.shape[-2]), (0, 0)))


def up_to(count, multiple):
    return -(-count // multiple) * multiple


def body(
    n_dp,
    n_rep,
    tokens,
    conditioning,
    ada_weight,
    ada_bias,
    qkv_weight,
    qv_bias,
    out_weight,
    out_bias,
    up_weight,
    up_bias,
    down_weight,
    down_bias,
    cotangent,
):
    latents, length, width = tokens.shape
    hidden_width = up_weight.shape[1] * n_dp
    heads = width // HEAD_DIM
    rows = latents * length
    hops = Hops(n_dp, n_rep)
    dp_bits = hops.bits("dp")
    folds = hidden_width // width

    up_rows, out_rows = up_weight.shape[1], out_weight.shape[1]
    down_shard = down_weight.T.reshape(out_rows, folds, width).transpose(1, 0, 2)
    late_shard = jnp.concatenate(
        [up_weight.T, down_shard.reshape(folds * out_rows, width), out_weight.T]
    )
    late = lax.all_gather(late_shard, "dp", axis=0)
    silu_low = jax.nn.silu(conditioning).astype(BF16)
    ada_shard, _ = lax.optimization_barrier((ada_weight.T, late))
    ada_all = lax.all_gather(ada_shard, "dp", axis=0, tiled=True)

    qkv_rows = qkv_weight.shape[1]
    half_rows = qkv_rows // 2
    core = hops.mine("rep", 1)
    bias_shard = jnp.concatenate([qv_bias, out_bias, up_bias, down_bias, ada_bias])
    bias_rows = up_to(bias_shard.shape[0], width) // width
    bias_block = jnp.pad(bias_shard, (0, bias_rows * width - bias_shard.shape[0]))
    front = jnp.concatenate(
        [
            lax.dynamic_slice_in_dim(qkv_weight.T, core * half_rows, half_rows, axis=0),
            silu_low,
            bias_block.reshape(bias_rows, width),
        ]
    )
    front = pad_rows(front, up_to(front.shape[0], 8))
    ada_pair = hops.both(ada_weight.T, hops.swap(ada_weight.T, "dp", 1), "dp", 1, 0)
    high_bits = dp_bits[:0:-1]
    for done, bit in enumerate(high_bits):
        front = hops.both(front, hops.swap(front, "dp", bit), "dp", bit, done)

    silu_part = front[..., half_rows : half_rows + latents, :].reshape(-1, width)
    mod = dot_nt(silu_part, ada_pair.reshape(-1, width))
    mod = mod.reshape((2,) * len(high_bits) + (latents, -1))
    for done, bit in enumerate(high_bits):
        kept, sent = hops.cut(mod, "dp", bit, done)
        mod = hops.both(kept, hops.swap(sent, "dp", bit), "dp", bit, done)
    mod = mod.reshape(n_dp // 2, latents, -1).transpose(1, 0, 2).reshape(latents, -1)

    front = hops.both(front, hops.swap(front, "dp", 1), "dp", 1, len(high_bits))
    front = front.reshape(n_dp, -1, width)
    front = front[:, : half_rows + latents + bias_rows]
    silu_group = front[:, half_rows : half_rows + latents].reshape(n_dp * latents, width)
    halves = front[:, : half_rows + latents]
    halves = hops.both(halves, hops.swap(halves, "rep", 1), "rep", 1, 0)
    qkv_full = halves[:, :, :half_rows].transpose(1, 0, 2, 3).reshape(3 * width, width)
    silu_all = halves[:, :, half_rows:]
    for bit in hops.bits("rep")[1:]:
        silu_all = hops.both(silu_all, hops.swap(silu_all, "rep", bit), "rep", bit, 0)
    silu_all = silu_all.reshape(n_rep // 2, 2, n_dp * latents, width).transpose(1, 0, 2, 3)
    silu_all = silu_all.reshape(-1, width)

    bias_all = front[:, half_rows + latents : half_rows + latents + bias_rows]
    bias_all = bias_all.reshape(n_dp, -1).astype(F32)
    cuts = [0]
    for part in (qv_bias, out_bias, up_bias, down_bias, ada_bias):
        cuts.append(cuts[-1] + part.shape[0])
    qv_full, out_full, up_full, down_full, ada_full = (
        bias_all[:, low:high].reshape(1, -1) for low, high in zip(cuts[:-1], cuts[1:])
    )
    qkv_bias = jnp.concatenate(
        [qv_full[:, :width], jnp.zeros((1, width), F32), qv_full[:, width:]], axis=1
    )
    qkv_bias = jnp.broadcast_to(qkv_bias.reshape(-1, 1), (3 * width, 128))

    modulation = (mod + ada_full).reshape(latents, 6, width)

    normed, qkv, lse, attended = run_kernel(
        attention_forward_kernel,
        4,
        [
            shape_of((latents, length, width), BF16),
            shape_of((latents, 3 * width, length), BF16),
            shape_of((latents, 8 * ((heads + 7) // 8), length), F32),
            shape_of((latents, width, length), BF16),
        ],
        [],
        [],
        [tokens, modulation],
        [qkv_full, qkv_bias],
        pl.CostEstimate(
            flops=2 * rows * width * (3 * width + 2 * length),
            bytes_accessed=rows * width * 12,
            transcendentals=rows * heads * length,
        ),
    )

    attended, silu_all = lax.optimization_barrier((attended, silu_all))
    (
        output,
        grad_middle,
        grad_attended,
        grad_mod_two,
        late_grad,
        out_bias_grad,
        up_bias_grad,
        down_bias_grad,
    ) = run_kernel(
        functools.partial(feed_kernel, chunk=256),
        4,
        [
            shape_of((latents, length, width), BF16),
            shape_of((latents, length, width), F32),
            shape_of((latents, width, length), BF16),
            shape_of((latents, 4, width), F32),
        ],
        [
            shape_of(late.shape, BF16),
            shape_of((1, width), F32),
            shape_of((hidden_width, 128), F32),
            shape_of((1, width), F32),
        ],
        [
            pltpu.VMEM((width, width), F32),
            pltpu.VMEM((hidden_width, width + 128), F32),
            pltpu.VMEM((hidden_width, width), F32),
            pltpu.VMEM((8, width), F32),
            pltpu.VMEM((width, width), BF16),
            pltpu.VMEM((hidden_width, width), BF16),
            pltpu.VMEM((width, hidden_width), BF16),
            pltpu.VMEM((hidden_width, 128), F32),
            pltpu.VMEM((width, width), BF16),
            pltpu.VMEM((width, hidden_width), BF16),
            pltpu.VMEM((hidden_width, width), BF16),
            pltpu.VMEM((hidden_width, 4 * length), BF16),
            pltpu.VMEM((hidden_width, 4 * length), BF16),
            pltpu.VMEM((4 * length, width), F32),
            pltpu.VMEM((4 * length, width), F32),
            pltpu.VMEM((4 * length, width), F32),
        ],
        [tokens, cotangent, attended, modulation],
        [late, out_full, up_full, down_full],
        pl.CostEstimate(
            flops=6 * rows * width * (width + 2 * hidden_width),
            bytes_accessed=rows * width * 14,
            transcendentals=rows * hidden_width,
        ),
    )

    late_sum = lax.psum_scatter(late_grad, "dp", scatter_dimension=0, tiled=True)
    late_sum = late_sum.reshape(-1, width)

    normed, ada_all = lax.optimization_barrier((normed, ada_all))
    tokens_grad, grad_mod_one, qkv_grad, qkv_bias_grad = run_kernel(
        attention_backward_kernel,
        2,
        [shape_of((latents, length, width), BF16), shape_of((latents, 2, width), F32)],
        [shape_of((3 * width, width), BF16), shape_of((3 * width, 128), F32)],
        [
            pltpu.VMEM((3 * width, width + 128), F32),
            pltpu.VMEM((width, 3 * width), BF16),
            pltpu.VMEM((2, 3 * width, length), BF16),
        ],
        [qkv, lse, grad_attended, normed, tokens, grad_middle, modulation],
        [qkv_full],
        pl.CostEstimate(flops=1, bytes_accessed=1, transcendentals=0),
    )

    qkv_columns = qkv_bias_grad[:, 0]
    bias_blocks = jnp.concatenate(
        [
            jnp.concatenate([qkv_columns[:width], qkv_columns[2 * width :]]).reshape(n_dp, -1),
            out_bias_grad.reshape(n_dp, -1),
            up_bias_grad[:, 0].reshape(n_dp, -1),
            down_bias_grad.reshape(n_dp, -1),
        ],
        axis=1,
    ).astype(BF16)
    bias_part = cuts[-2] // 2
    bias_blocks = bias_blocks.reshape(n_dp, 2, 1, bias_part)
    tail_rows = up_to(half_rows + 1, 8)
    bias_blocks = jnp.pad(
        bias_blocks,
        ((0, 0), (0, 0), (0, tail_rows - half_rows - 1), (0, width - bias_part)),
    )
    blocks = jnp.concatenate([qkv_grad.reshape(n_dp, 2, half_rows, width), bias_blocks], axis=2)
    kept, sent = hops.cut(blocks, "rep", 1, 1)
    total = kept.astype(F32) + hops.swap(sent, "rep", 1).astype(F32)

    grad_modulation = jnp.concatenate([grad_mod_one, grad_mod_two], axis=1).reshape(
        latents, 6 * width
    )

    own = 6 * width // n_dp
    columns = grad_modulation.reshape(latents, n_dp, own).transpose(1, 0, 2).astype(BF16)
    columns = jnp.pad(columns, ((0, 0), (0, 0), (0, up_to(own, width) - own)))
    columns = columns.reshape((2,) * len(dp_bits) + (latents, width))
    total = total.reshape((2,) * len(dp_bits) + (tail_rows, width))
    axis = len(dp_bits) - 1
    for bit in dp_bits:
        kept, sent = hops.cut(total, "dp", bit, axis)
        column_kept, column_sent = hops.cut(columns, "dp", bit, axis)
        lead = sent.shape[:axis]
        sources = column_sent.shape[axis:-2]
        came = hops.swap(
            jnp.concatenate(
                [sent.astype(BF16), column_sent.reshape(lead + (-1, width))], axis=-2
            ),
            "dp",
            bit,
        )
        total = kept.astype(F32) + came[..., :tail_rows, :].astype(F32)
        column_came = came[..., tail_rows:, :].reshape(lead + sources + (latents, width))
        columns = hops.both(column_kept, column_came, "dp", bit, axis)
        axis -= 1
    columns = columns.reshape(n_dp * latents, width)

    qkv_total = total.astype(BF16)
    end = tail_rows + late_sum.shape[0]
    for bit in hops.bits("rep")[1:]:
        sums = jnp.concatenate([qkv_total, late_sum])
        came = hops.swap(jnp.concatenate([sums, columns]), "rep", bit)
        sums = (sums.astype(F32) + came[:end].astype(F32)).astype(BF16)
        qkv_total, late_sum = sums[:tail_rows], sums[tail_rows:]
        columns = hops.both(columns, came[end:], "rep", bit, 0).reshape(-1, width)
    mine = jnp.concatenate([qkv_total, late_sum, columns])
    came = hops.swap(mine, "rep", 1)
    smem = pl.BlockSpec(memory_space=pltpu.SMEM)
    vmem = pl.BlockSpec(memory_space=pltpu.VMEM)
    ada_grad, ada_bias_grad, qkv_owned, up_owned, down_owned, out_owned, bias_owned = pl.pallas_call(
        functools.partial(finish_kernel, tail_rows=tail_rows),
        in_specs=[smem, vmem, vmem, vmem],
        out_specs=[vmem] * 7,
        out_shape=[
            shape_of((own, width), F32),
            shape_of((1, width), F32),
            shape_of((qkv_rows, width), F32),
            shape_of((up_rows, width), F32),
            shape_of((out_rows, hidden_width), F32),
            shape_of((out_rows, width), F32),
            shape_of((2, width), F32),
        ],
        compiler_params=pltpu.CompilerParams(vmem_limit_bytes=VMEM_LIMIT),
    )(core.astype(jnp.int32).reshape(1), mine, came, silu_all)
    ada_bias_grad = ada_bias_grad[0, :own]
    bias_owned = bias_owned[:, :bias_part].reshape(-1)

    grad_silu = lax.dot_general(
        grad_modulation,
        ada_all.astype(F32),
        (((1,), (0,)), ((), ())),
        precision=lax.Precision.HIGHEST,
    )
    _, silu_pull = jax.vjp(jax.nn.silu, conditioning)
    condition_grad = silu_pull(grad_silu)[0]

    qv_sum, out_bias_sum, up_bias_sum, down_bias_sum = (
        bias_owned[low:high] for low, high in zip(cuts[:-2], cuts[1:-1])
    )
    return (
        output,
        tokens_grad,
        condition_grad,
        ada_grad.T,
        ada_bias_grad,
        qkv_owned.T,
        qv_sum,
        out_owned.T,
        out_bias_sum,
        up_owned.T,
        up_bias_sum,
        down_owned.T,
        down_bias_sum,
    )


def solution(mesh):
    return jax.shard_map(
        functools.partial(body, mesh.shape["dp"], mesh.shape["rep"]),
        mesh=mesh,
        in_specs=(
            P(("dp", "rep"), None, None),
            P(("dp", "rep"), None),
            P(None, "dp"),
            P("dp"),
            P(None, "dp"),
            P("dp"),
            P(None, "dp"),
            P("dp"),
            P(None, "dp"),
            P("dp"),
            P(None, "dp"),
            P("dp"),
            P(("dp", "rep"), None, None),
        ),
        out_specs=(
            P(("dp", "rep"), None, None),
            P(("dp", "rep"), None, None),
            P(("dp", "rep"), None),
            P(None, "dp"),
            P("dp"),
            P(None, "dp"),
            P("dp"),
            P(None, "dp"),
            P("dp"),
            P(None, "dp"),
            P("dp"),
            P(None, "dp"),
            P("dp"),
        ),
        check_vma=False,
    )
```

```python
import functools

import jax
import jax.numpy as jnp
from jax import lax
from jax.experimental import pallas as pl
from jax.experimental.pallas import tpu as pltpu
from jax.sharding import PartitionSpec as P

HEAD_DIM = 64
EPS = 1e-06
GELU_C = 0.7978845608028654
VMEM_LIMIT = 56 * 1024 * 1024
F32 = jnp.float32
BF16 = jnp.bfloat16


def dot_nn(left, right):
    return lax.dot_general(left, right, (((1,), (0,)), ((), ())), preferred_element_type=F32)


def dot_nt(left, right):
    return lax.dot_general(left, right, (((1,), (1,)), ((), ())), preferred_element_type=F32)


def dot_tn(left, right):
    return lax.dot_general(left, right, (((0,), (0,)), ((), ())), preferred_element_type=F32)


def normalise(values):
    average = jnp.mean(values, axis=-1, keepdims=True)
    centred = values - average
    spread = jnp.mean(centred * centred, axis=-1, keepdims=True)
    inverse = lax.rsqrt(spread + EPS)
    return centred * inverse, inverse


def normalise_back(upstream, normal, inverse):
    first = jnp.mean(upstream, axis=-1, keepdims=True)
    second = jnp.mean(upstream * normal, axis=-1, keepdims=True)
    return inverse * (upstream - first - normal * second)


STRIP = 64
GROUP = 6


def beside(*parts):
    return jnp.concatenate(parts, axis=1)


def above(*parts):
    return jnp.concatenate(parts, axis=0)


def strips(extent, size):
    return [slice(low, low + size) for low in range(0, extent, size)]


def head_slices(head):
    low = head * HEAD_DIM
    pair = low - low % (2 * HEAD_DIM)
    return slice(low, low + HEAD_DIM), slice(pair, pair + 2 * HEAD_DIM), low == pair


def in_groups(items, size):
    return [items[low : low + size] for low in range(0, len(items), size)]


def attention_forward_kernel(
    core_ref,
    tokens_ref,
    mod_ref,
    mine_ref,
    came_ref,
    bias_row_ref,
    normed_ref,
    qkv_ref,
    lse_ref,
    attended_ref,
    weight_ref,
    bias_ref,
):
    latents, length, width = tokens_ref.shape
    blank = jnp.zeros((HEAD_DIM, length), BF16)

    @pl.when(pl.program_id(0) == 0)
    def _():
        first = core_ref[0] == 0
        n_dp = mine_ref.shape[0]
        half_rows = weight_ref.shape[0] // (2 * n_dp)
        for owner in range(n_dp):
            mine = mine_ref[owner, :half_rows, :]
            came = came_ref[owner, :half_rows, :]
            low = 2 * owner * half_rows
            weight_ref[low : low + half_rows, :] = jnp.where(first, mine, came)
            weight_ref[low + half_rows : low + 2 * half_rows, :] = jnp.where(first, came, mine)
        bias_ref[...] = jnp.broadcast_to(bias_row_ref[...], (128, 3 * width)).T

    for latent in range(latents):
        for rows in strips(length, STRIP):
            normal, _ = normalise(tokens_ref[latent, rows, :].astype(F32))
            normed = normal * (1.0 + mod_ref[latent, 1:2, :]) + mod_ref[latent, 0:1, :]
            normed_ref[latent, rows, :] = normed.astype(BF16)
    normed = normed_ref[...].reshape(latents * length, width)
    for part in strips(3 * width, 2 * HEAD_DIM):
        bias = bias_ref[part, :]
        qkv = dot_nt(weight_ref[part, :], normed) + beside(*([bias] * (latents * length // 128)))
        qkv = qkv.astype(BF16)
        for latent in range(latents):
            qkv_ref[latent, part, :] = qkv[:, latent * length : (latent + 1) * length]
    keys_all = [qkv_ref[latent, width : 2 * width, :].T for latent in range(latents)]

    def scores_of(latent, head):
        own, pair, first = head_slices(head)
        queries = qkv_ref[latent, own, :]
        queries = above(queries, blank) if first else above(blank, queries)
        return dot_nn(keys_all[latent][:, pair], queries)

    def probs_of(latent, head, scores):
        parts = []
        for columns in strips(length, 128):
            strip = scores[:, columns] * HEAD_DIM ** (-0.5)
            highest = jnp.max(strip, axis=0, keepdims=True)
            shifted = jnp.exp(strip - highest)
            total = jnp.sum(shifted, axis=0, keepdims=True)
            parts.append((shifted * (1.0 / total)).astype(BF16))
            lse_ref[latent, head : head + 1, columns] = highest + jnp.log(total)
        return beside(*parts)

    def attend(latent, head, probs):
        own, _, _ = head_slices(head)
        values_in = qkv_ref[latent, 2 * width + own.start : 2 * width + own.stop, :]
        attended_ref[latent, own, :] = dot_nn(values_in, probs).astype(BF16)

    items = [(latent, head) for latent in range(latents) for head in range(width // HEAD_DIM)]
    groups = in_groups(items, GROUP)
    scores = [scores_of(*item) for item in groups[0]]
    previous = []
    for place, group in enumerate(groups):
        later = groups[place + 1] if place + 1 < len(groups) else []
        next_scores = [scores_of(*item) for item in later]
        probs = [probs_of(*item, value) for item, value in zip(group, scores)]
        for item, value in previous:
            attend(*item, value)
        previous = list(zip(group, probs))
        scores = next_scores
    for item, value in previous:
        attend(*item, value)


def feed_kernel(
    tokens_ref,
    cotangent_ref,
    attended_ref,
    mod_ref,
    late_ref,
    out_bias_ref,
    up_bias_row_ref,
    down_bias_ref,
    output_ref,
    grad_middle_ref,
    grad_attended_ref,
    grad_mod_ref,
    late_grad_ref,
    out_bias_grad_ref,
    up_bias_grad_ref,
    down_bias_grad_ref,
    out_acc,
    up_acc,
    down_acc,
    bias_acc,
    out_weight_ref,
    up_weight_ref,
    down_weight_ref,
    up_bias_ref,
    out_back,
    up_back,
    down_back,
    active_all,
    grad_hidden_all,
    middle_all,
    normal_all,
    branch_all,
    *,
    chunk,
):
    step = pl.program_id(0)
    n_dp = late_ref.shape[0]
    latents, length, width = tokens_ref.shape
    hidden_width = up_weight_ref.shape[0]
    tokens_all = latents * length
    up_rows, out_rows = hidden_width // n_dp, width // n_dp
    out_low = up_rows + out_rows * (hidden_width // width)

    @pl.when(step == 0)
    def _():
        out_acc[...] = jnp.zeros_like(out_acc)
        up_acc[...] = jnp.zeros_like(up_acc)
        down_acc[...] = jnp.zeros_like(down_acc)
        bias_acc[...] = jnp.zeros_like(bias_acc)
        for owner in range(n_dp):
            up_weight_ref[owner * up_rows : (owner + 1) * up_rows, :] = late_ref[owner, :up_rows, :]
            outs = slice(owner * out_rows, (owner + 1) * out_rows)
            for fold in range(hidden_width // width):
                low = up_rows + fold * out_rows
                down_weight_ref[outs, fold * width : (fold + 1) * width] = late_ref[
                    owner, low : low + out_rows, :
                ]
            out_weight_ref[outs, :] = late_ref[owner, out_low:, :]
        out_back[...] = out_weight_ref[...].T
        up_back[...] = up_weight_ref[...].T
        down_back[...] = down_weight_ref[...].T
        up_bias_ref[...] = jnp.broadcast_to(up_bias_row_ref[...], (128, hidden_width)).T

    attended = beside(*[attended_ref[latent] for latent in range(latents)])
    branch_wide = dot_nn(out_weight_ref[...], attended)
    normed_parts = []
    grad_feed_parts = []
    inverses = []
    down_sum = jnp.zeros((1, width), F32)
    for latent in range(latents):
        gate_one = mod_ref[latent, 2:3, :]
        shift_two = mod_ref[latent, 3:4, :]
        scale_two = 1.0 + mod_ref[latent, 4:5, :]
        gate_two = mod_ref[latent, 5:6, :]
        branch_tall = branch_wide[:, latent * length : (latent + 1) * length].T
        for rows in strips(length, STRIP):
            there = slice(latent * length + rows.start, latent * length + rows.stop)
            branch = branch_tall[rows] + out_bias_ref[...]
            branch_all[there, :] = branch
            middle = tokens_ref[latent, rows, :].astype(F32) + gate_one * branch
            middle_all[there, :] = middle
            normal, inverse = normalise(middle)
            normal_all[there, :] = normal
            inverses.append(inverse)
            normed_parts.append((normal * scale_two + shift_two).astype(BF16))
            grad_feed = (cotangent_ref[latent, rows, :].astype(F32) * gate_two).astype(BF16)
            grad_feed_parts.append(grad_feed)
            down_sum += jnp.sum(grad_feed.astype(F32), axis=0, keepdims=True)
    bias_acc[0:1, :] += down_sum
    normed_all = above(*normed_parts)
    grad_feed_all = above(*grad_feed_parts)

    def products(rows):
        return (
            dot_nt(up_weight_ref[rows, :], normed_all),
            dot_nt(down_back[rows, :], grad_feed_all),
        )

    parts = strips(hidden_width, chunk)
    ahead = products(parts[0])
    for place, part in enumerate(parts):
        hidden_wide, grad_wide = ahead
        if place + 1 < len(parts):
            ahead = products(parts[place + 1])
        for rows in strips(chunk, STRIP):
            there = slice(part.start + rows.start, part.start + rows.stop)
            bias = up_bias_ref[there, :]
            bias = beside(bias, bias)
            for columns in strips(tokens_all, 256):
                hidden = hidden_wide[rows, columns] + bias
                square = hidden * hidden
                bent = jnp.tanh(hidden * (GELU_C + (GELU_C * 0.044715) * square))
                half = 0.5 + 0.5 * bent
                active_all[there, columns] = (hidden * half).astype(BF16)
                slope = half + hidden * (0.5 - 0.5 * (bent * bent)) * (
                    GELU_C + (3.0 * GELU_C * 0.044715) * square
                )
                grad_hidden_all[there, columns] = (grad_wide[rows, columns] * slope).astype(BF16)

    feed_wide = dot_nn(down_weight_ref[...], active_all[...])
    grad_normed_wide = dot_nn(up_back[...], grad_hidden_all[...])
    ones = jnp.ones((tokens_all, 128), BF16)
    up_acc[...] += dot_nn(grad_hidden_all[...], beside(normed_all, ones))
    down_acc[...] += dot_nn(active_all[...], grad_feed_all)

    grad_branch_parts = []
    out_sum = jnp.zeros((1, width), F32)
    for latent in range(latents):
        gate_one = mod_ref[latent, 2:3, :]
        scale_two = 1.0 + mod_ref[latent, 4:5, :]
        gate_two = mod_ref[latent, 5:6, :]
        here = slice(latent * length, (latent + 1) * length)
        feed_tall = feed_wide[:, here].T
        grad_normed_tall = grad_normed_wide[:, here].T
        sums = [jnp.zeros((1, width), F32) for _ in range(4)]
        for rows in strips(length, STRIP):
            there = slice(here.start + rows.start, here.start + rows.stop)
            feed = feed_tall[rows] + down_bias_ref[...]
            grad_normed = grad_normed_tall[rows]
            incoming = cotangent_ref[latent, rows, :].astype(F32)
            normal = normal_all[there, :]
            output_ref[latent, rows, :] = (middle_all[there, :] + gate_two * feed).astype(BF16)
            grad_middle = incoming + normalise_back(
                grad_normed * scale_two, normal, inverses[there.start // STRIP]
            )
            grad_middle_ref[latent, rows, :] = grad_middle
            grad_branch = (grad_middle * gate_one).astype(BF16)
            grad_branch_parts.append(grad_branch)
            terms = (
                grad_middle * branch_all[there, :],
                grad_normed,
                grad_normed * normal,
                incoming * feed,
            )
            for place, term in enumerate(terms):
                sums[place] += jnp.sum(term, axis=0, keepdims=True)
            out_sum += jnp.sum(grad_branch.astype(F32), axis=0, keepdims=True)
        grad_mod_ref[latent] = above(*sums)
    bias_acc[1:2, :] += out_sum
    grad_branch_all = above(*grad_branch_parts)
    grad_attended = dot_nt(out_back[...], grad_branch_all).astype(BF16)
    for latent in range(latents):
        grad_attended_ref[latent] = grad_attended[:, latent * length : (latent + 1) * length]
    out_acc[...] += dot_nn(attended, grad_branch_all)

    @pl.when(step == pl.num_programs(0) - 1)
    def _():
        out_tall = out_acc[...].T
        up_back[...] = down_acc[...].T.astype(BF16)
        folds = hidden_width // width // 2
        for side in range(2):
            for owner in range(n_dp):
                ups = owner * up_rows + side * (up_rows // 2)
                late_grad_ref[side, owner, : up_rows // 2, :] = up_acc[
                    ups : ups + up_rows // 2, :width
                ].astype(BF16)
                outs = slice(owner * out_rows, (owner + 1) * out_rows)
                for place in range(folds):
                    low = up_rows // 2 + place * out_rows
                    fold = side * folds + place
                    late_grad_ref[side, owner, low : low + out_rows, :] = up_back[
                        outs, fold * width : (fold + 1) * width
                    ]
                outs = owner * out_rows + side * (out_rows // 2)
                late_grad_ref[side, owner, out_low // 2 :, :] = out_tall[
                    outs : outs + out_rows // 2
                ].astype(BF16)
        up_bias_grad_ref[...] = up_acc[:, width:]
        down_bias_grad_ref[...] = bias_acc[0:1, :]
        out_bias_grad_ref[...] = bias_acc[1:2, :]


def attention_backward_kernel(
    qkv_ref,
    lse_ref,
    grad_attended_ref,
    normed_ref,
    tokens_ref,
    grad_middle_ref,
    mod_ref,
    weight_ref,
    tokens_grad_ref,
    grad_mod_ref,
    weight_grad_ref,
    bias_grad_ref,
    acc,
    weight_back,
    grad_qkv_ref,
):
    step = pl.program_id(0)
    latents, length, width = normed_ref.shape
    blank = jnp.zeros((HEAD_DIM, length), BF16)

    @pl.when(step == 0)
    def _():
        acc[...] = jnp.zeros_like(acc)
        weight_back[...] = weight_ref[...].T

    keys_all = [qkv_ref[latent, width : 2 * width, :].T for latent in range(latents)]
    values_all = [qkv_ref[latent, 2 * width : 3 * width, :].T for latent in range(latents)]

    def products(latent, head):
        own, pair, first = head_slices(head)
        queries = qkv_ref[latent, own, :]
        grad_out = grad_attended_ref[latent, own, :]
        queries = above(queries, blank) if first else above(blank, queries)
        grad_out = above(grad_out, blank) if first else above(blank, grad_out)
        return (
            dot_nn(keys_all[latent][:, pair], queries),
            dot_nn(values_all[latent][:, pair], grad_out),
        )

    def middle_of(latent, head, scores, grad_probs):
        low_parts = []
        grad_parts = []
        for columns in strips(length, 128):
            total = lse_ref[latent, head : head + 1, columns]
            probs = jnp.exp(scores[:, columns] * HEAD_DIM ** (-0.5) - total)
            terms = probs * grad_probs[:, columns]
            row_terms = jnp.sum(terms, axis=0, keepdims=True)
            grad_parts.append((probs * (grad_probs[:, columns] - row_terms)).astype(BF16))
            low_parts.append(probs.astype(BF16))
        return beside(*low_parts), beside(*grad_parts)

    def finish(latent, head, probs, grad_scores):
        own, _, _ = head_slices(head)
        low, high = own.start, own.stop
        queries = qkv_ref[latent, own, :]
        keys_in = qkv_ref[latent, width + low : width + high, :]
        grad_out = grad_attended_ref[latent, own, :]
        scale = HEAD_DIM ** (-0.5)
        grad_qkv_ref[latent, own, :] = (dot_nn(keys_in, grad_scores) * scale).astype(BF16)
        grad_qkv_ref[latent, width + low : width + high, :] = (
            dot_nt(queries, grad_scores) * scale
        ).astype(BF16)
        grad_qkv_ref[latent, 2 * width + low : 2 * width + high, :] = dot_nt(
            grad_out, probs
        ).astype(BF16)

    items = [(latent, head) for latent in range(latents) for head in range(width // HEAD_DIM)]
    groups = in_groups(items, GROUP)
    values = [products(*item) for item in groups[0]]
    previous = []
    for place, group in enumerate(groups):
        later = groups[place + 1] if place + 1 < len(groups) else []
        next_values = [products(*item) for item in later]
        middles = [middle_of(*item, *value) for item, value in zip(group, values)]
        for item, value in previous:
            finish(*item, *value)
        previous = list(zip(group, middles))
        values = next_values
    for item, value in previous:
        finish(*item, *value)

    grad_qkv = beside(*[grad_qkv_ref[latent] for latent in range(latents)])
    normed = normed_ref[...].reshape(latents * length, width)
    grad_normed_wide = dot_nn(weight_back[...], grad_qkv)
    acc[...] += dot_nn(grad_qkv, beside(normed, jnp.ones((latents * length, 128), BF16)))
    for latent in range(latents):
        grad_normed_tall = grad_normed_wide[:, latent * length : (latent + 1) * length].T
        scale_one = 1.0 + mod_ref[latent, 1:2, :]
        first = jnp.zeros((1, width), F32)
        second = jnp.zeros((1, width), F32)
        for rows in strips(length, STRIP):
            normal, inverse = normalise(tokens_ref[latent, rows, :].astype(F32))
            grad_normed = grad_normed_tall[rows]
            first += jnp.sum(grad_normed, axis=0, keepdims=True)
            second += jnp.sum(grad_normed * normal, axis=0, keepdims=True)
            back = normalise_back(grad_normed * scale_one, normal, inverse)
            tokens_grad_ref[latent, rows, :] = (grad_middle_ref[latent, rows, :] + back).astype(
                BF16
            )
        grad_mod_ref[latent] = above(first, second)

    @pl.when(step == pl.num_programs(0) - 1)
    def _():
        n_dp, _, tail_rows, _ = weight_grad_ref.shape
        half_rows = 3 * width // (2 * n_dp)
        for owner in range(n_dp):
            for side in range(2):
                low = (2 * owner + side) * half_rows
                rows = acc[low : low + half_rows, :width]
                rest = jnp.zeros((tail_rows - half_rows, width), F32)
                weight_grad_ref[owner, side] = above(rows, rest).astype(BF16)
        bias_grad_ref[...] = acc[:, width:]


def finish_kernel(
    core_ref,
    mine_ref,
    came_ref,
    silu_ref,
    ada_ref,
    ada_bias_ref,
    qkv_ref,
    up_ref,
    down_ref,
    out_ref,
    qv_bias_ref,
    out_bias_ref,
    up_bias_ref,
    down_bias_ref,
    *,
    tail_rows,
):
    first = core_ref[0] == 0
    own = ada_ref.shape[0]
    half_rows = qkv_ref.shape[0] // 2
    up_half, out_rows = up_ref.shape[0] // 2, out_ref.shape[0]
    width = out_ref.shape[1]
    folds = down_ref.shape[1] // width // 2
    out_low = tail_rows + up_half + folds * out_rows
    end = out_low + out_rows // 2
    mine = mine_ref[:end, :].astype(F32)
    came = came_ref[:end, :].astype(F32)
    for side in range(2):
        part = jnp.where(first, mine, came) if side == 0 else jnp.where(first, came, mine)
        qkv_ref[side * half_rows : (side + 1) * half_rows, :] = part[:half_rows]
        up_ref[side * up_half : (side + 1) * up_half, :] = part[tail_rows : tail_rows + up_half]
        for place in range(folds):
            low = tail_rows + up_half + place * out_rows
            columns = (side * folds + place) * width
            down_ref[:, columns : columns + width] = part[low : low + out_rows]
        out_ref[side * (out_rows // 2) : (side + 1) * (out_rows // 2), :] = part[out_low:]
    biases = mine[half_rows : half_rows + 1] + came[half_rows : half_rows + 1]
    low = 0
    for ref in (qv_bias_ref, out_bias_ref, up_bias_ref, down_bias_ref):
        ref[...] = biases[:, low : low + ref.shape[1]]
        low += ref.shape[1]
    mine = mine_ref[end:, :]
    came = came_ref[end:, :]
    columns = above(jnp.where(first, mine, came), jnp.where(first, came, mine))
    ada_ref[...] = dot_tn(columns, silu_ref[...])[:own]
    ada_bias_ref[...] = jnp.sum(columns.astype(F32), axis=0, keepdims=True)[:, :own]


def each(shape, count):
    zeros = (0,) * (len(shape) - 1)
    return pl.BlockSpec((count,) + tuple(shape[1:]), lambda step: (step,) + zeros)


def whole(shape):
    zeros = (0,) * len(shape)
    return pl.BlockSpec(tuple(shape), lambda step: zeros)


def run_kernel(kernel, count, streamed_out, fixed_out, scratch, streamed, fixed, cost, scalars=()):
    return pl.pallas_call(
        kernel,
        grid=(streamed[0].shape[0] // count,),
        in_specs=[pl.BlockSpec(memory_space=pltpu.SMEM)] * len(scalars)
        + [each(item.shape, count) for item in streamed]
        + [whole(item.shape) for item in fixed],
        out_specs=[each(item.shape, count) for item in streamed_out]
        + [whole(item.shape) for item in fixed_out],
        out_shape=list(streamed_out) + list(fixed_out),
        scratch_shapes=scratch,
        compiler_params=pltpu.CompilerParams(
            dimension_semantics=("arbitrary",), vmem_limit_bytes=VMEM_LIMIT
        ),
        cost_estimate=cost,
    )(*scalars, *streamed, *fixed)


def shape_of(dims, kind):
    return jax.ShapeDtypeStruct(tuple(dims), kind)


AXES = ("dp", "rep")


class Hops:
    def __init__(self, n_dp, n_rep):
        self.sizes = {"dp": n_dp, "rep": n_rep}
        self.place = {name: lax.axis_index(name) for name in AXES}

    def bits(self, name):
        return [1 << shift for shift in range(self.sizes[name].bit_length() - 1)]

    def mine(self, name, bit):
        return (self.place[name] // bit) % 2

    def swap(self, value, name, bit):
        n_dp, n_rep = self.sizes["dp"], self.sizes["rep"]
        flip_dp, flip_rep = (bit, 0) if name == "dp" else (0, bit)
        pairs = [
            (d * n_rep + r, (d ^ flip_dp) * n_rep + (r ^ flip_rep))
            for d in range(n_dp)
            for r in range(n_rep)
        ]
        return lax.ppermute(value, AXES, pairs)

    def both(self, kept, came, name, bit, axis):
        upper = self.mine(name, bit) == 1
        return jnp.stack(
            [jnp.where(upper, came, kept), jnp.where(upper, kept, came)], axis=axis
        )

    def cut(self, value, name, bit, axis):
        here = self.mine(name, bit)
        return (
            lax.dynamic_index_in_dim(value, here, axis, keepdims=False),
            lax.dynamic_index_in_dim(value, 1 - here, axis, keepdims=False),
        )


def pad_rows(values, count):
    return jnp.pad(values, ((0, 0),) * (values.ndim - 2) + ((0, count - values.shape[-2]), (0, 0)))


def up_to(count, multiple):
    return -(-count // multiple) * multiple


def body(
    n_dp,
    n_rep,
    tokens,
    conditioning,
    ada_weight,
    ada_bias,
    qkv_weight,
    qv_bias,
    out_weight,
    out_bias,
    up_weight,
    up_bias,
    down_weight,
    down_bias,
    cotangent,
):
    latents, length, width = tokens.shape
    hidden_width = up_weight.shape[1] * n_dp
    heads = width // HEAD_DIM
    rows = latents * length
    hops = Hops(n_dp, n_rep)
    dp_bits = hops.bits("dp")
    folds = hidden_width // width

    up_rows, out_rows = up_weight.shape[1], out_weight.shape[1]
    down_shard = down_weight.T.reshape(out_rows, folds, width).transpose(1, 0, 2)
    late_shard = jnp.concatenate(
        [up_weight.T, down_shard.reshape(folds * out_rows, width), out_weight.T]
    )
    silu_low = jax.nn.silu(conditioning).astype(BF16)
    qkv_rows = qkv_weight.shape[1]
    half_rows = qkv_rows // 2
    core = hops.mine("rep", 1)
    bias_shard = jnp.concatenate([qv_bias, out_bias, up_bias, down_bias])
    bias_rows = 2
    front = jnp.concatenate(
        [
            lax.dynamic_slice_in_dim(qkv_weight.T, core * half_rows, half_rows, axis=0),
            silu_low,
            jnp.pad(bias_shard, (0, width - bias_shard.shape[0]))[None],
            jnp.pad(ada_bias, (0, width - ada_bias.shape[0]))[None],
        ]
    )
    front = pad_rows(front, up_to(front.shape[0], 8))
    front, late_shard = lax.optimization_barrier((front, late_shard))
    late = lax.all_gather(late_shard, "dp", axis=0)
    ada_shard, _ = lax.optimization_barrier((ada_weight.T, late))
    ada_all = lax.all_gather(ada_shard, "dp", axis=0, tiled=True)
    ada_pair = hops.both(ada_weight.T, hops.swap(ada_weight.T, "dp", 1), "dp", 1, 0)
    high_bits = dp_bits[:0:-1]
    for done, bit in enumerate(high_bits):
        front = hops.both(front, hops.swap(front, "dp", bit), "dp", bit, done)

    silu_part = front[..., half_rows : half_rows + latents, :].reshape(-1, width)
    mod = dot_nt(silu_part, ada_pair.reshape(-1, width))
    mod = mod.reshape((2,) * len(high_bits) + (latents, -1))
    for done, bit in enumerate(high_bits):
        kept, sent = hops.cut(mod, "dp", bit, done)
        mod = hops.both(kept, hops.swap(sent, "dp", bit), "dp", bit, done)
    mod = mod.reshape(n_dp // 2, latents, -1).transpose(1, 0, 2).reshape(latents, -1)

    front = hops.both(front, hops.swap(front, "dp", 1), "dp", 1, len(high_bits))
    front = front.reshape(n_dp, -1, width)
    mine = front[:, : half_rows + latents]
    came = hops.swap(mine, "rep", 1)
    silu_all = hops.both(mine[:, half_rows:], came[:, half_rows:], "rep", 1, 0)
    for bit in hops.bits("rep")[1:]:
        silu_all = hops.both(silu_all, hops.swap(silu_all, "rep", bit), "rep", bit, 0)
    silu_all = silu_all.reshape(n_rep // 2, 2, n_dp * latents, width).transpose(1, 0, 2, 3)
    silu_all = silu_all.reshape(-1, width)

    bias_all = front[:, half_rows + latents].astype(F32)
    cuts = [0]
    for part in (qv_bias, out_bias, up_bias, down_bias):
        cuts.append(cuts[-1] + part.shape[0])
    qv_full, out_full, up_full, down_full = (
        bias_all[:, low:high].reshape(1, -1) for low, high in zip(cuts[:-1], cuts[1:])
    )
    ada_full = front[:, half_rows + latents + 1, : ada_bias.shape[0]].astype(F32).reshape(1, -1)
    qkv_bias = jnp.concatenate(
        [qv_full[:, :width], jnp.zeros((1, width), F32), qv_full[:, width:]], axis=1
    )

    modulation = (mod + ada_full).reshape(latents, 6, width)

    core_scalar = core.astype(jnp.int32).reshape(1)
    normed, qkv, lse, attended, qkv_full = run_kernel(
        attention_forward_kernel,
        4,
        [
            shape_of((latents, length, width), BF16),
            shape_of((latents, 3 * width, length), BF16),
            shape_of((latents, 8 * ((heads + 7) // 8), length), F32),
            shape_of((latents, width, length), BF16),
        ],
        [shape_of((3 * width, width), BF16)],
        [pltpu.VMEM((3 * width, 128), F32)],
        [tokens, modulation],
        [mine, came, qkv_bias],
        pl.CostEstimate(
            flops=2 * rows * width * (3 * width + 2 * length),
            bytes_accessed=rows * width * 12,
            transcendentals=rows * heads * length,
        ),
        [core_scalar],
    )

    attended, silu_all = lax.optimization_barrier((attended, silu_all))
    (
        output,
        grad_middle,
        grad_attended,
        grad_mod_two,
        late_grad,
        out_bias_grad,
        up_bias_grad,
        down_bias_grad,
    ) = run_kernel(
        functools.partial(feed_kernel, chunk=256),
        4,
        [
            shape_of((latents, length, width), BF16),
            shape_of((latents, length, width), F32),
            shape_of((latents, width, length), BF16),
            shape_of((latents, 4, width), F32),
        ],
        [
            shape_of((2, n_dp, late.shape[1] // 2, width), BF16),
            shape_of((1, width), F32),
            shape_of((hidden_width, 128), F32),
            shape_of((1, width), F32),
        ],
        [
            pltpu.VMEM((width, width), F32),
            pltpu.VMEM((hidden_width, width + 128), F32),
            pltpu.VMEM((hidden_width, width), F32),
            pltpu.VMEM((8, width), F32),
            pltpu.VMEM((width, width), BF16),
            pltpu.VMEM((hidden_width, width), BF16),
            pltpu.VMEM((width, hidden_width), BF16),
            pltpu.VMEM((hidden_width, 128), F32),
            pltpu.VMEM((width, width), BF16),
            pltpu.VMEM((width, hidden_width), BF16),
            pltpu.VMEM((hidden_width, width), BF16),
            pltpu.VMEM((hidden_width, 4 * length), BF16),
            pltpu.VMEM((hidden_width, 4 * length), BF16),
            pltpu.VMEM((4 * length, width), F32),
            pltpu.VMEM((4 * length, width), F32),
            pltpu.VMEM((4 * length, width), F32),
        ],
        [tokens, cotangent, attended, modulation],
        [late, out_full, up_full, down_full],
        pl.CostEstimate(
            flops=6 * rows * width * (width + 2 * hidden_width),
            bytes_accessed=rows * width * 14,
            transcendentals=rows * hidden_width,
        ),
    )

    kept, sent = hops.cut(late_grad, "rep", 1, 0)
    late_half = (kept.astype(F32) + hops.swap(sent, "rep", 1).astype(F32)).astype(BF16)
    late_sum = lax.psum_scatter(late_half, "dp", scatter_dimension=0, tiled=True)
    late_sum = late_sum.reshape(-1, width)

    normed, ada_all, _ = lax.optimization_barrier((normed, ada_all, late_half))
    tail_rows = up_to(half_rows + 1, 8)
    tokens_grad, grad_mod_one, qkv_grad, qkv_bias_grad = run_kernel(
        attention_backward_kernel,
        2,
        [shape_of((latents, length, width), BF16), shape_of((latents, 2, width), F32)],
        [shape_of((n_dp, 2, tail_rows, width), BF16), shape_of((3 * width, 128), F32)],
        [
            pltpu.VMEM((3 * width, width + 128), F32),
            pltpu.VMEM((width, 3 * width), BF16),
            pltpu.VMEM((2, 3 * width, length), BF16),
        ],
        [qkv, lse, grad_attended, normed, tokens, grad_middle, modulation],
        [qkv_full],
        pl.CostEstimate(flops=1, bytes_accessed=1, transcendentals=0),
    )

    qkv_columns = qkv_bias_grad[:, 0]
    bias_blocks = jnp.concatenate(
        [
            jnp.concatenate([qkv_columns[:width], qkv_columns[2 * width :]]).reshape(n_dp, -1),
            out_bias_grad.reshape(n_dp, -1),
            up_bias_grad[:, 0].reshape(n_dp, -1),
            down_bias_grad.reshape(n_dp, -1),
        ],
        axis=1,
    )
    bias_blocks = jnp.pad(
        bias_blocks[:, None],
        ((0, 0), (half_rows, tail_rows - half_rows - 1), (0, width - cuts[-1])),
    )
    kept, sent = hops.cut(qkv_grad, "rep", 1, 1)
    total = kept.astype(F32) + hops.swap(sent, "rep", 1).astype(F32) + bias_blocks

    grad_modulation = jnp.concatenate([grad_mod_one, grad_mod_two], axis=1).reshape(
        latents, 6 * width
    )

    own = 6 * width // n_dp
    columns = grad_modulation.reshape(latents, n_dp, own).transpose(1, 0, 2).astype(BF16)
    columns = jnp.pad(columns, ((0, 0), (0, 0), (0, up_to(own, width) - own)))
    columns = columns.reshape((2,) * len(dp_bits) + (latents, width))
    total = total.reshape((2,) * len(dp_bits) + (tail_rows, width))
    axis = len(dp_bits) - 1
    for bit in dp_bits:
        kept, sent = hops.cut(total, "dp", bit, axis)
        column_kept, column_sent = hops.cut(columns, "dp", bit, axis)
        lead = sent.shape[:axis]
        sources = column_sent.shape[axis:-2]
        came = hops.swap(
            jnp.concatenate(
                [sent.astype(BF16), column_sent.reshape(lead + (-1, width))], axis=-2
            ),
            "dp",
            bit,
        )
        total = kept.astype(F32) + came[..., :tail_rows, :].astype(F32)
        column_came = came[..., tail_rows:, :].reshape(lead + sources + (latents, width))
        columns = hops.both(column_kept, column_came, "dp", bit, axis)
        axis -= 1
    columns = columns.reshape(n_dp * latents, width)

    qkv_total = total.astype(BF16)
    end = tail_rows + late_sum.shape[0]
    for bit in hops.bits("rep")[1:]:
        sums = jnp.concatenate([qkv_total, late_sum])
        came = hops.swap(jnp.concatenate([sums, columns]), "rep", bit)
        sums = (sums.astype(F32) + came[:end].astype(F32)).astype(BF16)
        qkv_total, late_sum = sums[:tail_rows], sums[tail_rows:]
        columns = hops.both(columns, came[end:], "rep", bit, 0).reshape(-1, width)
    mine = jnp.concatenate([qkv_total, late_sum, columns])
    came = hops.swap(mine, "rep", 1)
    smem = pl.BlockSpec(memory_space=pltpu.SMEM)
    vmem = pl.BlockSpec(memory_space=pltpu.VMEM)
    ada_grad, ada_bias_grad, qkv_owned, up_owned, down_owned, out_owned, *bias_sums = pl.pallas_call(
        functools.partial(finish_kernel, tail_rows=tail_rows),
        in_specs=[smem, vmem, vmem, vmem],
        out_specs=[vmem] * 10,
        out_shape=[
            shape_of((own, width), F32),
            shape_of((1, own), F32),
            shape_of((qkv_rows, width), F32),
            shape_of((up_rows, width), F32),
            shape_of((out_rows, hidden_width), F32),
            shape_of((out_rows, width), F32),
        ]
        + [shape_of((1, part.shape[0]), F32) for part in (qv_bias, out_bias, up_bias, down_bias)],
        compiler_params=pltpu.CompilerParams(vmem_limit_bytes=VMEM_LIMIT),
    )(core_scalar, mine, came, silu_all)
    ada_bias_grad = ada_bias_grad.reshape(-1)

    grad_silu = lax.dot_general(
        grad_modulation,
        ada_all.astype(F32),
        (((1,), (0,)), ((), ())),
        precision=lax.Precision.HIGHEST,
    )
    _, silu_pull = jax.vjp(jax.nn.silu, conditioning)
    condition_grad = silu_pull(grad_silu)[0]

    qv_sum, out_bias_sum, up_bias_sum, down_bias_sum = (part.reshape(-1) for part in bias_sums)
    return (
        output,
        tokens_grad,
        condition_grad,
        ada_grad.T,
        ada_bias_grad,
        qkv_owned.T,
        qv_sum,
        out_owned.T,
        out_bias_sum,
        up_owned.T,
        up_bias_sum,
        down_owned.T,
        down_bias_sum,
    )


def solution(mesh):
    return jax.shard_map(
        functools.partial(body, mesh.shape["dp"], mesh.shape["rep"]),
        mesh=mesh,
        in_specs=(
            P(("dp", "rep"), None, None),
            P(("dp", "rep"), None),
            P(None, "dp"),
            P("dp"),
            P(None, "dp"),
            P("dp"),
            P(None, "dp"),
            P("dp"),
            P(None, "dp"),
            P("dp"),
            P(None, "dp"),
            P("dp"),
            P(("dp", "rep"), None, None),
        ),
        out_specs=(
            P(("dp", "rep"), None, None),
            P(("dp", "rep"), None, None),
            P(("dp", "rep"), None),
            P(None, "dp"),
            P("dp"),
            P(None, "dp"),
            P("dp"),
            P(None, "dp"),
            P("dp"),
            P(None, "dp"),
            P("dp"),
            P(None, "dp"),
            P("dp"),
        ),
        check_vma=False,
    )
```

```python
import functools

import jax
import jax.numpy as jnp
from jax import lax
from jax.experimental import pallas as pl
from jax.experimental.pallas import tpu as pltpu
from jax.sharding import PartitionSpec as P

HEAD_DIM = 64
EPS = 1e-06
GELU_C = 0.7978845608028654
VMEM_LIMIT = 56 * 1024 * 1024
F32 = jnp.float32
BF16 = jnp.bfloat16


def dot_nn(left, right):
    return lax.dot_general(left, right, (((1,), (0,)), ((), ())), preferred_element_type=F32)


def dot_nt(left, right):
    return lax.dot_general(left, right, (((1,), (1,)), ((), ())), preferred_element_type=F32)


def dot_tn(left, right):
    return lax.dot_general(left, right, (((0,), (0,)), ((), ())), preferred_element_type=F32)


def normalise(values):
    average = jnp.mean(values, axis=-1, keepdims=True)
    centred = values - average
    spread = jnp.mean(centred * centred, axis=-1, keepdims=True)
    inverse = lax.rsqrt(spread + EPS)
    return centred * inverse, inverse


def normalise_back(upstream, normal, inverse):
    first = jnp.mean(upstream, axis=-1, keepdims=True)
    second = jnp.mean(upstream * normal, axis=-1, keepdims=True)
    return inverse * (upstream - first - normal * second)


STRIP = 64
GROUP = 3


def beside(*parts):
    return jnp.concatenate(parts, axis=1)


def above(*parts):
    return jnp.concatenate(parts, axis=0)


def strips(extent, size):
    return [slice(low, low + size) for low in range(0, extent, size)]


def head_slices(head):
    low = head * HEAD_DIM
    pair = low - low % (2 * HEAD_DIM)
    return slice(low, low + HEAD_DIM), slice(pair, pair + 2 * HEAD_DIM), low == pair


def in_groups(items, size):
    return [items[low : low + size] for low in range(0, len(items), size)]


def attention_forward_kernel(
    core_ref,
    tokens_ref,
    mod_ref,
    mine_ref,
    came_ref,
    bias_row_ref,
    normed_ref,
    qkv_ref,
    lse_ref,
    attended_ref,
    weight_ref,
    bias_ref,
):
    latents, length, width = tokens_ref.shape
    blank = jnp.zeros((HEAD_DIM, length), BF16)

    @pl.when(pl.program_id(0) == 0)
    def _():
        first = core_ref[0] == 0
        n_dp = mine_ref.shape[0]
        half_rows = weight_ref.shape[0] // (2 * n_dp)
        for owner in range(n_dp):
            mine = mine_ref[owner, :half_rows, :]
            came = came_ref[owner, :half_rows, :]
            low = 2 * owner * half_rows
            weight_ref[low : low + half_rows, :] = jnp.where(first, mine, came)
            weight_ref[low + half_rows : low + 2 * half_rows, :] = jnp.where(first, came, mine)
        bias_ref[...] = jnp.broadcast_to(bias_row_ref[...], (128, 3 * width)).T

    for latent in range(latents):
        for rows in strips(length, STRIP):
            normal, _ = normalise(tokens_ref[latent, rows, :].astype(F32))
            normed = normal * (1.0 + mod_ref[latent, 1:2, :]) + mod_ref[latent, 0:1, :]
            normed_ref[latent, rows, :] = normed.astype(BF16)
    normed = normed_ref[...].reshape(latents * length, width)
    for part in strips(3 * width, 2 * HEAD_DIM):
        bias = bias_ref[part, :]
        qkv = dot_nt(weight_ref[part, :], normed) + beside(*([bias] * (latents * length // 128)))
        qkv = qkv.astype(BF16)
        for latent in range(latents):
            qkv_ref[latent, part, :] = qkv[:, latent * length : (latent + 1) * length]
    keys_all = [qkv_ref[latent, width : 2 * width, :].T for latent in range(latents)]

    def scores_of(latent, head):
        own, pair, first = head_slices(head)
        queries = qkv_ref[latent, own, :]
        queries = above(queries, blank) if first else above(blank, queries)
        return dot_nn(keys_all[latent][:, pair], queries)

    def probs_of(latent, head, scores):
        parts = []
        for columns in strips(length, 128):
            strip = scores[:, columns] * HEAD_DIM ** (-0.5)
            highest = jnp.max(strip, axis=0, keepdims=True)
            shifted = jnp.exp(strip - highest)
            total = jnp.sum(shifted, axis=0, keepdims=True)
            parts.append((shifted * (1.0 / total)).astype(BF16))
            lse_ref[latent, head : head + 1, columns] = highest + jnp.log(total)
        return beside(*parts)

    def attend(latent, head, probs):
        own, _, _ = head_slices(head)
        values_in = qkv_ref[latent, 2 * width + own.start : 2 * width + own.stop, :]
        attended_ref[latent, own, :] = dot_nn(values_in, probs).astype(BF16)

    items = [(latent, head) for latent in range(latents) for head in range(width // HEAD_DIM)]
    groups = in_groups(items, GROUP)
    scores = [scores_of(*item) for item in groups[0]]
    previous = []
    for place, group in enumerate(groups):
        later = groups[place + 1] if place + 1 < len(groups) else []
        next_scores = [scores_of(*item) for item in later]
        probs = [probs_of(*item, value) for item, value in zip(group, scores)]
        for item, value in previous:
            attend(*item, value)
        previous = list(zip(group, probs))
        scores = next_scores
    for item, value in previous:
        attend(*item, value)


def by_side(core_ref, side, kept_ref, sent_ref, write):
    @pl.when(core_ref[0] == side)
    def _():
        write(kept_ref)

    @pl.when(core_ref[0] != side)
    def _():
        write(sent_ref)


def feed_kernel(
    core_ref,
    tokens_ref,
    cotangent_ref,
    attended_ref,
    mod_ref,
    late_ref,
    out_bias_ref,
    up_bias_row_ref,
    down_bias_ref,
    output_ref,
    grad_middle_ref,
    grad_attended_ref,
    grad_mod_ref,
    late_kept_ref,
    late_sent_ref,
    out_bias_grad_ref,
    up_bias_grad_ref,
    down_bias_grad_ref,
    out_acc,
    up_acc,
    down_acc,
    bias_acc,
    out_weight_ref,
    up_weight_ref,
    down_weight_ref,
    up_bias_ref,
    out_back,
    up_back,
    down_back,
    active_all,
    grad_hidden_all,
    middle_all,
    normal_all,
    branch_all,
    *,
    chunk,
):
    step = pl.program_id(0)
    n_dp = late_ref.shape[0]
    latents, length, width = tokens_ref.shape
    hidden_width = up_weight_ref.shape[0]
    tokens_all = latents * length
    up_rows, out_rows = hidden_width // n_dp, width // n_dp
    out_low = up_rows + out_rows * (hidden_width // width)

    @pl.when(step == 0)
    def _():
        out_acc[...] = jnp.zeros_like(out_acc)
        up_acc[...] = jnp.zeros_like(up_acc)
        down_acc[...] = jnp.zeros_like(down_acc)
        bias_acc[...] = jnp.zeros_like(bias_acc)
        for owner in range(n_dp):
            up_weight_ref[owner * up_rows : (owner + 1) * up_rows, :] = late_ref[owner, :up_rows, :]
            outs = slice(owner * out_rows, (owner + 1) * out_rows)
            for fold in range(hidden_width // width):
                low = up_rows + fold * out_rows
                down_weight_ref[outs, fold * width : (fold + 1) * width] = late_ref[
                    owner, low : low + out_rows, :
                ]
            out_weight_ref[outs, :] = late_ref[owner, out_low:, :]
        out_back[...] = out_weight_ref[...].T
        up_back[...] = up_weight_ref[...].T
        down_back[...] = down_weight_ref[...].T
        up_bias_ref[...] = jnp.broadcast_to(up_bias_row_ref[...], (128, hidden_width)).T

    attended = beside(*[attended_ref[latent] for latent in range(latents)])
    branch_wide = dot_nn(out_weight_ref[...], attended)
    normed_parts = []
    grad_feed_parts = []
    inverses = []
    down_sum = jnp.zeros((1, width), F32)
    for latent in range(latents):
        gate_one = mod_ref[latent, 2:3, :]
        shift_two = mod_ref[latent, 3:4, :]
        scale_two = 1.0 + mod_ref[latent, 4:5, :]
        gate_two = mod_ref[latent, 5:6, :]
        branch_tall = branch_wide[:, latent * length : (latent + 1) * length].T
        for rows in strips(length, STRIP):
            there = slice(latent * length + rows.start, latent * length + rows.stop)
            branch = branch_tall[rows] + out_bias_ref[...]
            branch_all[there, :] = branch
            middle = tokens_ref[latent, rows, :].astype(F32) + gate_one * branch
            middle_all[there, :] = middle
            normal, inverse = normalise(middle)
            normal_all[there, :] = normal
            inverses.append(inverse)
            normed_parts.append((normal * scale_two + shift_two).astype(BF16))
            grad_feed = (cotangent_ref[latent, rows, :].astype(F32) * gate_two).astype(BF16)
            grad_feed_parts.append(grad_feed)
            down_sum += jnp.sum(grad_feed.astype(F32), axis=0, keepdims=True)
    bias_acc[0:1, :] += down_sum
    normed_all = above(*normed_parts)
    grad_feed_all = above(*grad_feed_parts)

    def products(rows):
        return (
            dot_nt(up_weight_ref[rows, :], normed_all),
            dot_nt(down_back[rows, :], grad_feed_all),
        )

    parts = strips(hidden_width, chunk)
    ahead = products(parts[0])
    for place, part in enumerate(parts):
        hidden_wide, grad_wide = ahead
        if place + 1 < len(parts):
            ahead = products(parts[place + 1])
        for rows in strips(chunk, STRIP):
            there = slice(part.start + rows.start, part.start + rows.stop)
            bias = up_bias_ref[there, :]
            bias = beside(bias, bias)
            for columns in strips(tokens_all, 256):
                hidden = hidden_wide[rows, columns] + bias
                square = hidden * hidden
                bent = jnp.tanh(hidden * (GELU_C + (GELU_C * 0.044715) * square))
                half = 0.5 + 0.5 * bent
                active_all[there, columns] = (hidden * half).astype(BF16)
                slope = half + hidden * (0.5 - 0.5 * (bent * bent)) * (
                    GELU_C + (3.0 * GELU_C * 0.044715) * square
                )
                grad_hidden_all[there, columns] = (grad_wide[rows, columns] * slope).astype(BF16)

    feed_wide = dot_nn(down_weight_ref[...], active_all[...])
    grad_normed_wide = dot_nn(up_back[...], grad_hidden_all[...])
    ones = jnp.ones((tokens_all, 128), BF16)
    up_acc[...] += dot_nn(grad_hidden_all[...], beside(normed_all, ones))
    down_acc[...] += dot_nn(active_all[...], grad_feed_all)

    grad_branch_parts = []
    out_sum = jnp.zeros((1, width), F32)
    for latent in range(latents):
        gate_one = mod_ref[latent, 2:3, :]
        scale_two = 1.0 + mod_ref[latent, 4:5, :]
        gate_two = mod_ref[latent, 5:6, :]
        here = slice(latent * length, (latent + 1) * length)
        feed_tall = feed_wide[:, here].T
        grad_normed_tall = grad_normed_wide[:, here].T
        sums = [jnp.zeros((1, width), F32) for _ in range(4)]
        for rows in strips(length, STRIP):
            there = slice(here.start + rows.start, here.start + rows.stop)
            feed = feed_tall[rows] + down_bias_ref[...]
            grad_normed = grad_normed_tall[rows]
            incoming = cotangent_ref[latent, rows, :].astype(F32)
            normal = normal_all[there, :]
            output_ref[latent, rows, :] = (middle_all[there, :] + gate_two * feed).astype(BF16)
            grad_middle = incoming + normalise_back(
                grad_normed * scale_two, normal, inverses[there.start // STRIP]
            )
            grad_middle_ref[latent, rows, :] = grad_middle
            grad_branch = (grad_middle * gate_one).astype(BF16)
            grad_branch_parts.append(grad_branch)
            terms = (
                grad_middle * branch_all[there, :],
                grad_normed,
                grad_normed * normal,
                incoming * feed,
            )
            for place, term in enumerate(terms):
                sums[place] += jnp.sum(term, axis=0, keepdims=True)
            out_sum += jnp.sum(grad_branch.astype(F32), axis=0, keepdims=True)
        grad_mod_ref[latent] = above(*sums)
    bias_acc[1:2, :] += out_sum
    grad_branch_all = above(*grad_branch_parts)
    grad_attended = dot_nt(out_back[...], grad_branch_all).astype(BF16)
    for latent in range(latents):
        grad_attended_ref[latent] = grad_attended[:, latent * length : (latent + 1) * length]
    out_acc[...] += dot_nn(attended, grad_branch_all)

    @pl.when(step == pl.num_programs(0) - 1)
    def _():
        out_acc[...] = out_acc[...].T
        up_back[...] = down_acc[...].T.astype(BF16)
        folds = hidden_width // width // 2
        out_back_rows = out_rows // 2
        for side in range(2):

            def write(ref, side=side):
                for owner in range(n_dp):
                    ups = owner * up_rows + side * (up_rows // 2)
                    ref[owner, : up_rows // 2, :] = up_acc[
                        ups : ups + up_rows // 2, :width
                    ].astype(BF16)
                    outs = slice(owner * out_rows, (owner + 1) * out_rows)
                    for place in range(folds):
                        low = up_rows // 2 + place * out_rows
                        fold = side * folds + place
                        ref[owner, low : low + out_rows, :] = up_back[
                            outs, fold * width : (fold + 1) * width
                        ]
                    outs = owner * out_rows + side * out_back_rows
                    ref[owner, out_low // 2 :, :] = out_acc[
                        outs : outs + out_back_rows
                    ].astype(BF16)

            by_side(core_ref, side, late_kept_ref, late_sent_ref, write)
        up_bias_grad_ref[...] = up_acc[:, width:]
        down_bias_grad_ref[...] = bias_acc[0:1, :]
        out_bias_grad_ref[...] = bias_acc[1:2, :]


def attention_backward_kernel(
    core_ref,
    qkv_ref,
    lse_ref,
    grad_attended_ref,
    normed_ref,
    tokens_ref,
    grad_middle_ref,
    mod_ref,
    weight_ref,
    tokens_grad_ref,
    grad_mod_ref,
    kept_ref,
    sent_ref,
    bias_grad_ref,
    acc,
    weight_back,
    grad_qkv_ref,
):
    step = pl.program_id(0)
    latents, length, width = normed_ref.shape
    blank = jnp.zeros((HEAD_DIM, length), BF16)

    @pl.when(step == 0)
    def _():
        acc[...] = jnp.zeros_like(acc)
        weight_back[...] = weight_ref[...].T

    keys_all = [qkv_ref[latent, width : 2 * width, :].T for latent in range(latents)]
    values_all = [qkv_ref[latent, 2 * width : 3 * width, :].T for latent in range(latents)]

    def products(latent, head):
        own, pair, first = head_slices(head)
        queries = qkv_ref[latent, own, :]
        grad_out = grad_attended_ref[latent, own, :]
        queries = above(queries, blank) if first else above(blank, queries)
        grad_out = above(grad_out, blank) if first else above(blank, grad_out)
        return (
            dot_nn(keys_all[latent][:, pair], queries),
            dot_nn(values_all[latent][:, pair], grad_out),
        )

    def middle_of(latent, head, scores, grad_probs):
        low_parts = []
        grad_parts = []
        for columns in strips(length, 128):
            total = lse_ref[latent, head : head + 1, columns]
            probs = jnp.exp(scores[:, columns] * HEAD_DIM ** (-0.5) - total)
            terms = probs * grad_probs[:, columns]
            row_terms = jnp.sum(terms, axis=0, keepdims=True)
            grad_parts.append((probs * (grad_probs[:, columns] - row_terms)).astype(BF16))
            low_parts.append(probs.astype(BF16))
        return beside(*low_parts), beside(*grad_parts)

    def finish(latent, head, probs, grad_scores):
        own, _, _ = head_slices(head)
        low, high = own.start, own.stop
        queries = qkv_ref[latent, own, :]
        keys_in = qkv_ref[latent, width + low : width + high, :]
        grad_out = grad_attended_ref[latent, own, :]
        scale = HEAD_DIM ** (-0.5)
        grad_qkv_ref[latent, own, :] = (dot_nn(keys_in, grad_scores) * scale).astype(BF16)
        grad_qkv_ref[latent, width + low : width + high, :] = (
            dot_nt(queries, grad_scores) * scale
        ).astype(BF16)
        grad_qkv_ref[latent, 2 * width + low : 2 * width + high, :] = dot_nt(
            grad_out, probs
        ).astype(BF16)

    items = [(latent, head) for latent in range(latents) for head in range(width // HEAD_DIM)]
    groups = in_groups(items, GROUP)
    values = [products(*item) for item in groups[0]]
    previous = []
    for place, group in enumerate(groups):
        later = groups[place + 1] if place + 1 < len(groups) else []
        next_values = [products(*item) for item in later]
        middles = [middle_of(*item, *value) for item, value in zip(group, values)]
        for item, value in previous:
            finish(*item, *value)
        previous = list(zip(group, middles))
        values = next_values
    for item, value in previous:
        finish(*item, *value)

    grad_qkv = beside(*[grad_qkv_ref[latent] for latent in range(latents)])
    normed = normed_ref[...].reshape(latents * length, width)
    grad_normed_wide = dot_nn(weight_back[...], grad_qkv)
    acc[...] += dot_nn(grad_qkv, beside(normed, jnp.ones((latents * length, 128), BF16)))
    for latent in range(latents):
        grad_normed_tall = grad_normed_wide[:, latent * length : (latent + 1) * length].T
        scale_one = 1.0 + mod_ref[latent, 1:2, :]
        first = jnp.zeros((1, width), F32)
        second = jnp.zeros((1, width), F32)
        for rows in strips(length, STRIP):
            normal, inverse = normalise(tokens_ref[latent, rows, :].astype(F32))
            grad_normed = grad_normed_tall[rows]
            first += jnp.sum(grad_normed, axis=0, keepdims=True)
            second += jnp.sum(grad_normed * normal, axis=0, keepdims=True)
            back = normalise_back(grad_normed * scale_one, normal, inverse)
            tokens_grad_ref[latent, rows, :] = (grad_middle_ref[latent, rows, :] + back).astype(
                BF16
            )
        grad_mod_ref[latent] = above(first, second)

    @pl.when(step == pl.num_programs(0) - 1)
    def _():
        n_dp, tail_rows, _ = kept_ref.shape
        half_rows = 3 * width // (2 * n_dp)
        for side in range(2):

            def write(ref, side=side):
                for owner in range(n_dp):
                    low = (2 * owner + side) * half_rows
                    rows = acc[low : low + half_rows, :width]
                    rest = jnp.zeros((tail_rows - half_rows, width), F32)
                    ref[owner] = above(rows, rest).astype(BF16)

            by_side(core_ref, side, kept_ref, sent_ref, write)
        bias_grad_ref[...] = acc[:, width:]


def finish_kernel(
    core_ref,
    mine_ref,
    came_ref,
    silu_ref,
    ada_ref,
    ada_bias_ref,
    qkv_ref,
    up_ref,
    down_ref,
    out_ref,
    qv_bias_ref,
    out_bias_ref,
    up_bias_ref,
    down_bias_ref,
    *,
    tail_rows,
):
    first = core_ref[0] == 0
    own = ada_ref.shape[0]
    half_rows = qkv_ref.shape[0] // 2
    up_half, out_rows = up_ref.shape[0] // 2, out_ref.shape[0]
    width = out_ref.shape[1]
    folds = down_ref.shape[1] // width // 2
    out_low = tail_rows + up_half + folds * out_rows
    end = out_low + out_rows // 2
    mine = mine_ref[:end, :].astype(F32)
    came = came_ref[:end, :].astype(F32)
    for side in range(2):
        part = jnp.where(first, mine, came) if side == 0 else jnp.where(first, came, mine)
        qkv_ref[side * half_rows : (side + 1) * half_rows, :] = part[:half_rows]
        up_ref[side * up_half : (side + 1) * up_half, :] = part[tail_rows : tail_rows + up_half]
        for place in range(folds):
            low = tail_rows + up_half + place * out_rows
            columns = (side * folds + place) * width
            down_ref[:, columns : columns + width] = part[low : low + out_rows]
        out_ref[side * (out_rows // 2) : (side + 1) * (out_rows // 2), :] = part[out_low:]
    biases = mine[half_rows : half_rows + 1] + came[half_rows : half_rows + 1]
    low = 0
    for ref in (qv_bias_ref, out_bias_ref, up_bias_ref, down_bias_ref):
        ref[...] = biases[:, low : low + ref.shape[1]]
        low += ref.shape[1]
    mine = mine_ref[end:, :]
    came = came_ref[end:, :]
    columns = above(jnp.where(first, mine, came), jnp.where(first, came, mine))
    ada_ref[...] = dot_tn(columns, silu_ref[...])[:own]
    ada_bias_ref[...] = jnp.sum(columns.astype(F32), axis=0, keepdims=True)[:, :own]


def each(shape, count):
    zeros = (0,) * (len(shape) - 1)
    return pl.BlockSpec((count,) + tuple(shape[1:]), lambda step: (step,) + zeros)


def whole(shape):
    zeros = (0,) * len(shape)
    return pl.BlockSpec(tuple(shape), lambda step: zeros)


def run_kernel(kernel, count, streamed_out, fixed_out, scratch, streamed, fixed, cost, scalars=()):
    return pl.pallas_call(
        kernel,
        grid=(streamed[0].shape[0] // count,),
        in_specs=[pl.BlockSpec(memory_space=pltpu.SMEM)] * len(scalars)
        + [each(item.shape, count) for item in streamed]
        + [whole(item.shape) for item in fixed],
        out_specs=[each(item.shape, count) for item in streamed_out]
        + [whole(item.shape) for item in fixed_out],
        out_shape=list(streamed_out) + list(fixed_out),
        scratch_shapes=scratch,
        compiler_params=pltpu.CompilerParams(
            dimension_semantics=("arbitrary",), vmem_limit_bytes=VMEM_LIMIT
        ),
        cost_estimate=cost,
    )(*scalars, *streamed, *fixed)


def shape_of(dims, kind):
    return jax.ShapeDtypeStruct(tuple(dims), kind)


AXES = ("dp", "rep")


class Hops:
    def __init__(self, n_dp, n_rep):
        self.sizes = {"dp": n_dp, "rep": n_rep}
        self.place = {name: lax.axis_index(name) for name in AXES}

    def bits(self, name):
        return [1 << shift for shift in range(self.sizes[name].bit_length() - 1)]

    def mine(self, name, bit):
        return (self.place[name] // bit) % 2

    def swap(self, value, name, bit):
        n_dp, n_rep = self.sizes["dp"], self.sizes["rep"]
        flip_dp, flip_rep = (bit, 0) if name == "dp" else (0, bit)
        pairs = [
            (d * n_rep + r, (d ^ flip_dp) * n_rep + (r ^ flip_rep))
            for d in range(n_dp)
            for r in range(n_rep)
        ]
        return lax.ppermute(value, AXES, pairs)

    def both(self, kept, came, name, bit, axis):
        upper = self.mine(name, bit) == 1
        return jnp.stack(
            [jnp.where(upper, came, kept), jnp.where(upper, kept, came)], axis=axis
        )

    def cut(self, value, name, bit, axis):
        here = self.mine(name, bit)
        return (
            lax.dynamic_index_in_dim(value, here, axis, keepdims=False),
            lax.dynamic_index_in_dim(value, 1 - here, axis, keepdims=False),
        )


def pad_rows(values, count):
    return jnp.pad(values, ((0, 0),) * (values.ndim - 2) + ((0, count - values.shape[-2]), (0, 0)))


def up_to(count, multiple):
    return -(-count // multiple) * multiple


def body(
    n_dp,
    n_rep,
    tokens,
    conditioning,
    ada_weight,
    ada_bias,
    qkv_weight,
    qv_bias,
    out_weight,
    out_bias,
    up_weight,
    up_bias,
    down_weight,
    down_bias,
    cotangent,
):
    latents, length, width = tokens.shape
    hidden_width = up_weight.shape[1] * n_dp
    heads = width // HEAD_DIM
    rows = latents * length
    hops = Hops(n_dp, n_rep)
    dp_bits = hops.bits("dp")
    folds = hidden_width // width

    up_rows, out_rows = up_weight.shape[1], out_weight.shape[1]
    down_shard = down_weight.T.reshape(out_rows, folds, width).transpose(1, 0, 2)
    late_shard = jnp.concatenate(
        [up_weight.T, down_shard.reshape(folds * out_rows, width), out_weight.T]
    )
    silu_low = jax.nn.silu(conditioning).astype(BF16)
    qkv_rows = qkv_weight.shape[1]
    half_rows = qkv_rows // 2
    core = hops.mine("rep", 1)
    bias_shard = jnp.concatenate([qv_bias, out_bias, up_bias, down_bias])
    bias_rows = 2
    front = jnp.concatenate(
        [
            lax.dynamic_slice_in_dim(qkv_weight.T, core * half_rows, half_rows, axis=0),
            silu_low,
            jnp.pad(bias_shard, (0, width - bias_shard.shape[0]))[None],
            jnp.pad(ada_bias, (0, width - ada_bias.shape[0]))[None],
        ]
    )
    front = pad_rows(front, up_to(front.shape[0], 8))
    front, late_shard = lax.optimization_barrier((front, late_shard))
    late = lax.all_gather(late_shard, "dp", axis=0)
    ada_shard, _ = lax.optimization_barrier((ada_weight.T, late))
    ada_all = lax.all_gather(ada_shard, "dp", axis=0, tiled=True)
    ada_pair = hops.both(ada_weight.T, hops.swap(ada_weight.T, "dp", 1), "dp", 1, 0)
    high_bits = dp_bits[:0:-1]
    for done, bit in enumerate(high_bits):
        front = hops.both(front, hops.swap(front, "dp", bit), "dp", bit, done)

    silu_part = front[..., half_rows : half_rows + latents, :].reshape(-1, width)
    mod = dot_nt(silu_part, ada_pair.reshape(-1, width))
    mod = mod.reshape((2,) * len(high_bits) + (latents, -1))
    for done, bit in enumerate(high_bits):
        kept, sent = hops.cut(mod, "dp", bit, done)
        mod = hops.both(kept, hops.swap(sent, "dp", bit), "dp", bit, done)
    mod = mod.reshape(n_dp // 2, latents, -1).transpose(1, 0, 2).reshape(latents, -1)

    front = hops.both(front, hops.swap(front, "dp", 1), "dp", 1, len(high_bits))
    front = front.reshape(n_dp, -1, width)
    mine = front[:, : half_rows + latents]
    came = hops.swap(mine, "rep", 1)
    silu_all = hops.both(mine[:, half_rows:], came[:, half_rows:], "rep", 1, 0)
    for bit in hops.bits("rep")[1:]:
        silu_all = hops.both(silu_all, hops.swap(silu_all, "rep", bit), "rep", bit, 0)
    silu_all = silu_all.reshape(n_rep // 2, 2, n_dp * latents, width).transpose(1, 0, 2, 3)
    silu_all = silu_all.reshape(-1, width)

    bias_all = front[:, half_rows + latents].astype(F32)
    cuts = [0]
    for part in (qv_bias, out_bias, up_bias, down_bias):
        cuts.append(cuts[-1] + part.shape[0])
    qv_full, out_full, up_full, down_full = (
        bias_all[:, low:high].reshape(1, -1) for low, high in zip(cuts[:-1], cuts[1:])
    )
    ada_full = front[:, half_rows + latents + 1, : ada_bias.shape[0]].astype(F32).reshape(1, -1)
    qkv_bias = jnp.concatenate(
        [qv_full[:, :width], jnp.zeros((1, width), F32), qv_full[:, width:]], axis=1
    )

    modulation = (mod + ada_full).reshape(latents, 6, width)

    core_scalar = core.astype(jnp.int32).reshape(1)
    normed, qkv, lse, attended, qkv_full = run_kernel(
        attention_forward_kernel,
        4,
        [
            shape_of((latents, length, width), BF16),
            shape_of((latents, 3 * width, length), BF16),
            shape_of((latents, 8 * ((heads + 7) // 8), length), F32),
            shape_of((latents, width, length), BF16),
        ],
        [shape_of((3 * width, width), BF16)],
        [pltpu.VMEM((3 * width, 128), F32)],
        [tokens, modulation],
        [mine, came, qkv_bias],
        pl.CostEstimate(
            flops=2 * rows * width * (3 * width + 2 * length),
            bytes_accessed=rows * width * 12,
            transcendentals=rows * heads * length,
        ),
        [core_scalar],
    )

    attended, silu_all = lax.optimization_barrier((attended, silu_all))
    (
        output,
        grad_middle,
        grad_attended,
        grad_mod_two,
        late_kept,
        late_sent,
        out_bias_grad,
        up_bias_grad,
        down_bias_grad,
    ) = run_kernel(
        functools.partial(feed_kernel, chunk=256),
        4,
        [
            shape_of((latents, length, width), BF16),
            shape_of((latents, length, width), F32),
            shape_of((latents, width, length), BF16),
            shape_of((latents, 4, width), F32),
        ],
        [
            shape_of((n_dp, late.shape[1] // 2, width), BF16),
            shape_of((n_dp, late.shape[1] // 2, width), BF16),
            shape_of((1, width), F32),
            shape_of((hidden_width, 128), F32),
            shape_of((1, width), F32),
        ],
        [
            pltpu.VMEM((width, width), F32),
            pltpu.VMEM((hidden_width, width + 128), F32),
            pltpu.VMEM((hidden_width, width), F32),
            pltpu.VMEM((8, width), F32),
            pltpu.VMEM((width, width), BF16),
            pltpu.VMEM((hidden_width, width), BF16),
            pltpu.VMEM((width, hidden_width), BF16),
            pltpu.VMEM((hidden_width, 128), F32),
            pltpu.VMEM((width, width), BF16),
            pltpu.VMEM((width, hidden_width), BF16),
            pltpu.VMEM((hidden_width, width), BF16),
            pltpu.VMEM((hidden_width, 4 * length), BF16),
            pltpu.VMEM((hidden_width, 4 * length), BF16),
            pltpu.VMEM((4 * length, width), F32),
            pltpu.VMEM((4 * length, width), F32),
            pltpu.VMEM((4 * length, width), F32),
        ],
        [tokens, cotangent, attended, modulation],
        [late, out_full, up_full, down_full],
        pl.CostEstimate(
            flops=6 * rows * width * (width + 2 * hidden_width),
            bytes_accessed=rows * width * 14,
            transcendentals=rows * hidden_width,
        ),
        [core_scalar],
    )

    late_half = late_kept.astype(F32) + hops.swap(late_sent, "rep", 1).astype(F32)
    late_half = late_half.astype(BF16)
    late_parts = lax.all_to_all(late_half, "dp", 0, 0, tiled=True)

    normed, ada_all, _ = lax.optimization_barrier((normed, ada_all, late_half))
    tail_rows = up_to(half_rows + 1, 8)
    tokens_grad, grad_mod_one, qkv_kept, qkv_sent, qkv_bias_grad = run_kernel(
        attention_backward_kernel,
        2,
        [shape_of((latents, length, width), BF16), shape_of((latents, 2, width), F32)],
        [
            shape_of((n_dp, tail_rows, width), BF16),
            shape_of((n_dp, tail_rows, width), BF16),
            shape_of((3 * width, 128), F32),
        ],
        [
            pltpu.VMEM((3 * width, width + 128), F32),
            pltpu.VMEM((width, 3 * width), BF16),
            pltpu.VMEM((2, 3 * width, length), BF16),
        ],
        [qkv, lse, grad_attended, normed, tokens, grad_middle, modulation],
        [qkv_full],
        pl.CostEstimate(flops=1, bytes_accessed=1, transcendentals=0),
        [core_scalar],
    )
    qkv_sent, late_parts = lax.optimization_barrier((qkv_sent, late_parts))
    late_sum = jnp.sum(late_parts.astype(F32), axis=0).astype(BF16)

    qkv_columns = qkv_bias_grad[:, 0]
    bias_blocks = jnp.concatenate(
        [
            jnp.concatenate([qkv_columns[:width], qkv_columns[2 * width :]]).reshape(n_dp, -1),
            out_bias_grad.reshape(n_dp, -1),
            up_bias_grad[:, 0].reshape(n_dp, -1),
            down_bias_grad.reshape(n_dp, -1),
        ],
        axis=1,
    )
    bias_blocks = jnp.pad(
        bias_blocks[:, None],
        ((0, 0), (half_rows, tail_rows - half_rows - 1), (0, width - cuts[-1])),
    )
    total = qkv_kept.astype(F32) + hops.swap(qkv_sent, "rep", 1).astype(F32) + bias_blocks

    grad_modulation = jnp.concatenate([grad_mod_one, grad_mod_two], axis=1).reshape(
        latents, 6 * width
    )

    own = 6 * width // n_dp
    columns = grad_modulation.reshape(latents, n_dp, own).transpose(1, 0, 2).astype(BF16)
    columns = jnp.pad(columns, ((0, 0), (0, 0), (0, up_to(own, width) - own)))
    columns = columns.reshape((2,) * len(dp_bits) + (latents, width))
    total = total.reshape((2,) * len(dp_bits) + (tail_rows, width))
    axis = len(dp_bits) - 1
    for bit in dp_bits:
        kept, sent = hops.cut(total, "dp", bit, axis)
        column_kept, column_sent = hops.cut(columns, "dp", bit, axis)
        lead = sent.shape[:axis]
        sources = column_sent.shape[axis:-2]
        came = hops.swap(
            jnp.concatenate(
                [sent.astype(BF16), column_sent.reshape(lead + (-1, width))], axis=-2
            ),
            "dp",
            bit,
        )
        total = kept.astype(F32) + came[..., :tail_rows, :].astype(F32)
        column_came = came[..., tail_rows:, :].reshape(lead + sources + (latents, width))
        columns = hops.both(column_kept, column_came, "dp", bit, axis)
        axis -= 1
    columns = columns.reshape(n_dp * latents, width)

    qkv_total = total.astype(BF16)
    end = tail_rows + late_sum.shape[0]
    for bit in hops.bits("rep")[1:]:
        sums = jnp.concatenate([qkv_total, late_sum])
        came = hops.swap(jnp.concatenate([sums, columns]), "rep", bit)
        sums = (sums.astype(F32) + came[:end].astype(F32)).astype(BF16)
        qkv_total, late_sum = sums[:tail_rows], sums[tail_rows:]
        columns = hops.both(columns, came[end:], "rep", bit, 0).reshape(-1, width)
    mine = jnp.concatenate([qkv_total, late_sum, columns])
    came = hops.swap(mine, "rep", 1)
    smem = pl.BlockSpec(memory_space=pltpu.SMEM)
    vmem = pl.BlockSpec(memory_space=pltpu.VMEM)
    ada_grad, ada_bias_grad, qkv_owned, up_owned, down_owned, out_owned, *bias_sums = pl.pallas_call(
        functools.partial(finish_kernel, tail_rows=tail_rows),
        in_specs=[smem, vmem, vmem, vmem],
        out_specs=[vmem] * 10,
        out_shape=[
            shape_of((own, width), F32),
            shape_of((1, own), F32),
            shape_of((qkv_rows, width), F32),
            shape_of((up_rows, width), F32),
            shape_of((out_rows, hidden_width), F32),
            shape_of((out_rows, width), F32),
        ]
        + [shape_of((1, part.shape[0]), F32) for part in (qv_bias, out_bias, up_bias, down_bias)],
        compiler_params=pltpu.CompilerParams(vmem_limit_bytes=VMEM_LIMIT),
    )(core_scalar, mine, came, silu_all)
    ada_bias_grad = ada_bias_grad.reshape(-1)

    grad_silu = lax.dot_general(
        grad_modulation,
        ada_all.astype(F32),
        (((1,), (0,)), ((), ())),
        precision=lax.Precision.HIGHEST,
    )
    _, silu_pull = jax.vjp(jax.nn.silu, conditioning)
    condition_grad = silu_pull(grad_silu)[0]

    qv_sum, out_bias_sum, up_bias_sum, down_bias_sum = (part.reshape(-1) for part in bias_sums)
    return (
        output,
        tokens_grad,
        condition_grad,
        ada_grad.T,
        ada_bias_grad,
        qkv_owned.T,
        qv_sum,
        out_owned.T,
        out_bias_sum,
        up_owned.T,
        up_bias_sum,
        down_owned.T,
        down_bias_sum,
    )


def solution(mesh):
    return jax.shard_map(
        functools.partial(body, mesh.shape["dp"], mesh.shape["rep"]),
        mesh=mesh,
        in_specs=(
            P(("dp", "rep"), None, None),
            P(("dp", "rep"), None),
            P(None, "dp"),
            P("dp"),
            P(None, "dp"),
            P("dp"),
            P(None, "dp"),
            P("dp"),
            P(None, "dp"),
            P("dp"),
            P(None, "dp"),
            P("dp"),
            P(("dp", "rep"), None, None),
        ),
        out_specs=(
            P(("dp", "rep"), None, None),
            P(("dp", "rep"), None, None),
            P(("dp", "rep"), None),
            P(None, "dp"),
            P("dp"),
            P(None, "dp"),
            P("dp"),
            P(None, "dp"),
            P("dp"),
            P(None, "dp"),
            P("dp"),
            P(None, "dp"),
            P("dp"),
        ),
        check_vma=False,
    )
```

```python
import functools

import jax
import jax.numpy as jnp
from jax import lax
from jax.experimental import pallas as pl
from jax.experimental.pallas import tpu as pltpu
from jax.sharding import PartitionSpec as P

HEAD_DIM = 64
EPS = 1e-06
GELU_C = 0.7978845608028654
VMEM_LIMIT = 56 * 1024 * 1024
F32 = jnp.float32
BF16 = jnp.bfloat16


def dot_nn(left, right):
    return lax.dot_general(left, right, (((1,), (0,)), ((), ())), preferred_element_type=F32)


def dot_nt(left, right):
    return lax.dot_general(left, right, (((1,), (1,)), ((), ())), preferred_element_type=F32)


def dot_tn(left, right):
    return lax.dot_general(left, right, (((0,), (0,)), ((), ())), preferred_element_type=F32)


def normalise(values):
    average = jnp.mean(values, axis=-1, keepdims=True)
    centred = values - average
    spread = jnp.mean(centred * centred, axis=-1, keepdims=True)
    inverse = lax.rsqrt(spread + EPS)
    return centred * inverse, inverse


def normalise_back(upstream, normal, inverse):
    first = jnp.mean(upstream, axis=-1, keepdims=True)
    second = jnp.mean(upstream * normal, axis=-1, keepdims=True)
    return inverse * (upstream - first - normal * second)


STRIP = 64
GROUP = 3


def beside(*parts):
    return jnp.concatenate(parts, axis=1)


def above(*parts):
    return jnp.concatenate(parts, axis=0)


def strips(extent, size):
    return [slice(low, low + size) for low in range(0, extent, size)]


def head_slices(head):
    low = head * HEAD_DIM
    pair = low - low % (2 * HEAD_DIM)
    return slice(low, low + HEAD_DIM), slice(pair, pair + 2 * HEAD_DIM), low == pair


def in_groups(items, size):
    return [items[low : low + size] for low in range(0, len(items), size)]


def attention_forward_kernel(
    core_ref,
    tokens_ref,
    mod_ref,
    mine_ref,
    came_ref,
    bias_row_ref,
    normed_ref,
    qkv_ref,
    lse_ref,
    attended_ref,
    weight_ref,
    bias_ref,
):
    latents, length, width = tokens_ref.shape
    blank = jnp.zeros((HEAD_DIM, length), BF16)

    @pl.when(pl.program_id(0) == 0)
    def _():
        first = core_ref[0] == 0
        n_dp = mine_ref.shape[0]
        half_rows = weight_ref.shape[0] // (2 * n_dp)
        for owner in range(n_dp):
            mine = mine_ref[owner, :half_rows, :]
            came = came_ref[owner, :half_rows, :]
            low = 2 * owner * half_rows
            weight_ref[low : low + half_rows, :] = jnp.where(first, mine, came)
            weight_ref[low + half_rows : low + 2 * half_rows, :] = jnp.where(first, came, mine)
        bias_ref[...] = jnp.broadcast_to(bias_row_ref[...], (128, 3 * width)).T

    for latent in range(latents):
        for rows in strips(length, STRIP):
            normal, _ = normalise(tokens_ref[latent, rows, :].astype(F32))
            normed = normal * (1.0 + mod_ref[latent, 1:2, :]) + mod_ref[latent, 0:1, :]
            normed_ref[latent, rows, :] = normed.astype(BF16)
    normed = normed_ref[...].reshape(latents * length, width)
    for part in strips(3 * width, 2 * HEAD_DIM):
        bias = bias_ref[part, :]
        qkv = dot_nt(weight_ref[part, :], normed) + beside(*([bias] * (latents * length // 128)))
        qkv = qkv.astype(BF16)
        for latent in range(latents):
            qkv_ref[latent, part, :] = qkv[:, latent * length : (latent + 1) * length]
    keys_all = [qkv_ref[latent, width : 2 * width, :].T for latent in range(latents)]

    def scores_of(latent, head):
        own, pair, first = head_slices(head)
        queries = qkv_ref[latent, own, :]
        queries = above(queries, blank) if first else above(blank, queries)
        return dot_nn(keys_all[latent][:, pair], queries)

    def probs_of(latent, head, scores):
        parts = []
        for columns in strips(length, 128):
            strip = scores[:, columns] * HEAD_DIM ** (-0.5)
            highest = jnp.max(strip, axis=0, keepdims=True)
            shifted = jnp.exp(strip - highest)
            total = jnp.sum(shifted, axis=0, keepdims=True)
            parts.append((shifted * (1.0 / total)).astype(BF16))
            lse_ref[latent, head : head + 1, columns] = highest + jnp.log(total)
        return beside(*parts)

    def attend(latent, head, probs):
        own, _, _ = head_slices(head)
        values_in = qkv_ref[latent, 2 * width + own.start : 2 * width + own.stop, :]
        attended_ref[latent, own, :] = dot_nn(values_in, probs).astype(BF16)

    items = [(latent, head) for latent in range(latents) for head in range(width // HEAD_DIM)]
    groups = in_groups(items, GROUP)
    scores = [scores_of(*item) for item in groups[0]]
    previous = []
    for place, group in enumerate(groups):
        later = groups[place + 1] if place + 1 < len(groups) else []
        next_scores = [scores_of(*item) for item in later]
        probs = [probs_of(*item, value) for item, value in zip(group, scores)]
        for item, value in previous:
            attend(*item, value)
        previous = list(zip(group, probs))
        scores = next_scores
    for item, value in previous:
        attend(*item, value)


def by_side(core_ref, side, kept_ref, sent_ref, write):
    @pl.when(core_ref[0] == side)
    def _():
        write(kept_ref)

    @pl.when(core_ref[0] != side)
    def _():
        write(sent_ref)


def feed_kernel(
    core_ref,
    tokens_ref,
    cotangent_ref,
    attended_ref,
    mod_ref,
    late_ref,
    out_bias_ref,
    up_bias_row_ref,
    down_bias_ref,
    output_ref,
    grad_middle_ref,
    grad_attended_ref,
    grad_mod_ref,
    late_kept_ref,
    late_sent_ref,
    out_bias_grad_ref,
    up_bias_grad_ref,
    down_bias_grad_ref,
    out_acc,
    up_acc,
    down_acc,
    bias_acc,
    out_weight_ref,
    up_weight_ref,
    down_weight_ref,
    up_bias_ref,
    out_back,
    up_back,
    down_back,
    active_all,
    grad_hidden_all,
    middle_all,
    normal_all,
    branch_all,
    *,
    chunk,
):
    step = pl.program_id(0)
    n_dp = late_ref.shape[0]
    latents, length, width = tokens_ref.shape
    hidden_width = up_weight_ref.shape[0]
    tokens_all = latents * length
    up_rows, out_rows = hidden_width // n_dp, width // n_dp
    out_low = up_rows + out_rows * (hidden_width // width)

    @pl.when(step == 0)
    def _():
        out_acc[...] = jnp.zeros_like(out_acc)
        up_acc[...] = jnp.zeros_like(up_acc)
        down_acc[...] = jnp.zeros_like(down_acc)
        bias_acc[...] = jnp.zeros_like(bias_acc)
        for owner in range(n_dp):
            up_weight_ref[owner * up_rows : (owner + 1) * up_rows, :] = late_ref[owner, :up_rows, :]
            outs = slice(owner * out_rows, (owner + 1) * out_rows)
            for fold in range(hidden_width // width):
                low = up_rows + fold * out_rows
                down_weight_ref[outs, fold * width : (fold + 1) * width] = late_ref[
                    owner, low : low + out_rows, :
                ]
            out_weight_ref[outs, :] = late_ref[owner, out_low:, :]
        out_back[...] = out_weight_ref[...].T
        up_back[...] = up_weight_ref[...].T
        down_back[...] = down_weight_ref[...].T
        up_bias_ref[...] = jnp.broadcast_to(up_bias_row_ref[...], (128, hidden_width)).T

    attended = beside(*[attended_ref[latent] for latent in range(latents)])
    branch_wide = dot_nn(out_weight_ref[...], attended)
    normed_parts = []
    grad_feed_parts = []
    inverses = []
    down_sum = jnp.zeros((1, width), F32)
    for latent in range(latents):
        gate_one = mod_ref[latent, 2:3, :]
        shift_two = mod_ref[latent, 3:4, :]
        scale_two = 1.0 + mod_ref[latent, 4:5, :]
        gate_two = mod_ref[latent, 5:6, :]
        branch_tall = branch_wide[:, latent * length : (latent + 1) * length].T
        for rows in strips(length, STRIP):
            there = slice(latent * length + rows.start, latent * length + rows.stop)
            branch = branch_tall[rows] + out_bias_ref[...]
            branch_all[there, :] = branch
            middle = tokens_ref[latent, rows, :].astype(F32) + gate_one * branch
            middle_all[there, :] = middle
            normal, inverse = normalise(middle)
            normal_all[there, :] = normal
            inverses.append(inverse)
            normed_parts.append((normal * scale_two + shift_two).astype(BF16))
            grad_feed = (cotangent_ref[latent, rows, :].astype(F32) * gate_two).astype(BF16)
            grad_feed_parts.append(grad_feed)
            down_sum += jnp.sum(grad_feed.astype(F32), axis=0, keepdims=True)
    bias_acc[0:1, :] += down_sum
    normed_all = above(*normed_parts)
    grad_feed_all = above(*grad_feed_parts)

    def products(rows):
        return (
            dot_nt(up_weight_ref[rows, :], normed_all),
            dot_nt(down_back[rows, :], grad_feed_all),
        )

    parts = strips(hidden_width, chunk)
    ahead = products(parts[0])
    for place, part in enumerate(parts):
        hidden_wide, grad_wide = ahead
        if place + 1 < len(parts):
            ahead = products(parts[place + 1])
        for rows in strips(chunk, STRIP):
            there = slice(part.start + rows.start, part.start + rows.stop)
            bias = up_bias_ref[there, :]
            bias = beside(bias, bias)
            for columns in strips(tokens_all, 256):
                hidden = hidden_wide[rows, columns] + bias
                square = hidden * hidden
                bent = jnp.tanh(hidden * (GELU_C + (GELU_C * 0.044715) * square))
                half = 0.5 + 0.5 * bent
                active_all[there, columns] = (hidden * half).astype(BF16)
                slope = half + hidden * (0.5 - 0.5 * (bent * bent)) * (
                    GELU_C + (3.0 * GELU_C * 0.044715) * square
                )
                grad_hidden_all[there, columns] = (grad_wide[rows, columns] * slope).astype(BF16)

    feed_wide = dot_nn(down_weight_ref[...], active_all[...])
    grad_normed_wide = dot_nn(up_back[...], grad_hidden_all[...])
    ones = jnp.ones((tokens_all, 128), BF16)
    up_acc[...] += dot_nn(grad_hidden_all[...], beside(normed_all, ones))
    down_acc[...] += dot_nn(active_all[...], grad_feed_all)

    grad_branch_parts = []
    out_sum = jnp.zeros((1, width), F32)
    for latent in range(latents):
        gate_one = mod_ref[latent, 2:3, :]
        scale_two = 1.0 + mod_ref[latent, 4:5, :]
        gate_two = mod_ref[latent, 5:6, :]
        here = slice(latent * length, (latent + 1) * length)
        feed_tall = feed_wide[:, here].T
        grad_normed_tall = grad_normed_wide[:, here].T
        sums = [jnp.zeros((1, width), F32) for _ in range(4)]
        for rows in strips(length, STRIP):
            there = slice(here.start + rows.start, here.start + rows.stop)
            feed = feed_tall[rows] + down_bias_ref[...]
            grad_normed = grad_normed_tall[rows]
            incoming = cotangent_ref[latent, rows, :].astype(F32)
            normal = normal_all[there, :]
            output_ref[latent, rows, :] = (middle_all[there, :] + gate_two * feed).astype(BF16)
            grad_middle = incoming + normalise_back(
                grad_normed * scale_two, normal, inverses[there.start // STRIP]
            )
            grad_middle_ref[latent, rows, :] = grad_middle
            grad_branch = (grad_middle * gate_one).astype(BF16)
            grad_branch_parts.append(grad_branch)
            terms = (
                grad_middle * branch_all[there, :],
                grad_normed,
                grad_normed * normal,
                incoming * feed,
            )
            for place, term in enumerate(terms):
                sums[place] += jnp.sum(term, axis=0, keepdims=True)
            out_sum += jnp.sum(grad_branch.astype(F32), axis=0, keepdims=True)
        grad_mod_ref[latent] = above(*sums)
    bias_acc[1:2, :] += out_sum
    grad_branch_all = above(*grad_branch_parts)
    grad_attended = dot_nt(out_back[...], grad_branch_all).astype(BF16)
    for latent in range(latents):
        grad_attended_ref[latent] = grad_attended[:, latent * length : (latent + 1) * length]
    out_acc[...] += dot_nn(attended, grad_branch_all)

    @pl.when(step == pl.num_programs(0) - 1)
    def _():
        out_acc[...] = out_acc[...].T
        up_back[...] = down_acc[...].T.astype(BF16)
        folds = hidden_width // width // 2
        out_back_rows = out_rows // 2
        for side in range(2):

            def write(ref, side=side):
                for owner in range(n_dp):
                    ups = owner * up_rows + side * (up_rows // 2)
                    ref[owner, : up_rows // 2, :] = up_acc[
                        ups : ups + up_rows // 2, :width
                    ].astype(BF16)
                    outs = slice(owner * out_rows, (owner + 1) * out_rows)
                    for place in range(folds):
                        low = up_rows // 2 + place * out_rows
                        fold = side * folds + place
                        ref[owner, low : low + out_rows, :] = up_back[
                            outs, fold * width : (fold + 1) * width
                        ]
                    outs = owner * out_rows + side * out_back_rows
                    ref[owner, out_low // 2 :, :] = out_acc[
                        outs : outs + out_back_rows
                    ].astype(BF16)

            by_side(core_ref, side, late_kept_ref, late_sent_ref, write)
        up_bias_grad_ref[...] = up_acc[:, width:]
        down_bias_grad_ref[...] = bias_acc[0:1, :]
        out_bias_grad_ref[...] = bias_acc[1:2, :]


def attention_backward_kernel(
    core_ref,
    qkv_ref,
    lse_ref,
    grad_attended_ref,
    normed_ref,
    tokens_ref,
    grad_middle_ref,
    mod_ref,
    weight_ref,
    tokens_grad_ref,
    grad_mod_ref,
    kept_ref,
    sent_ref,
    bias_grad_ref,
    acc,
    weight_back,
    grad_qkv_ref,
):
    step = pl.program_id(0)
    latents, length, width = normed_ref.shape
    blank = jnp.zeros((HEAD_DIM, length), BF16)

    @pl.when(step == 0)
    def _():
        acc[...] = jnp.zeros_like(acc)
        weight_back[...] = weight_ref[...].T

    keys_all = [qkv_ref[latent, width : 2 * width, :].T for latent in range(latents)]
    values_all = [qkv_ref[latent, 2 * width : 3 * width, :].T for latent in range(latents)]

    def products(latent, head):
        own, pair, first = head_slices(head)
        queries = qkv_ref[latent, own, :]
        grad_out = grad_attended_ref[latent, own, :]
        queries = above(queries, blank) if first else above(blank, queries)
        grad_out = above(grad_out, blank) if first else above(blank, grad_out)
        return (
            dot_nn(keys_all[latent][:, pair], queries),
            dot_nn(values_all[latent][:, pair], grad_out),
        )

    def middle_of(latent, head, scores, grad_probs):
        low_parts = []
        grad_parts = []
        for columns in strips(length, 128):
            total = lse_ref[latent, head : head + 1, columns]
            probs = jnp.exp(scores[:, columns] * HEAD_DIM ** (-0.5) - total)
            terms = probs * grad_probs[:, columns]
            row_terms = jnp.sum(terms, axis=0, keepdims=True)
            grad_parts.append((probs * (grad_probs[:, columns] - row_terms)).astype(BF16))
            low_parts.append(probs.astype(BF16))
        return beside(*low_parts), beside(*grad_parts)

    def finish(latent, head, probs, grad_scores):
        own, _, _ = head_slices(head)
        low, high = own.start, own.stop
        queries = qkv_ref[latent, own, :]
        keys_in = qkv_ref[latent, width + low : width + high, :]
        grad_out = grad_attended_ref[latent, own, :]
        scale = HEAD_DIM ** (-0.5)
        grad_qkv_ref[latent, own, :] = (dot_nn(keys_in, grad_scores) * scale).astype(BF16)
        grad_qkv_ref[latent, width + low : width + high, :] = (
            dot_nt(queries, grad_scores) * scale
        ).astype(BF16)
        grad_qkv_ref[latent, 2 * width + low : 2 * width + high, :] = dot_nt(
            grad_out, probs
        ).astype(BF16)

    items = [(latent, head) for latent in range(latents) for head in range(width // HEAD_DIM)]
    groups = in_groups(items, GROUP)
    values = [products(*item) for item in groups[0]]
    previous = []
    for place, group in enumerate(groups):
        later = groups[place + 1] if place + 1 < len(groups) else []
        next_values = [products(*item) for item in later]
        middles = [middle_of(*item, *value) for item, value in zip(group, values)]
        for item, value in previous:
            finish(*item, *value)
        previous = list(zip(group, middles))
        values = next_values
    for item, value in previous:
        finish(*item, *value)

    grad_qkv = beside(*[grad_qkv_ref[latent] for latent in range(latents)])
    normed = normed_ref[...].reshape(latents * length, width)
    grad_normed_wide = dot_nn(weight_back[...], grad_qkv)
    acc[...] += dot_nn(grad_qkv, beside(normed, jnp.ones((latents * length, 128), BF16)))
    for latent in range(latents):
        grad_normed_tall = grad_normed_wide[:, latent * length : (latent + 1) * length].T
        scale_one = 1.0 + mod_ref[latent, 1:2, :]
        first = jnp.zeros((1, width), F32)
        second = jnp.zeros((1, width), F32)
        for rows in strips(length, STRIP):
            normal, inverse = normalise(tokens_ref[latent, rows, :].astype(F32))
            grad_normed = grad_normed_tall[rows]
            first += jnp.sum(grad_normed, axis=0, keepdims=True)
            second += jnp.sum(grad_normed * normal, axis=0, keepdims=True)
            back = normalise_back(grad_normed * scale_one, normal, inverse)
            tokens_grad_ref[latent, rows, :] = (grad_middle_ref[latent, rows, :] + back).astype(
                BF16
            )
        grad_mod_ref[latent] = above(first, second)

    @pl.when(step == pl.num_programs(0) - 1)
    def _():
        n_dp, tail_rows, _ = kept_ref.shape
        half_rows = 3 * width // (2 * n_dp)
        for side in range(2):

            def write(ref, side=side):
                for owner in range(n_dp):
                    low = (2 * owner + side) * half_rows
                    rows = acc[low : low + half_rows, :width]
                    rest = jnp.zeros((tail_rows - half_rows, width), F32)
                    ref[owner] = above(rows, rest).astype(BF16)

            by_side(core_ref, side, kept_ref, sent_ref, write)
        bias_grad_ref[...] = acc[:, width:]


def finish_kernel(
    core_ref,
    mine_ref,
    came_ref,
    silu_ref,
    ada_ref,
    ada_bias_ref,
    qkv_ref,
    up_ref,
    down_ref,
    out_ref,
    qv_bias_ref,
    out_bias_ref,
    up_bias_ref,
    down_bias_ref,
    *,
    tail_rows,
):
    first = core_ref[0] == 0
    own = ada_ref.shape[0]
    half_rows = qkv_ref.shape[0] // 2
    up_half, out_rows = up_ref.shape[0] // 2, out_ref.shape[0]
    width = out_ref.shape[1]
    folds = down_ref.shape[1] // width // 2
    out_low = tail_rows + up_half + folds * out_rows
    end = out_low + out_rows // 2
    mine = mine_ref[:end, :].astype(F32)
    came = came_ref[:end, :].astype(F32)
    for side in range(2):
        part = jnp.where(first, mine, came) if side == 0 else jnp.where(first, came, mine)
        qkv_ref[side * half_rows : (side + 1) * half_rows, :] = part[:half_rows]
        up_ref[side * up_half : (side + 1) * up_half, :] = part[tail_rows : tail_rows + up_half]
        for place in range(folds):
            low = tail_rows + up_half + place * out_rows
            columns = (side * folds + place) * width
            down_ref[:, columns : columns + width] = part[low : low + out_rows]
        out_ref[side * (out_rows // 2) : (side + 1) * (out_rows // 2), :] = part[out_low:]
    biases = mine[half_rows : half_rows + 1] + came[half_rows : half_rows + 1]
    low = 0
    for ref in (qv_bias_ref, out_bias_ref, up_bias_ref, down_bias_ref):
        ref[...] = biases[:, low : low + ref.shape[1]]
        low += ref.shape[1]
    mine = mine_ref[end:, :]
    came = came_ref[end:, :]
    columns = above(jnp.where(first, mine, came), jnp.where(first, came, mine))
    ada_ref[...] = dot_tn(columns, silu_ref[...])[:own]
    ada_bias_ref[...] = jnp.sum(columns.astype(F32), axis=0, keepdims=True)[:, :own]


def each(shape, count):
    zeros = (0,) * (len(shape) - 1)
    return pl.BlockSpec((count,) + tuple(shape[1:]), lambda step: (step,) + zeros)


def whole(shape):
    zeros = (0,) * len(shape)
    return pl.BlockSpec(tuple(shape), lambda step: zeros)


def run_kernel(kernel, count, streamed_out, fixed_out, scratch, streamed, fixed, cost, scalars=()):
    return pl.pallas_call(
        kernel,
        grid=(streamed[0].shape[0] // count,),
        in_specs=[pl.BlockSpec(memory_space=pltpu.SMEM)] * len(scalars)
        + [each(item.shape, count) for item in streamed]
        + [whole(item.shape) for item in fixed],
        out_specs=[each(item.shape, count) for item in streamed_out]
        + [whole(item.shape) for item in fixed_out],
        out_shape=list(streamed_out) + list(fixed_out),
        scratch_shapes=scratch,
        compiler_params=pltpu.CompilerParams(
            dimension_semantics=("arbitrary",), vmem_limit_bytes=VMEM_LIMIT
        ),
        cost_estimate=cost,
    )(*scalars, *streamed, *fixed)


def shape_of(dims, kind):
    return jax.ShapeDtypeStruct(tuple(dims), kind)


AXES = ("dp", "rep")


class Hops:
    def __init__(self, n_dp, n_rep):
        self.sizes = {"dp": n_dp, "rep": n_rep}
        self.place = {name: lax.axis_index(name) for name in AXES}

    def bits(self, name):
        return [1 << shift for shift in range(self.sizes[name].bit_length() - 1)]

    def mine(self, name, bit):
        return (self.place[name] // bit) % 2

    def swap(self, value, name, bit):
        n_dp, n_rep = self.sizes["dp"], self.sizes["rep"]
        flip_dp, flip_rep = (bit, 0) if name == "dp" else (0, bit)
        pairs = [
            (d * n_rep + r, (d ^ flip_dp) * n_rep + (r ^ flip_rep))
            for d in range(n_dp)
            for r in range(n_rep)
        ]
        return lax.ppermute(value, AXES, pairs)

    def both(self, kept, came, name, bit, axis):
        upper = self.mine(name, bit) == 1
        return jnp.stack(
            [jnp.where(upper, came, kept), jnp.where(upper, kept, came)], axis=axis
        )

    def cut(self, value, name, bit, axis):
        here = self.mine(name, bit)
        return (
            lax.dynamic_index_in_dim(value, here, axis, keepdims=False),
            lax.dynamic_index_in_dim(value, 1 - here, axis, keepdims=False),
        )


def pad_rows(values, count):
    return jnp.pad(values, ((0, 0),) * (values.ndim - 2) + ((0, count - values.shape[-2]), (0, 0)))


def up_to(count, multiple):
    return -(-count // multiple) * multiple


def body(
    n_dp,
    n_rep,
    tokens,
    conditioning,
    ada_weight,
    ada_bias,
    qkv_weight,
    qv_bias,
    out_weight,
    out_bias,
    up_weight,
    up_bias,
    down_weight,
    down_bias,
    cotangent,
):
    latents, length, width = tokens.shape
    hidden_width = up_weight.shape[1] * n_dp
    heads = width // HEAD_DIM
    rows = latents * length
    hops = Hops(n_dp, n_rep)
    folds = hidden_width // width

    up_rows, out_rows = up_weight.shape[1], out_weight.shape[1]
    down_shard = down_weight.T.reshape(out_rows, folds, width).transpose(1, 0, 2)
    late_shard = jnp.concatenate(
        [up_weight.T, down_shard.reshape(folds * out_rows, width), out_weight.T]
    )
    silu_low = jax.nn.silu(conditioning).astype(BF16)
    qkv_rows = qkv_weight.shape[1]
    half_rows = qkv_rows // 2
    core = hops.mine("rep", 1)
    bias_shard = jnp.concatenate([qv_bias, out_bias, up_bias, down_bias])
    bias_rows = 1
    front = jnp.concatenate(
        [
            lax.dynamic_slice_in_dim(qkv_weight.T, core * half_rows, half_rows, axis=0),
            silu_low,
            jnp.pad(bias_shard, (0, width - bias_shard.shape[0]))[None],
        ]
    )
    front = pad_rows(front, up_to(front.shape[0], 8))
    front, late_shard = lax.optimization_barrier((front, late_shard))
    late = lax.all_gather(late_shard, "dp", axis=0)
    ada_shard, _ = lax.optimization_barrier((ada_weight.T, late))
    ada_all = lax.all_gather(ada_shard, "dp", axis=0, tiled=True)
    front = lax.all_to_all(
        jnp.broadcast_to(front, (n_dp,) + front.shape), "dp", 0, 0, tiled=True
    )

    silu_group = front[:, half_rows : half_rows + latents].reshape(n_dp * latents, width)
    mod = jnp.dot(silu_group, ada_weight, preferred_element_type=F32) + ada_bias.astype(F32)
    mod = lax.all_to_all(mod.reshape(n_dp, latents, -1), "dp", 0, 0, tiled=True)
    modulation = mod.transpose(1, 0, 2).reshape(latents, 6, width)

    mine = front[:, : half_rows + latents]
    came = hops.swap(mine, "rep", 1)
    silu_all = hops.both(mine[:, half_rows:], came[:, half_rows:], "rep", 1, 0)
    for bit in hops.bits("rep")[1:]:
        silu_all = hops.both(silu_all, hops.swap(silu_all, "rep", bit), "rep", bit, 0)
    silu_all = silu_all.reshape(n_rep // 2, 2, n_dp * latents, width).transpose(1, 0, 2, 3)
    silu_all = silu_all.reshape(-1, width)

    bias_all = front[:, half_rows + latents].astype(F32)
    cuts = [0]
    for part in (qv_bias, out_bias, up_bias, down_bias):
        cuts.append(cuts[-1] + part.shape[0])
    qv_full, out_full, up_full, down_full = (
        bias_all[:, low:high].reshape(1, -1) for low, high in zip(cuts[:-1], cuts[1:])
    )
    qkv_bias = jnp.concatenate(
        [qv_full[:, :width], jnp.zeros((1, width), F32), qv_full[:, width:]], axis=1
    )

    core_scalar = core.astype(jnp.int32).reshape(1)
    normed, qkv, lse, attended, qkv_full = run_kernel(
        attention_forward_kernel,
        4,
        [
            shape_of((latents, length, width), BF16),
            shape_of((latents, 3 * width, length), BF16),
            shape_of((latents, 8 * ((heads + 7) // 8), length), F32),
            shape_of((latents, width, length), BF16),
        ],
        [shape_of((3 * width, width), BF16)],
        [pltpu.VMEM((3 * width, 128), F32)],
        [tokens, modulation],
        [mine, came, qkv_bias],
        pl.CostEstimate(
            flops=2 * rows * width * (3 * width + 2 * length),
            bytes_accessed=rows * width * 12,
            transcendentals=rows * heads * length,
        ),
        [core_scalar],
    )

    attended, silu_all = lax.optimization_barrier((attended, silu_all))
    (
        output,
        grad_middle,
        grad_attended,
        grad_mod_two,
        late_kept,
        late_sent,
        out_bias_grad,
        up_bias_grad,
        down_bias_grad,
    ) = run_kernel(
        functools.partial(feed_kernel, chunk=256),
        4,
        [
            shape_of((latents, length, width), BF16),
            shape_of((latents, length, width), F32),
            shape_of((latents, width, length), BF16),
            shape_of((latents, 4, width), F32),
        ],
        [
            shape_of((n_dp, late.shape[1] // 2, width), BF16),
            shape_of((n_dp, late.shape[1] // 2, width), BF16),
            shape_of((1, width), F32),
            shape_of((hidden_width, 128), F32),
            shape_of((1, width), F32),
        ],
        [
            pltpu.VMEM((width, width), F32),
            pltpu.VMEM((hidden_width, width + 128), F32),
            pltpu.VMEM((hidden_width, width), F32),
            pltpu.VMEM((8, width), F32),
            pltpu.VMEM((width, width), BF16),
            pltpu.VMEM((hidden_width, width), BF16),
            pltpu.VMEM((width, hidden_width), BF16),
            pltpu.VMEM((hidden_width, 128), F32),
            pltpu.VMEM((width, width), BF16),
            pltpu.VMEM((width, hidden_width), BF16),
            pltpu.VMEM((hidden_width, width), BF16),
            pltpu.VMEM((hidden_width, 4 * length), BF16),
            pltpu.VMEM((hidden_width, 4 * length), BF16),
            pltpu.VMEM((4 * length, width), F32),
            pltpu.VMEM((4 * length, width), F32),
            pltpu.VMEM((4 * length, width), F32),
        ],
        [tokens, cotangent, attended, modulation],
        [late, out_full, up_full, down_full],
        pl.CostEstimate(
            flops=6 * rows * width * (width + 2 * hidden_width),
            bytes_accessed=rows * width * 14,
            transcendentals=rows * hidden_width,
        ),
        [core_scalar],
    )

    late_sent, ada_all = lax.optimization_barrier((late_sent, ada_all))
    late_half = late_kept.astype(F32) + hops.swap(late_sent, "rep", 1).astype(F32)
    late_half = late_half.astype(BF16)
    late_parts = lax.all_to_all(late_half, "dp", 0, 0, tiled=True)

    normed, _ = lax.optimization_barrier((normed, late_half))
    tail_rows = up_to(half_rows + 1, 8)
    tokens_grad, grad_mod_one, qkv_kept, qkv_sent, qkv_bias_grad = run_kernel(
        attention_backward_kernel,
        2,
        [shape_of((latents, length, width), BF16), shape_of((latents, 2, width), F32)],
        [
            shape_of((n_dp, tail_rows, width), BF16),
            shape_of((n_dp, tail_rows, width), BF16),
            shape_of((3 * width, 128), F32),
        ],
        [
            pltpu.VMEM((3 * width, width + 128), F32),
            pltpu.VMEM((width, 3 * width), BF16),
            pltpu.VMEM((2, 3 * width, length), BF16),
        ],
        [qkv, lse, grad_attended, normed, tokens, grad_middle, modulation],
        [qkv_full],
        pl.CostEstimate(flops=1, bytes_accessed=1, transcendentals=0),
        [core_scalar],
    )
    qkv_sent, late_parts = lax.optimization_barrier((qkv_sent, late_parts))
    late_sum = jnp.sum(late_parts.astype(F32), axis=0).astype(BF16)

    qkv_columns = qkv_bias_grad[:, 0]
    bias_blocks = jnp.concatenate(
        [
            jnp.concatenate([qkv_columns[:width], qkv_columns[2 * width :]]).reshape(n_dp, -1),
            out_bias_grad.reshape(n_dp, -1),
            up_bias_grad[:, 0].reshape(n_dp, -1),
            down_bias_grad.reshape(n_dp, -1),
        ],
        axis=1,
    )
    bias_blocks = jnp.pad(
        bias_blocks[:, None],
        ((0, 0), (half_rows, tail_rows - half_rows - 1), (0, width - cuts[-1])),
    )
    total = qkv_kept.astype(F32) + hops.swap(qkv_sent, "rep", 1).astype(F32) + bias_blocks

    grad_modulation = jnp.concatenate([grad_mod_one, grad_mod_two], axis=1).reshape(
        latents, 6 * width
    )

    own = 6 * width // n_dp
    columns = grad_modulation.reshape(latents, n_dp, own).transpose(1, 0, 2).astype(BF16)
    columns = jnp.pad(columns, ((0, 0), (0, 0), (0, up_to(own, width) - own)))
    parts = lax.all_to_all(
        jnp.concatenate([total.astype(BF16), columns], axis=1), "dp", 0, 0, tiled=True
    )
    total = jnp.sum(parts[:, :tail_rows].astype(F32), axis=0)
    columns = parts[:, tail_rows:].reshape(n_dp * latents, width)

    qkv_total = total.astype(BF16)
    end = tail_rows + late_sum.shape[0]
    for bit in hops.bits("rep")[1:]:
        sums = jnp.concatenate([qkv_total, late_sum])
        came = hops.swap(jnp.concatenate([sums, columns]), "rep", bit)
        sums = (sums.astype(F32) + came[:end].astype(F32)).astype(BF16)
        qkv_total, late_sum = sums[:tail_rows], sums[tail_rows:]
        columns = hops.both(columns, came[end:], "rep", bit, 0).reshape(-1, width)
    mine = jnp.concatenate([qkv_total, late_sum, columns])
    came = hops.swap(mine, "rep", 1)
    smem = pl.BlockSpec(memory_space=pltpu.SMEM)
    vmem = pl.BlockSpec(memory_space=pltpu.VMEM)
    ada_grad, ada_bias_grad, qkv_owned, up_owned, down_owned, out_owned, *bias_sums = pl.pallas_call(
        functools.partial(finish_kernel, tail_rows=tail_rows),
        in_specs=[smem, vmem, vmem, vmem],
        out_specs=[vmem] * 10,
        out_shape=[
            shape_of((own, width), F32),
            shape_of((1, own), F32),
            shape_of((qkv_rows, width), F32),
            shape_of((up_rows, width), F32),
            shape_of((out_rows, hidden_width), F32),
            shape_of((out_rows, width), F32),
        ]
        + [shape_of((1, part.shape[0]), F32) for part in (qv_bias, out_bias, up_bias, down_bias)],
        compiler_params=pltpu.CompilerParams(vmem_limit_bytes=VMEM_LIMIT),
    )(core_scalar, mine, came, silu_all)
    ada_bias_grad = ada_bias_grad.reshape(-1)

    grad_silu = lax.dot_general(
        grad_modulation,
        ada_all.astype(F32),
        (((1,), (0,)), ((), ())),
        precision=lax.Precision.HIGHEST,
    )
    _, silu_pull = jax.vjp(jax.nn.silu, conditioning)
    condition_grad = silu_pull(grad_silu)[0]

    qv_sum, out_bias_sum, up_bias_sum, down_bias_sum = (part.reshape(-1) for part in bias_sums)
    return (
        output,
        tokens_grad,
        condition_grad,
        ada_grad.T,
        ada_bias_grad,
        qkv_owned.T,
        qv_sum,
        out_owned.T,
        out_bias_sum,
        up_owned.T,
        up_bias_sum,
        down_owned.T,
        down_bias_sum,
    )


def solution(mesh):
    return jax.shard_map(
        functools.partial(body, mesh.shape["dp"], mesh.shape["rep"]),
        mesh=mesh,
        in_specs=(
            P(("dp", "rep"), None, None),
            P(("dp", "rep"), None),
            P(None, "dp"),
            P("dp"),
            P(None, "dp"),
            P("dp"),
            P(None, "dp"),
            P("dp"),
            P(None, "dp"),
            P("dp"),
            P(None, "dp"),
            P("dp"),
            P(("dp", "rep"), None, None),
        ),
        out_specs=(
            P(("dp", "rep"), None, None),
            P(("dp", "rep"), None, None),
            P(("dp", "rep"), None),
            P(None, "dp"),
            P("dp"),
            P(None, "dp"),
            P("dp"),
            P(None, "dp"),
            P("dp"),
            P(None, "dp"),
            P("dp"),
            P(None, "dp"),
            P("dp"),
        ),
        check_vma=False,
    )
```

```python
import functools

import jax
import jax.numpy as jnp
from jax import lax
from jax.experimental import pallas as pl
from jax.experimental.pallas import tpu as pltpu
from jax.sharding import PartitionSpec as P

HEAD_DIM = 64
EPS = 1e-06
GELU_C = 0.7978845608028654
VMEM_LIMIT = 56 * 1024 * 1024
F32 = jnp.float32
BF16 = jnp.bfloat16


def dot_nn(left, right):
    return lax.dot_general(left, right, (((1,), (0,)), ((), ())), preferred_element_type=F32)


def dot_nt(left, right):
    return lax.dot_general(left, right, (((1,), (1,)), ((), ())), preferred_element_type=F32)


def dot_tn(left, right):
    return lax.dot_general(left, right, (((0,), (0,)), ((), ())), preferred_element_type=F32)


def normalise(values):
    average = jnp.mean(values, axis=-1, keepdims=True)
    centred = values - average
    spread = jnp.mean(centred * centred, axis=-1, keepdims=True)
    inverse = lax.rsqrt(spread + EPS)
    return centred * inverse, inverse


def normalise_back(upstream, normal, inverse):
    first = jnp.mean(upstream, axis=-1, keepdims=True)
    second = jnp.mean(upstream * normal, axis=-1, keepdims=True)
    return inverse * (upstream - first - normal * second)


STRIP = 32
GROUP = 3


def beside(*parts):
    return jnp.concatenate(parts, axis=1)


def above(*parts):
    return jnp.concatenate(parts, axis=0)


def strips(extent, size):
    return [slice(low, low + size) for low in range(0, extent, size)]


def head_slices(head):
    low = head * HEAD_DIM
    pair = low - low % (2 * HEAD_DIM)
    return slice(low, low + HEAD_DIM), slice(pair, pair + 2 * HEAD_DIM), low == pair


def in_groups(items, size):
    return [items[low : low + size] for low in range(0, len(items), size)]


def attention_forward_kernel(
    core_ref,
    tokens_ref,
    mod_ref,
    mine_ref,
    came_ref,
    bias_row_ref,
    normed_ref,
    qkv_ref,
    lse_ref,
    attended_ref,
    weight_ref,
    bias_ref,
):
    latents, length, width = tokens_ref.shape
    blank = jnp.zeros((HEAD_DIM, length), BF16)

    @pl.when(pl.program_id(0) == 0)
    def _():
        first = core_ref[0] == 0
        n_dp = mine_ref.shape[0]
        half_rows = weight_ref.shape[0] // (2 * n_dp)
        for owner in range(n_dp):
            mine = mine_ref[owner, :half_rows, :]
            came = came_ref[owner, :half_rows, :]
            low = 2 * owner * half_rows
            weight_ref[low : low + half_rows, :] = jnp.where(first, mine, came)
            weight_ref[low + half_rows : low + 2 * half_rows, :] = jnp.where(first, came, mine)
        bias_ref[...] = jnp.broadcast_to(bias_row_ref[...], (128, 3 * width)).T

    for latent in range(latents):
        for rows in strips(length, STRIP):
            normal, _ = normalise(tokens_ref[latent, rows, :].astype(F32))
            normed = normal * (1.0 + mod_ref[latent, 1:2, :]) + mod_ref[latent, 0:1, :]
            normed_ref[latent, rows, :] = normed.astype(BF16)
    normed = normed_ref[...].reshape(latents * length, width)
    for part in strips(3 * width, 2 * HEAD_DIM):
        bias = bias_ref[part, :]
        qkv = dot_nt(weight_ref[part, :], normed) + beside(*([bias] * (latents * length // 128)))
        qkv = qkv.astype(BF16)
        for latent in range(latents):
            qkv_ref[latent, part, :] = qkv[:, latent * length : (latent + 1) * length]
    keys_all = [qkv_ref[latent, width : 2 * width, :].T for latent in range(latents)]

    def scores_of(latent, head):
        own, pair, first = head_slices(head)
        queries = qkv_ref[latent, own, :]
        queries = above(queries, blank) if first else above(blank, queries)
        return dot_nn(keys_all[latent][:, pair], queries)

    def probs_of(latent, head, scores):
        parts = []
        for columns in strips(length, 128):
            strip = scores[:, columns] * HEAD_DIM ** (-0.5)
            highest = jnp.max(strip, axis=0, keepdims=True)
            shifted = jnp.exp(strip - highest)
            total = jnp.sum(shifted, axis=0, keepdims=True)
            parts.append((shifted * (1.0 / total)).astype(BF16))
            lse_ref[latent, head : head + 1, columns] = highest + jnp.log(total)
        return beside(*parts)

    def attend(latent, head, probs):
        own, _, _ = head_slices(head)
        values_in = qkv_ref[latent, 2 * width + own.start : 2 * width + own.stop, :]
        attended_ref[latent, own, :] = dot_nn(values_in, probs).astype(BF16)

    items = [(latent, head) for latent in range(latents) for head in range(width // HEAD_DIM)]
    groups = in_groups(items, GROUP)
    scores = [scores_of(*item) for item in groups[0]]
    previous = []
    for place, group in enumerate(groups):
        later = groups[place + 1] if place + 1 < len(groups) else []
        next_scores = [scores_of(*item) for item in later]
        probs = [probs_of(*item, value) for item, value in zip(group, scores)]
        for item, value in previous:
            attend(*item, value)
        previous = list(zip(group, probs))
        scores = next_scores
    for item, value in previous:
        attend(*item, value)


def by_side(core_ref, side, kept_ref, sent_ref, write):
    @pl.when(core_ref[0] == side)
    def _():
        write(kept_ref)

    @pl.when(core_ref[0] != side)
    def _():
        write(sent_ref)


def feed_kernel(
    core_ref,
    tokens_ref,
    cotangent_ref,
    attended_ref,
    mod_ref,
    late_ref,
    biases_ref,
    output_ref,
    grad_middle_ref,
    grad_attended_ref,
    grad_mod_ref,
    late_kept_ref,
    late_sent_ref,
    out_bias_grad_ref,
    up_bias_grad_ref,
    down_bias_grad_ref,
    out_acc,
    up_acc,
    down_acc,
    bias_acc,
    out_weight_ref,
    up_weight_ref,
    down_weight_ref,
    up_bias_ref,
    out_bias_ref,
    down_bias_ref,
    up_bias_row_ref,
    out_back,
    up_back,
    down_back,
    active_all,
    grad_hidden_all,
    middle_all,
    normal_all,
    branch_all,
    *,
    chunk,
):
    step = pl.program_id(0)
    n_dp = late_ref.shape[0]
    latents, length, width = tokens_ref.shape
    hidden_width = up_weight_ref.shape[0]
    tokens_all = latents * length
    up_rows, out_rows = hidden_width // n_dp, width // n_dp
    out_low = up_rows + out_rows * (hidden_width // width)

    @pl.when(step == 0)
    def _():
        out_acc[...] = jnp.zeros_like(out_acc)
        up_acc[...] = jnp.zeros_like(up_acc)
        down_acc[...] = jnp.zeros_like(down_acc)
        bias_acc[...] = jnp.zeros_like(bias_acc)
        for owner in range(n_dp):
            up_weight_ref[owner * up_rows : (owner + 1) * up_rows, :] = late_ref[owner, :up_rows, :]
            outs = slice(owner * out_rows, (owner + 1) * out_rows)
            for fold in range(hidden_width // width):
                low = up_rows + fold * out_rows
                down_weight_ref[outs, fold * width : (fold + 1) * width] = late_ref[
                    owner, low : low + out_rows, :
                ]
            out_weight_ref[outs, :] = late_ref[owner, out_low:, :]
        out_back[...] = out_weight_ref[...].T
        up_back[...] = up_weight_ref[...].T
        down_back[...] = down_weight_ref[...].T
        low = biases_ref.shape[1] - 2 * out_rows - up_rows
        for ref, size in ((out_bias_ref, out_rows), (up_bias_row_ref, up_rows), (down_bias_ref, out_rows)):
            for owner in range(n_dp):
                ref[0:1, owner * size : (owner + 1) * size] = biases_ref[
                    owner : owner + 1, low : low + size
                ]
            low += size
        up_bias_ref[...] = jnp.broadcast_to(up_bias_row_ref[...], (128, hidden_width)).T

    attended = beside(*[attended_ref[latent] for latent in range(latents)])
    branch_wide = dot_nn(out_weight_ref[...], attended)
    normed_parts = []
    grad_feed_parts = []
    inverses = []
    down_sum = jnp.zeros((1, width), F32)
    for latent in range(latents):
        gate_one = mod_ref[latent, 2:3, :]
        shift_two = mod_ref[latent, 3:4, :]
        scale_two = 1.0 + mod_ref[latent, 4:5, :]
        gate_two = mod_ref[latent, 5:6, :]
        branch_tall = branch_wide[:, latent * length : (latent + 1) * length].T
        for rows in strips(length, STRIP):
            there = slice(latent * length + rows.start, latent * length + rows.stop)
            branch = branch_tall[rows] + out_bias_ref[...]
            branch_all[there, :] = branch
            middle = tokens_ref[latent, rows, :].astype(F32) + gate_one * branch
            middle_all[there, :] = middle
            normal, inverse = normalise(middle)
            normal_all[there, :] = normal
            inverses.append(inverse)
            normed_parts.append((normal * scale_two + shift_two).astype(BF16))
            grad_feed = (cotangent_ref[latent, rows, :].astype(F32) * gate_two).astype(BF16)
            grad_feed_parts.append(grad_feed)
            down_sum += jnp.sum(grad_feed.astype(F32), axis=0, keepdims=True)
    bias_acc[0:1, :] += down_sum
    normed_all = above(*normed_parts)
    grad_feed_all = above(*grad_feed_parts)

    def products(rows):
        return (
            dot_nt(up_weight_ref[rows, :], normed_all),
            dot_nt(down_back[rows, :], grad_feed_all),
        )

    parts = strips(hidden_width, chunk)
    ahead = products(parts[0])
    for place, part in enumerate(parts):
        hidden_wide, grad_wide = ahead
        if place + 1 < len(parts):
            ahead = products(parts[place + 1])
        for rows in strips(chunk, STRIP):
            there = slice(part.start + rows.start, part.start + rows.stop)
            bias = up_bias_ref[there, :]
            bias = beside(bias, bias)
            for columns in strips(tokens_all, 256):
                hidden = hidden_wide[rows, columns] + bias
                square = hidden * hidden
                bent = jnp.tanh(hidden * (GELU_C + (GELU_C * 0.044715) * square))
                half = 0.5 + 0.5 * bent
                active_all[there, columns] = (hidden * half).astype(BF16)
                slope = half + hidden * (0.5 - 0.5 * (bent * bent)) * (
                    GELU_C + (3.0 * GELU_C * 0.044715) * square
                )
                grad_hidden_all[there, columns] = (grad_wide[rows, columns] * slope).astype(BF16)

    feed_wide = dot_nn(down_weight_ref[...], active_all[...])
    grad_normed_wide = dot_nn(up_back[...], grad_hidden_all[...])
    ones = jnp.ones((tokens_all, 128), BF16)
    up_acc[...] += dot_nn(grad_hidden_all[...], beside(normed_all, ones))
    down_acc[...] += dot_nn(active_all[...], grad_feed_all)

    grad_branch_parts = []
    out_sum = jnp.zeros((1, width), F32)
    for latent in range(latents):
        gate_one = mod_ref[latent, 2:3, :]
        scale_two = 1.0 + mod_ref[latent, 4:5, :]
        gate_two = mod_ref[latent, 5:6, :]
        here = slice(latent * length, (latent + 1) * length)
        feed_tall = feed_wide[:, here].T
        grad_normed_tall = grad_normed_wide[:, here].T
        sums = [jnp.zeros((1, width), F32) for _ in range(4)]
        for rows in strips(length, STRIP):
            there = slice(here.start + rows.start, here.start + rows.stop)
            feed = feed_tall[rows] + down_bias_ref[...]
            grad_normed = grad_normed_tall[rows]
            incoming = cotangent_ref[latent, rows, :].astype(F32)
            normal = normal_all[there, :]
            output_ref[latent, rows, :] = (middle_all[there, :] + gate_two * feed).astype(BF16)
            grad_middle = incoming + normalise_back(
                grad_normed * scale_two, normal, inverses[there.start // STRIP]
            )
            grad_middle_ref[latent, rows, :] = grad_middle
            grad_branch = (grad_middle * gate_one).astype(BF16)
            grad_branch_parts.append(grad_branch)
            terms = (
                grad_middle * branch_all[there, :],
                grad_normed,
                grad_normed * normal,
                incoming * feed,
            )
            for place, term in enumerate(terms):
                sums[place] += jnp.sum(term, axis=0, keepdims=True)
            out_sum += jnp.sum(grad_branch.astype(F32), axis=0, keepdims=True)
        grad_mod_ref[latent] = above(*sums)
    bias_acc[1:2, :] += out_sum
    grad_branch_all = above(*grad_branch_parts)
    grad_attended = dot_nt(out_back[...], grad_branch_all).astype(BF16)
    for latent in range(latents):
        grad_attended_ref[latent] = grad_attended[:, latent * length : (latent + 1) * length]
    out_acc[...] += dot_nn(attended, grad_branch_all)

    @pl.when(step == pl.num_programs(0) - 1)
    def _():
        out_acc[...] = out_acc[...].T
        up_back[...] = down_acc[...].T.astype(BF16)
        folds = hidden_width // width // 2
        out_back_rows = out_rows // 2
        for side in range(2):

            def write(ref, side=side):
                for owner in range(n_dp):
                    ups = owner * up_rows + side * (up_rows // 2)
                    ref[owner, : up_rows // 2, :] = up_acc[
                        ups : ups + up_rows // 2, :width
                    ].astype(BF16)
                    outs = slice(owner * out_rows, (owner + 1) * out_rows)
                    for place in range(folds):
                        low = up_rows // 2 + place * out_rows
                        fold = side * folds + place
                        ref[owner, low : low + out_rows, :] = up_back[
                            outs, fold * width : (fold + 1) * width
                        ]
                    outs = owner * out_rows + side * out_back_rows
                    ref[owner, out_low // 2 :, :] = out_acc[
                        outs : outs + out_back_rows
                    ].astype(BF16)

            by_side(core_ref, side, late_kept_ref, late_sent_ref, write)
        up_bias_grad_ref[...] = up_acc[:, width:]
        down_bias_grad_ref[...] = bias_acc[0:1, :]
        out_bias_grad_ref[...] = bias_acc[1:2, :]


def attention_backward_kernel(
    core_ref,
    qkv_ref,
    lse_ref,
    grad_attended_ref,
    normed_ref,
    tokens_ref,
    grad_middle_ref,
    mod_ref,
    weight_ref,
    tokens_grad_ref,
    grad_mod_ref,
    kept_ref,
    sent_ref,
    bias_grad_ref,
    acc,
    weight_back,
    grad_qkv_ref,
):
    step = pl.program_id(0)
    latents, length, width = normed_ref.shape
    blank = jnp.zeros((HEAD_DIM, length), BF16)

    @pl.when(step == 0)
    def _():
        acc[...] = jnp.zeros_like(acc)
        weight_back[...] = weight_ref[...].T

    keys_all = [qkv_ref[latent, width : 2 * width, :].T for latent in range(latents)]
    values_all = [qkv_ref[latent, 2 * width : 3 * width, :].T for latent in range(latents)]

    def products(latent, head):
        own, pair, first = head_slices(head)
        queries = qkv_ref[latent, own, :]
        grad_out = grad_attended_ref[latent, own, :]
        queries = above(queries, blank) if first else above(blank, queries)
        grad_out = above(grad_out, blank) if first else above(blank, grad_out)
        return (
            dot_nn(keys_all[latent][:, pair], queries),
            dot_nn(values_all[latent][:, pair], grad_out),
        )

    def middle_of(latent, head, scores, grad_probs):
        low_parts = []
        grad_parts = []
        for columns in strips(length, 128):
            total = lse_ref[latent, head : head + 1, columns]
            probs = jnp.exp(scores[:, columns] * HEAD_DIM ** (-0.5) - total)
            terms = probs * grad_probs[:, columns]
            row_terms = jnp.sum(terms, axis=0, keepdims=True)
            grad_parts.append((probs * (grad_probs[:, columns] - row_terms)).astype(BF16))
            low_parts.append(probs.astype(BF16))
        return beside(*low_parts), beside(*grad_parts)

    def finish(latent, head, probs, grad_scores):
        own, _, _ = head_slices(head)
        low, high = own.start, own.stop
        queries = qkv_ref[latent, own, :]
        keys_in = qkv_ref[latent, width + low : width + high, :]
        grad_out = grad_attended_ref[latent, own, :]
        scale = HEAD_DIM ** (-0.5)
        grad_qkv_ref[latent, own, :] = (dot_nn(keys_in, grad_scores) * scale).astype(BF16)
        grad_qkv_ref[latent, width + low : width + high, :] = (
            dot_nt(queries, grad_scores) * scale
        ).astype(BF16)
        grad_qkv_ref[latent, 2 * width + low : 2 * width + high, :] = dot_nt(
            grad_out, probs
        ).astype(BF16)

    items = [(latent, head) for latent in range(latents) for head in range(width // HEAD_DIM)]
    groups = in_groups(items, GROUP)
    values = [products(*item) for item in groups[0]]
    previous = []
    for place, group in enumerate(groups):
        later = groups[place + 1] if place + 1 < len(groups) else []
        next_values = [products(*item) for item in later]
        middles = [middle_of(*item, *value) for item, value in zip(group, values)]
        for item, value in previous:
            finish(*item, *value)
        previous = list(zip(group, middles))
        values = next_values
    for item, value in previous:
        finish(*item, *value)

    grad_qkv = beside(*[grad_qkv_ref[latent] for latent in range(latents)])
    normed = normed_ref[...].reshape(latents * length, width)
    grad_normed_wide = dot_nn(weight_back[...], grad_qkv)
    acc[...] += dot_nn(grad_qkv, beside(normed, jnp.ones((latents * length, 128), BF16)))
    for latent in range(latents):
        grad_normed_tall = grad_normed_wide[:, latent * length : (latent + 1) * length].T
        scale_one = 1.0 + mod_ref[latent, 1:2, :]
        first = jnp.zeros((1, width), F32)
        second = jnp.zeros((1, width), F32)
        for rows in strips(length, STRIP):
            normal, inverse = normalise(tokens_ref[latent, rows, :].astype(F32))
            grad_normed = grad_normed_tall[rows]
            first += jnp.sum(grad_normed, axis=0, keepdims=True)
            second += jnp.sum(grad_normed * normal, axis=0, keepdims=True)
            back = normalise_back(grad_normed * scale_one, normal, inverse)
            tokens_grad_ref[latent, rows, :] = (grad_middle_ref[latent, rows, :] + back).astype(
                BF16
            )
        grad_mod_ref[latent] = above(first, second)

    @pl.when(step == pl.num_programs(0) - 1)
    def _():
        n_dp, tail_rows, _ = kept_ref.shape
        half_rows = 3 * width // (2 * n_dp)
        for side in range(2):

            def write(ref, side=side):
                for owner in range(n_dp):
                    low = (2 * owner + side) * half_rows
                    rows = acc[low : low + half_rows, :width]
                    rest = jnp.zeros((tail_rows - half_rows, width), F32)
                    ref[owner] = above(rows, rest).astype(BF16)

            by_side(core_ref, side, kept_ref, sent_ref, write)
        bias_grad_ref[...] = acc[:, width:]


def finish_kernel(
    core_ref,
    mine_ref,
    came_ref,
    silu_ref,
    ada_ref,
    ada_bias_ref,
    qkv_ref,
    up_ref,
    down_ref,
    out_ref,
    qv_bias_ref,
    out_bias_ref,
    up_bias_ref,
    down_bias_ref,
    *,
    tail_rows,
):
    first = core_ref[0] == 0
    own = ada_ref.shape[0]
    half_rows = qkv_ref.shape[0] // 2
    up_half, out_rows = up_ref.shape[0] // 2, out_ref.shape[0]
    width = out_ref.shape[1]
    folds = down_ref.shape[1] // width // 2
    out_low = tail_rows + up_half + folds * out_rows
    end = out_low + out_rows // 2
    mine = mine_ref[:end, :].astype(F32)
    came = came_ref[:end, :].astype(F32)
    for side in range(2):
        part = jnp.where(first, mine, came) if side == 0 else jnp.where(first, came, mine)
        qkv_ref[side * half_rows : (side + 1) * half_rows, :] = part[:half_rows]
        up_ref[side * up_half : (side + 1) * up_half, :] = part[tail_rows : tail_rows + up_half]
        for place in range(folds):
            low = tail_rows + up_half + place * out_rows
            columns = (side * folds + place) * width
            down_ref[:, columns : columns + width] = part[low : low + out_rows]
        out_ref[side * (out_rows // 2) : (side + 1) * (out_rows // 2), :] = part[out_low:]
    biases = mine[half_rows : half_rows + 1] + came[half_rows : half_rows + 1]
    low = 0
    for ref in (qv_bias_ref, out_bias_ref, up_bias_ref, down_bias_ref):
        ref[...] = biases[:, low : low + ref.shape[1]]
        low += ref.shape[1]
    mine = mine_ref[end:, :]
    came = came_ref[end:, :]
    columns = above(jnp.where(first, mine, came), jnp.where(first, came, mine))
    ada_ref[...] = dot_tn(columns, silu_ref[...])[:own]
    ada_bias_ref[...] = jnp.sum(columns.astype(F32), axis=0, keepdims=True)[:, :own]


def each(shape, count):
    zeros = (0,) * (len(shape) - 1)
    return pl.BlockSpec((count,) + tuple(shape[1:]), lambda step: (step,) + zeros)


def whole(shape):
    zeros = (0,) * len(shape)
    return pl.BlockSpec(tuple(shape), lambda step: zeros)


def run_kernel(kernel, count, streamed_out, fixed_out, scratch, streamed, fixed, cost, scalars=()):
    return pl.pallas_call(
        kernel,
        grid=(streamed[0].shape[0] // count,),
        in_specs=[pl.BlockSpec(memory_space=pltpu.SMEM)] * len(scalars)
        + [each(item.shape, count) for item in streamed]
        + [whole(item.shape) for item in fixed],
        out_specs=[each(item.shape, count) for item in streamed_out]
        + [whole(item.shape) for item in fixed_out],
        out_shape=list(streamed_out) + list(fixed_out),
        scratch_shapes=scratch,
        compiler_params=pltpu.CompilerParams(
            dimension_semantics=("arbitrary",), vmem_limit_bytes=VMEM_LIMIT
        ),
        cost_estimate=cost,
    )(*scalars, *streamed, *fixed)


def shape_of(dims, kind):
    return jax.ShapeDtypeStruct(tuple(dims), kind)


AXES = ("dp", "rep")


class Hops:
    def __init__(self, n_dp, n_rep):
        self.sizes = {"dp": n_dp, "rep": n_rep}
        self.place = {name: lax.axis_index(name) for name in AXES}

    def bits(self, name):
        return [1 << shift for shift in range(self.sizes[name].bit_length() - 1)]

    def mine(self, name, bit):
        return (self.place[name] // bit) % 2

    def swap(self, value, name, bit):
        n_dp, n_rep = self.sizes["dp"], self.sizes["rep"]
        flip_dp, flip_rep = (bit, 0) if name == "dp" else (0, bit)
        pairs = [
            (d * n_rep + r, (d ^ flip_dp) * n_rep + (r ^ flip_rep))
            for d in range(n_dp)
            for r in range(n_rep)
        ]
        return lax.ppermute(value, AXES, pairs)

    def both(self, kept, came, name, bit, axis):
        upper = self.mine(name, bit) == 1
        return jnp.stack(
            [jnp.where(upper, came, kept), jnp.where(upper, kept, came)], axis=axis
        )

    def cut(self, value, name, bit, axis):
        here = self.mine(name, bit)
        return (
            lax.dynamic_index_in_dim(value, here, axis, keepdims=False),
            lax.dynamic_index_in_dim(value, 1 - here, axis, keepdims=False),
        )


def pad_rows(values, count):
    return jnp.pad(values, ((0, 0),) * (values.ndim - 2) + ((0, count - values.shape[-2]), (0, 0)))


def up_to(count, multiple):
    return -(-count // multiple) * multiple


def body(
    n_dp,
    n_rep,
    tokens,
    conditioning,
    ada_weight,
    ada_bias,
    qkv_weight,
    qv_bias,
    out_weight,
    out_bias,
    up_weight,
    up_bias,
    down_weight,
    down_bias,
    cotangent,
):
    latents, length, width = tokens.shape
    hidden_width = up_weight.shape[1] * n_dp
    heads = width // HEAD_DIM
    rows = latents * length
    hops = Hops(n_dp, n_rep)
    dp_bits = hops.bits("dp")
    folds = hidden_width // width

    up_rows, out_rows = up_weight.shape[1], out_weight.shape[1]
    down_shard = down_weight.T.reshape(out_rows, folds, width).transpose(1, 0, 2)
    late_shard = jnp.concatenate(
        [up_weight.T, down_shard.reshape(folds * out_rows, width), out_weight.T]
    )
    silu_low = jax.nn.silu(conditioning).astype(BF16)
    qkv_rows = qkv_weight.shape[1]
    half_rows = qkv_rows // 2
    core = hops.mine("rep", 1)
    bias_shard = jnp.concatenate([qv_bias, out_bias, up_bias, down_bias])
    bias_rows = 2
    front = jnp.concatenate(
        [
            lax.dynamic_slice_in_dim(qkv_weight.T, core * half_rows, half_rows, axis=0),
            silu_low,
            jnp.pad(bias_shard, (0, width - bias_shard.shape[0]))[None],
            jnp.pad(ada_bias, (0, width - ada_bias.shape[0]))[None],
        ]
    )
    front = pad_rows(front, up_to(front.shape[0], 8))
    front, late_shard = lax.optimization_barrier((front, late_shard))
    late = lax.all_gather(late_shard, "dp", axis=0)
    ada_shard, _ = lax.optimization_barrier((ada_weight.T, late))
    ada_all = lax.all_gather(ada_shard, "dp", axis=0, tiled=True)
    ada_pair = hops.both(ada_weight.T, hops.swap(ada_weight.T, "dp", 1), "dp", 1, 0)
    high_bits = dp_bits[:0:-1]
    for done, bit in enumerate(high_bits):
        front = hops.both(front, hops.swap(front, "dp", bit), "dp", bit, done)

    silu_part = front[..., half_rows : half_rows + latents, :].reshape(-1, width)
    mod = dot_nt(silu_part, ada_pair.reshape(-1, width))
    mod = mod.reshape((2,) * len(high_bits) + (latents, -1))
    for done, bit in enumerate(high_bits):
        kept, sent = hops.cut(mod, "dp", bit, done)
        mod = hops.both(kept, hops.swap(sent, "dp", bit), "dp", bit, done)
    mod = mod.reshape(n_dp // 2, latents, -1).transpose(1, 0, 2).reshape(latents, -1)

    front = hops.both(front, hops.swap(front, "dp", 1), "dp", 1, len(high_bits))
    front = front.reshape(n_dp, -1, width)
    mine = front[:, : half_rows + latents]
    came = hops.swap(mine, "rep", 1)
    silu_all = hops.both(mine[:, half_rows:], came[:, half_rows:], "rep", 1, 0)
    for bit in hops.bits("rep")[1:]:
        silu_all = hops.both(silu_all, hops.swap(silu_all, "rep", bit), "rep", bit, 0)
    silu_all = silu_all.reshape(n_rep // 2, 2, n_dp * latents, width).transpose(1, 0, 2, 3)
    silu_all = silu_all.reshape(-1, width)

    bias_all = front[:, half_rows + latents].astype(F32)
    cuts = [0]
    for part in (qv_bias, out_bias, up_bias, down_bias):
        cuts.append(cuts[-1] + part.shape[0])
    bias_all = bias_all[:, : cuts[-1]]
    qv_full = bias_all[:, : cuts[1]].reshape(1, -1)
    ada_full = front[:, half_rows + latents + 1, : ada_bias.shape[0]].astype(F32).reshape(1, -1)
    qkv_bias = jnp.concatenate(
        [qv_full[:, :width], jnp.zeros((1, width), F32), qv_full[:, width:]], axis=1
    )

    modulation = (mod + ada_full).reshape(latents, 6, width)

    core_scalar = core.astype(jnp.int32).reshape(1)
    normed, qkv, lse, attended, qkv_full = run_kernel(
        attention_forward_kernel,
        4,
        [
            shape_of((latents, length, width), BF16),
            shape_of((latents, 3 * width, length), BF16),
            shape_of((latents, 8 * ((heads + 7) // 8), length), F32),
            shape_of((latents, width, length), BF16),
        ],
        [shape_of((3 * width, width), BF16)],
        [pltpu.VMEM((3 * width, 128), F32)],
        [tokens, modulation],
        [mine, came, qkv_bias],
        pl.CostEstimate(
            flops=2 * rows * width * (3 * width + 2 * length),
            bytes_accessed=rows * width * 12,
            transcendentals=rows * heads * length,
        ),
        [core_scalar],
    )

    attended, silu_all = lax.optimization_barrier((attended, silu_all))
    (
        output,
        grad_middle,
        grad_attended,
        grad_mod_two,
        late_kept,
        late_sent,
        out_bias_grad,
        up_bias_grad,
        down_bias_grad,
    ) = run_kernel(
        functools.partial(feed_kernel, chunk=256),
        4,
        [
            shape_of((latents, length, width), BF16),
            shape_of((latents, length, width), F32),
            shape_of((latents, width, length), BF16),
            shape_of((latents, 4, width), F32),
        ],
        [
            shape_of((n_dp, late.shape[1] // 2, width), BF16),
            shape_of((n_dp, late.shape[1] // 2, width), BF16),
            shape_of((1, width), F32),
            shape_of((hidden_width, 128), F32),
            shape_of((1, width), F32),
        ],
        [
            pltpu.VMEM((width, width), F32),
            pltpu.VMEM((hidden_width, width + 128), F32),
            pltpu.VMEM((hidden_width, width), F32),
            pltpu.VMEM((8, width), F32),
            pltpu.VMEM((width, width), BF16),
            pltpu.VMEM((hidden_width, width), BF16),
            pltpu.VMEM((width, hidden_width), BF16),
            pltpu.VMEM((hidden_width, 128), F32),
            pltpu.VMEM((1, width), F32),
            pltpu.VMEM((1, width), F32),
            pltpu.VMEM((1, hidden_width), F32),
            pltpu.VMEM((width, width), BF16),
            pltpu.VMEM((width, hidden_width), BF16),
            pltpu.VMEM((hidden_width, width), BF16),
            pltpu.VMEM((hidden_width, 4 * length), BF16),
            pltpu.VMEM((hidden_width, 4 * length), BF16),
            pltpu.VMEM((4 * length, width), F32),
            pltpu.VMEM((4 * length, width), F32),
            pltpu.VMEM((4 * length, width), F32),
        ],
        [tokens, cotangent, attended, modulation],
        [late, bias_all],
        pl.CostEstimate(
            flops=6 * rows * width * (width + 2 * hidden_width),
            bytes_accessed=rows * width * 14,
            transcendentals=rows * hidden_width,
        ),
        [core_scalar],
    )

    late_sent, ada_all = lax.optimization_barrier((late_sent, ada_all))
    late_half = late_kept.astype(F32) + hops.swap(late_sent, "rep", 1).astype(F32)
    late_half = late_half.astype(BF16)
    late_parts = lax.all_to_all(late_half, "dp", 0, 0, tiled=True)

    normed, _ = lax.optimization_barrier((normed, late_half))
    tail_rows = up_to(half_rows + 1, 8)
    tokens_grad, grad_mod_one, qkv_kept, qkv_sent, qkv_bias_grad = run_kernel(
        attention_backward_kernel,
        2,
        [shape_of((latents, length, width), BF16), shape_of((latents, 2, width), F32)],
        [
            shape_of((n_dp, tail_rows, width), BF16),
            shape_of((n_dp, tail_rows, width), BF16),
            shape_of((3 * width, 128), F32),
        ],
        [
            pltpu.VMEM((3 * width, width + 128), F32),
            pltpu.VMEM((width, 3 * width), BF16),
            pltpu.VMEM((2, 3 * width, length), BF16),
        ],
        [qkv, lse, grad_attended, normed, tokens, grad_middle, modulation],
        [qkv_full],
        pl.CostEstimate(flops=1, bytes_accessed=1, transcendentals=0),
        [core_scalar],
    )
    qkv_sent, late_parts = lax.optimization_barrier((qkv_sent, late_parts))
    late_sum = jnp.sum(late_parts.astype(F32), axis=0).astype(BF16)
    for bit in hops.bits("rep")[1:]:
        late_sum = late_sum.astype(F32) + hops.swap(late_sum, "rep", bit).astype(F32)
        late_sum = late_sum.astype(BF16)

    qkv_columns = qkv_bias_grad[:, 0]
    bias_blocks = jnp.concatenate(
        [
            jnp.concatenate([qkv_columns[:width], qkv_columns[2 * width :]]).reshape(n_dp, -1),
            out_bias_grad.reshape(n_dp, -1),
            up_bias_grad[:, 0].reshape(n_dp, -1),
            down_bias_grad.reshape(n_dp, -1),
        ],
        axis=1,
    )
    bias_blocks = jnp.pad(
        bias_blocks[:, None],
        ((0, 0), (half_rows, tail_rows - half_rows - 1), (0, width - cuts[-1])),
    )
    total = qkv_kept.astype(F32) + hops.swap(qkv_sent, "rep", 1).astype(F32) + bias_blocks

    grad_modulation = jnp.concatenate([grad_mod_one, grad_mod_two], axis=1).reshape(
        latents, 6 * width
    )

    own = 6 * width // n_dp
    columns = grad_modulation.reshape(latents, n_dp, own).transpose(1, 0, 2).astype(BF16)
    columns = jnp.pad(columns, ((0, 0), (0, 0), (0, up_to(own, width) - own)))
    columns = columns.reshape((2,) * len(dp_bits) + (latents, width))
    total = total.reshape((2,) * len(dp_bits) + (tail_rows, width))
    axis = len(dp_bits) - 1
    for bit in dp_bits:
        kept, sent = hops.cut(total, "dp", bit, axis)
        column_kept, column_sent = hops.cut(columns, "dp", bit, axis)
        lead = sent.shape[:axis]
        sources = column_sent.shape[axis:-2]
        came = hops.swap(
            jnp.concatenate(
                [sent.astype(BF16), column_sent.reshape(lead + (-1, width))], axis=-2
            ),
            "dp",
            bit,
        )
        total = kept.astype(F32) + came[..., :tail_rows, :].astype(F32)
        column_came = came[..., tail_rows:, :].reshape(lead + sources + (latents, width))
        columns = hops.both(column_kept, column_came, "dp", bit, axis)
        axis -= 1
    columns = columns.reshape(n_dp * latents, width)

    qkv_total = total.astype(BF16)
    for bit in hops.bits("rep")[1:]:
        came = hops.swap(jnp.concatenate([qkv_total, columns]), "rep", bit)
        qkv_total = (qkv_total.astype(F32) + came[:tail_rows].astype(F32)).astype(BF16)
        columns = hops.both(columns, came[tail_rows:], "rep", bit, 0).reshape(-1, width)
    mine = jnp.concatenate([qkv_total, late_sum, columns])
    came = hops.swap(mine, "rep", 1)
    smem = pl.BlockSpec(memory_space=pltpu.SMEM)
    vmem = pl.BlockSpec(memory_space=pltpu.VMEM)
    ada_grad, ada_bias_grad, qkv_owned, up_owned, down_owned, out_owned, *bias_sums = pl.pallas_call(
        functools.partial(finish_kernel, tail_rows=tail_rows),
        in_specs=[smem, vmem, vmem, vmem],
        out_specs=[vmem] * 10,
        out_shape=[
            shape_of((own, width), F32),
            shape_of((1, own), F32),
            shape_of((qkv_rows, width), F32),
            shape_of((up_rows, width), F32),
            shape_of((out_rows, hidden_width), F32),
            shape_of((out_rows, width), F32),
        ]
        + [shape_of((1, part.shape[0]), F32) for part in (qv_bias, out_bias, up_bias, down_bias)],
        compiler_params=pltpu.CompilerParams(vmem_limit_bytes=VMEM_LIMIT),
    )(core_scalar, mine, came, silu_all)
    ada_bias_grad = ada_bias_grad.reshape(-1)

    grad_silu = lax.dot_general(
        grad_modulation,
        ada_all.astype(F32),
        (((1,), (0,)), ((), ())),
        precision=lax.Precision.HIGHEST,
    )
    _, silu_pull = jax.vjp(jax.nn.silu, conditioning)
    condition_grad = silu_pull(grad_silu)[0]

    qv_sum, out_bias_sum, up_bias_sum, down_bias_sum = (part.reshape(-1) for part in bias_sums)
    return (
        output,
        tokens_grad,
        condition_grad,
        ada_grad.T,
        ada_bias_grad,
        qkv_owned.T,
        qv_sum,
        out_owned.T,
        out_bias_sum,
        up_owned.T,
        up_bias_sum,
        down_owned.T,
        down_bias_sum,
    )


def solution(mesh):
    return jax.shard_map(
        functools.partial(body, mesh.shape["dp"], mesh.shape["rep"]),
        mesh=mesh,
        in_specs=(
            P(("dp", "rep"), None, None),
            P(("dp", "rep"), None),
            P(None, "dp"),
            P("dp"),
            P(None, "dp"),
            P("dp"),
            P(None, "dp"),
            P("dp"),
            P(None, "dp"),
            P("dp"),
            P(None, "dp"),
            P("dp"),
            P(("dp", "rep"), None, None),
        ),
        out_specs=(
            P(("dp", "rep"), None, None),
            P(("dp", "rep"), None, None),
            P(("dp", "rep"), None),
            P(None, "dp"),
            P("dp"),
            P(None, "dp"),
            P("dp"),
            P(None, "dp"),
            P("dp"),
            P(None, "dp"),
            P("dp"),
            P(None, "dp"),
            P("dp"),
        ),
        check_vma=False,
    )
```

```python
import functools

import jax
import jax.numpy as jnp
from jax import lax
from jax.experimental import pallas as pl
from jax.experimental.pallas import tpu as pltpu
from jax.sharding import PartitionSpec as P

HEAD_DIM = 64
EPS = 1e-06
GELU_C = 0.7978845608028654
VMEM_LIMIT = 56 * 1024 * 1024
F32 = jnp.float32
BF16 = jnp.bfloat16


def dot_nn(left, right):
    return lax.dot_general(left, right, (((1,), (0,)), ((), ())), preferred_element_type=F32)


def dot_nt(left, right):
    return lax.dot_general(left, right, (((1,), (1,)), ((), ())), preferred_element_type=F32)


def dot_tn(left, right):
    return lax.dot_general(left, right, (((0,), (0,)), ((), ())), preferred_element_type=F32)


def normalise(values):
    average = jnp.mean(values, axis=-1, keepdims=True)
    centred = values - average
    spread = jnp.mean(centred * centred, axis=-1, keepdims=True)
    inverse = lax.rsqrt(spread + EPS)
    return centred * inverse, inverse


def normalise_back(upstream, normal, inverse):
    first = jnp.mean(upstream, axis=-1, keepdims=True)
    second = jnp.mean(upstream * normal, axis=-1, keepdims=True)
    return inverse * (upstream - first - normal * second)


STRIP = 32
GROUP = 3


def beside(*parts):
    return jnp.concatenate(parts, axis=1)


def above(*parts):
    return jnp.concatenate(parts, axis=0)


def strips(extent, size):
    return [slice(low, low + size) for low in range(0, extent, size)]


def head_slices(head):
    low = head * HEAD_DIM
    pair = low - low % (2 * HEAD_DIM)
    return slice(low, low + HEAD_DIM), slice(pair, pair + 2 * HEAD_DIM), low == pair


def interleave(first, second):
    done = 0
    for place, call in enumerate(first):
        call()
        until = (place + 1) * len(second) // len(first)
        for other in second[done:until]:
            other()
        done = until


def in_groups(items, size):
    return [items[low : low + size] for low in range(0, len(items), size)]


def attention_forward_kernel(
    core_ref,
    tokens_ref,
    mod_ref,
    mine_ref,
    came_ref,
    bias_row_ref,
    normed_ref,
    qkv_ref,
    lse_ref,
    attended_ref,
    weight_ref,
    bias_ref,
):
    latents, length, width = tokens_ref.shape
    blank = jnp.zeros((HEAD_DIM, length), BF16)

    @pl.when(pl.program_id(0) == 0)
    def _():
        first = core_ref[0] == 0
        n_dp = mine_ref.shape[0]
        half_rows = weight_ref.shape[0] // (2 * n_dp)
        for owner in range(n_dp):
            mine = mine_ref[owner, :half_rows, :]
            came = came_ref[owner, :half_rows, :]
            low = 2 * owner * half_rows
            weight_ref[low : low + half_rows, :] = jnp.where(first, mine, came)
            weight_ref[low + half_rows : low + 2 * half_rows, :] = jnp.where(first, came, mine)
        bias_ref[...] = jnp.broadcast_to(bias_row_ref[...], (128, 3 * width)).T


    def norm(latent, rows):
        normal, _ = normalise(tokens_ref[latent, rows, :].astype(F32))
        normed = normal * (1.0 + mod_ref[latent, 1:2, :]) + mod_ref[latent, 0:1, :]
        normed_ref[latent, rows, :] = normed.astype(BF16)

    def project(batch, part):
        normed = normed_ref[batch, :, :].reshape(-1, width)
        bias = bias_ref[part, :]
        qkv = dot_nt(weight_ref[part, :], normed) + beside(*([bias] * (normed.shape[0] // 128)))
        qkv = qkv.astype(BF16)
        for place, latent in enumerate(range(batch.start, batch.stop)):
            qkv_ref[latent, part, :] = qkv[:, place * length : (place + 1) * length]

    def norms(batch):
        return [
            functools.partial(norm, latent, rows)
            for latent in range(batch.start, batch.stop)
            for rows in strips(length, STRIP)
        ]

    def projections(batch):
        return [
            functools.partial(project, batch, part) for part in strips(3 * width, width)
        ]

    batches = strips(latents, 2)
    for call in norms(batches[0]):
        call()
    for batch, later in zip(batches[:-1], batches[1:]):
        interleave(projections(batch), norms(later))
    for call in projections(batches[-1]):
        call()
    keys_all = [qkv_ref[latent, width : 2 * width, :].T for latent in range(latents)]

    def scores_of(latent, head):
        own, pair, first = head_slices(head)
        queries = qkv_ref[latent, own, :]
        queries = above(queries, blank) if first else above(blank, queries)
        return dot_nn(keys_all[latent][:, pair], queries)

    def probs_of(latent, head, scores):
        parts = []
        for columns in strips(length, 128):
            strip = scores[:, columns] * HEAD_DIM ** (-0.5)
            highest = jnp.max(strip, axis=0, keepdims=True)
            shifted = jnp.exp(strip - highest)
            total = jnp.sum(shifted, axis=0, keepdims=True)
            parts.append((shifted * (1.0 / total)).astype(BF16))
            lse_ref[latent, head : head + 1, columns] = highest + jnp.log(total)
        return beside(*parts)

    def attend(latent, head, probs):
        own, _, _ = head_slices(head)
        values_in = qkv_ref[latent, 2 * width + own.start : 2 * width + own.stop, :]
        attended_ref[latent, own, :] = dot_nn(values_in, probs).astype(BF16)

    items = [(latent, head) for latent in range(latents) for head in range(width // HEAD_DIM)]
    groups = in_groups(items, GROUP)
    scores = [scores_of(*item) for item in groups[0]]
    previous = []
    for place, group in enumerate(groups):
        later = groups[place + 1] if place + 1 < len(groups) else []
        next_scores = [scores_of(*item) for item in later]
        probs = [probs_of(*item, value) for item, value in zip(group, scores)]
        for item, value in previous:
            attend(*item, value)
        previous = list(zip(group, probs))
        scores = next_scores
    for item, value in previous:
        attend(*item, value)


def by_side(core_ref, side, kept_ref, sent_ref, write):
    @pl.when(core_ref[0] == side)
    def _():
        write(kept_ref)

    @pl.when(core_ref[0] != side)
    def _():
        write(sent_ref)


def feed_kernel(
    core_ref,
    tokens_ref,
    cotangent_ref,
    attended_ref,
    mod_ref,
    late_ref,
    biases_ref,
    output_ref,
    grad_middle_ref,
    grad_attended_ref,
    grad_mod_ref,
    late_kept_ref,
    late_sent_ref,
    out_bias_grad_ref,
    up_bias_grad_ref,
    down_bias_grad_ref,
    out_acc,
    up_acc,
    down_acc,
    bias_acc,
    out_weight_ref,
    up_weight_ref,
    down_weight_ref,
    up_bias_ref,
    out_bias_ref,
    down_bias_ref,
    up_bias_row_ref,
    out_back,
    up_back,
    down_back,
    active_all,
    grad_hidden_all,
    middle_all,
    normal_all,
    branch_all,
    *,
    chunk,
):
    step = pl.program_id(0)
    n_dp = late_ref.shape[0]
    latents, length, width = tokens_ref.shape
    hidden_width = up_weight_ref.shape[0]
    tokens_all = latents * length
    up_rows, out_rows = hidden_width // n_dp, width // n_dp
    out_low = up_rows + out_rows * (hidden_width // width)

    @pl.when(step == 0)
    def _():
        out_acc[...] = jnp.zeros_like(out_acc)
        up_acc[...] = jnp.zeros_like(up_acc)
        down_acc[...] = jnp.zeros_like(down_acc)
        bias_acc[...] = jnp.zeros_like(bias_acc)
        for owner in range(n_dp):
            up_weight_ref[owner * up_rows : (owner + 1) * up_rows, :] = late_ref[owner, :up_rows, :]
            outs = slice(owner * out_rows, (owner + 1) * out_rows)
            for fold in range(hidden_width // width):
                low = up_rows + fold * out_rows
                down_weight_ref[outs, fold * width : (fold + 1) * width] = late_ref[
                    owner, low : low + out_rows, :
                ]
            out_weight_ref[outs, :] = late_ref[owner, out_low:, :]
        out_back[...] = out_weight_ref[...].T
        up_back[...] = up_weight_ref[...].T
        down_back[...] = down_weight_ref[...].T
        low = biases_ref.shape[1] - 2 * out_rows - up_rows
        for ref, size in ((out_bias_ref, out_rows), (up_bias_row_ref, up_rows), (down_bias_ref, out_rows)):
            for owner in range(n_dp):
                ref[0:1, owner * size : (owner + 1) * size] = biases_ref[
                    owner : owner + 1, low : low + size
                ]
            low += size
        up_bias_ref[...] = jnp.broadcast_to(up_bias_row_ref[...], (128, hidden_width)).T

    attended = beside(*[attended_ref[latent] for latent in range(latents)])
    branch_wide = dot_nn(out_weight_ref[...], attended)
    normed_parts = []
    grad_feed_parts = []
    inverses = []
    down_sum = jnp.zeros((1, width), F32)
    for latent in range(latents):
        gate_one = mod_ref[latent, 2:3, :]
        shift_two = mod_ref[latent, 3:4, :]
        scale_two = 1.0 + mod_ref[latent, 4:5, :]
        gate_two = mod_ref[latent, 5:6, :]
        branch_tall = branch_wide[:, latent * length : (latent + 1) * length].T
        for rows in strips(length, STRIP):
            there = slice(latent * length + rows.start, latent * length + rows.stop)
            branch = branch_tall[rows] + out_bias_ref[...]
            branch_all[there, :] = branch
            middle = tokens_ref[latent, rows, :].astype(F32) + gate_one * branch
            middle_all[there, :] = middle
            normal, inverse = normalise(middle)
            normal_all[there, :] = normal
            inverses.append(inverse)
            normed_parts.append((normal * scale_two + shift_two).astype(BF16))
            grad_feed = (cotangent_ref[latent, rows, :].astype(F32) * gate_two).astype(BF16)
            grad_feed_parts.append(grad_feed)
            down_sum += jnp.sum(grad_feed.astype(F32), axis=0, keepdims=True)
    bias_acc[0:1, :] += down_sum
    normed_all = above(*normed_parts)
    grad_feed_all = above(*grad_feed_parts)

    def products(rows):
        return (
            dot_nt(up_weight_ref[rows, :], normed_all),
            dot_nt(down_back[rows, :], grad_feed_all),
        )

    parts = strips(hidden_width, chunk)
    ahead = products(parts[0])
    for place, part in enumerate(parts):
        hidden_wide, grad_wide = ahead
        if place + 1 < len(parts):
            ahead = products(parts[place + 1])
        for rows in strips(chunk, STRIP):
            there = slice(part.start + rows.start, part.start + rows.stop)
            bias = up_bias_ref[there, :]
            bias = beside(bias, bias)
            for columns in strips(tokens_all, 256):
                hidden = hidden_wide[rows, columns] + bias
                square = hidden * hidden
                bent = jnp.tanh(hidden * (GELU_C + (GELU_C * 0.044715) * square))
                half = 0.5 + 0.5 * bent
                active_all[there, columns] = (hidden * half).astype(BF16)
                slope = half + hidden * (0.5 - 0.5 * (bent * bent)) * (
                    GELU_C + (3.0 * GELU_C * 0.044715) * square
                )
                grad_hidden_all[there, columns] = (grad_wide[rows, columns] * slope).astype(BF16)

    feed_wide = dot_nn(down_weight_ref[...], active_all[...])
    grad_normed_wide = dot_nn(up_back[...], grad_hidden_all[...])
    ones = jnp.ones((tokens_all, 128), BF16)
    normed_ones = beside(normed_all, ones)

    def up_product(part):
        up_acc[part, :] += dot_nn(grad_hidden_all[part, :], normed_ones)

    def down_product(part):
        down_acc[part, :] += dot_nn(active_all[part, :], grad_feed_all)

    products_left = [functools.partial(up_product, part) for part in strips(hidden_width, chunk)]
    products_left += [functools.partial(down_product, part) for part in strips(hidden_width, chunk)]
    share = -(-len(products_left) // latents)
    grad_branch_parts = []
    out_sum = jnp.zeros((1, width), F32)
    for latent in range(latents):
        gate_one = mod_ref[latent, 2:3, :]
        scale_two = 1.0 + mod_ref[latent, 4:5, :]
        gate_two = mod_ref[latent, 5:6, :]
        here = slice(latent * length, (latent + 1) * length)
        feed_tall = feed_wide[:, here].T
        grad_normed_tall = grad_normed_wide[:, here].T
        sums = [jnp.zeros((1, width), F32) for _ in range(4)]
        branch_parts = []
        out_sums = []

        def finish_rows(rows):
            there = slice(here.start + rows.start, here.start + rows.stop)
            feed = feed_tall[rows] + down_bias_ref[...]
            grad_normed = grad_normed_tall[rows]
            incoming = cotangent_ref[latent, rows, :].astype(F32)
            normal = normal_all[there, :]
            output_ref[latent, rows, :] = (middle_all[there, :] + gate_two * feed).astype(BF16)
            grad_middle = incoming + normalise_back(
                grad_normed * scale_two, normal, inverses[there.start // STRIP]
            )
            grad_middle_ref[latent, rows, :] = grad_middle
            grad_branch = (grad_middle * gate_one).astype(BF16)
            branch_parts.append(grad_branch)
            terms = (
                grad_middle * branch_all[there, :],
                grad_normed,
                grad_normed * normal,
                incoming * feed,
            )
            for place, term in enumerate(terms):
                sums[place] += jnp.sum(term, axis=0, keepdims=True)
            out_sums.append(jnp.sum(grad_branch.astype(F32), axis=0, keepdims=True))

        interleave(
            [functools.partial(finish_rows, rows) for rows in strips(length, STRIP)],
            products_left[latent * share : (latent + 1) * share],
        )
        grad_branch_parts += branch_parts
        for value in out_sums:
            out_sum += value
        grad_mod_ref[latent] = above(*sums)
    bias_acc[1:2, :] += out_sum
    grad_branch_all = above(*grad_branch_parts)
    grad_attended = dot_nt(out_back[...], grad_branch_all).astype(BF16)
    for latent in range(latents):
        grad_attended_ref[latent] = grad_attended[:, latent * length : (latent + 1) * length]
    out_acc[...] += dot_nn(attended, grad_branch_all)

    @pl.when(step == pl.num_programs(0) - 1)
    def _():
        out_acc[...] = out_acc[...].T
        up_back[...] = down_acc[...].T.astype(BF16)
        folds = hidden_width // width // 2
        out_back_rows = out_rows // 2
        for side in range(2):

            def write(ref, side=side):
                for owner in range(n_dp):
                    ups = owner * up_rows + side * (up_rows // 2)
                    ref[owner, : up_rows // 2, :] = up_acc[
                        ups : ups + up_rows // 2, :width
                    ].astype(BF16)
                    outs = slice(owner * out_rows, (owner + 1) * out_rows)
                    for place in range(folds):
                        low = up_rows // 2 + place * out_rows
                        fold = side * folds + place
                        ref[owner, low : low + out_rows, :] = up_back[
                            outs, fold * width : (fold + 1) * width
                        ]
                    outs = owner * out_rows + side * out_back_rows
                    ref[owner, out_low // 2 :, :] = out_acc[
                        outs : outs + out_back_rows
                    ].astype(BF16)

            by_side(core_ref, side, late_kept_ref, late_sent_ref, write)
        up_bias_grad_ref[...] = up_acc[:, width:].T[0:1, :]
        down_bias_grad_ref[...] = bias_acc[0:1, :]
        out_bias_grad_ref[...] = bias_acc[1:2, :]


def attention_backward_kernel(
    core_ref,
    qkv_ref,
    lse_ref,
    grad_attended_ref,
    normed_ref,
    tokens_ref,
    grad_middle_ref,
    mod_ref,
    weight_ref,
    tokens_grad_ref,
    grad_mod_ref,
    kept_ref,
    sent_ref,
    bias_grad_ref,
    acc,
    weight_back,
    grad_qkv_ref,
):
    step = pl.program_id(0)
    latents, length, width = normed_ref.shape
    blank = jnp.zeros((HEAD_DIM, length), BF16)

    @pl.when(step == 0)
    def _():
        acc[...] = jnp.zeros_like(acc)
        weight_back[...] = weight_ref[...].T

    keys_all = [qkv_ref[latent, width : 2 * width, :].T for latent in range(latents)]
    values_all = [qkv_ref[latent, 2 * width : 3 * width, :].T for latent in range(latents)]

    def products(latent, head):
        own, pair, first = head_slices(head)
        queries = qkv_ref[latent, own, :]
        grad_out = grad_attended_ref[latent, own, :]
        queries = above(queries, blank) if first else above(blank, queries)
        grad_out = above(grad_out, blank) if first else above(blank, grad_out)
        return (
            dot_nn(keys_all[latent][:, pair], queries),
            dot_nn(values_all[latent][:, pair], grad_out),
        )

    def middle_of(latent, head, scores, grad_probs):
        low_parts = []
        grad_parts = []
        for columns in strips(length, 128):
            total = lse_ref[latent, head : head + 1, columns]
            probs = jnp.exp(scores[:, columns] * HEAD_DIM ** (-0.5) - total)
            terms = probs * grad_probs[:, columns]
            row_terms = jnp.sum(terms, axis=0, keepdims=True)
            grad_parts.append((probs * (grad_probs[:, columns] - row_terms)).astype(BF16))
            low_parts.append(probs.astype(BF16))
        return beside(*low_parts), beside(*grad_parts)

    def finish(latent, head, probs, grad_scores):
        own, _, _ = head_slices(head)
        low, high = own.start, own.stop
        queries = qkv_ref[latent, own, :]
        keys_in = qkv_ref[latent, width + low : width + high, :]
        grad_out = grad_attended_ref[latent, own, :]
        scale = HEAD_DIM ** (-0.5)
        grad_qkv_ref[latent, own, :] = (dot_nn(keys_in, grad_scores) * scale).astype(BF16)
        grad_qkv_ref[latent, width + low : width + high, :] = (
            dot_nt(queries, grad_scores) * scale
        ).astype(BF16)
        grad_qkv_ref[latent, 2 * width + low : 2 * width + high, :] = dot_nt(
            grad_out, probs
        ).astype(BF16)

    items = [(latent, head) for latent in range(latents) for head in range(width // HEAD_DIM)]
    groups = in_groups(items, GROUP)
    values = [products(*item) for item in groups[0]]
    previous = []
    for place, group in enumerate(groups):
        later = groups[place + 1] if place + 1 < len(groups) else []
        next_values = [products(*item) for item in later]
        middles = [middle_of(*item, *value) for item, value in zip(group, values)]
        for item, value in previous:
            finish(*item, *value)
        previous = list(zip(group, middles))
        values = next_values
    for item, value in previous:
        finish(*item, *value)

    grad_qkv = beside(*[grad_qkv_ref[latent] for latent in range(latents)])
    normed = normed_ref[...].reshape(latents * length, width)
    grad_normed_wide = dot_nn(weight_back[...], grad_qkv)
    normed_ones = beside(normed, jnp.ones((latents * length, 128), BF16))

    def product(part):
        acc[part, :] += dot_nn(grad_qkv[part, :], normed_ones)

    products_left = [functools.partial(product, part) for part in strips(3 * width, 3 * width // 2)]
    share = -(-len(products_left) // latents)
    for latent in range(latents):
        grad_normed_tall = grad_normed_wide[:, latent * length : (latent + 1) * length].T
        scale_one = 1.0 + mod_ref[latent, 1:2, :]
        sums = [jnp.zeros((1, width), F32) for _ in range(2)]

        def finish_rows(rows):
            normal, inverse = normalise(tokens_ref[latent, rows, :].astype(F32))
            grad_normed = grad_normed_tall[rows]
            sums[0] += jnp.sum(grad_normed, axis=0, keepdims=True)
            sums[1] += jnp.sum(grad_normed * normal, axis=0, keepdims=True)
            back = normalise_back(grad_normed * scale_one, normal, inverse)
            tokens_grad_ref[latent, rows, :] = (grad_middle_ref[latent, rows, :] + back).astype(
                BF16
            )

        interleave(
            [functools.partial(finish_rows, rows) for rows in strips(length, STRIP)],
            products_left[latent * share : (latent + 1) * share],
        )
        grad_mod_ref[latent] = above(*sums)

    @pl.when(step == pl.num_programs(0) - 1)
    def _():
        n_dp, tail_rows, _ = kept_ref.shape
        half_rows = 3 * width // (2 * n_dp)
        for side in range(2):

            def write(ref, side=side):
                for owner in range(n_dp):
                    low = (2 * owner + side) * half_rows
                    rows = acc[low : low + half_rows, :width]
                    rest = jnp.zeros((tail_rows - half_rows, width), F32)
                    ref[owner] = above(rows, rest).astype(BF16)

            by_side(core_ref, side, kept_ref, sent_ref, write)
        bias_grad_ref[...] = acc[:, width:].T[0:1, :]


def finish_kernel(
    core_ref,
    mine_ref,
    came_ref,
    silu_ref,
    ada_ref,
    ada_bias_ref,
    qkv_ref,
    up_ref,
    down_ref,
    out_ref,
    qv_bias_ref,
    out_bias_ref,
    up_bias_ref,
    down_bias_ref,
    *,
    tail_rows,
):
    first = core_ref[0] == 0
    own = ada_ref.shape[0]
    half_rows = qkv_ref.shape[0] // 2
    up_half, out_rows = up_ref.shape[0] // 2, out_ref.shape[0]
    width = out_ref.shape[1]
    folds = down_ref.shape[1] // width // 2
    out_low = tail_rows + up_half + folds * out_rows
    end = out_low + out_rows // 2
    mine = mine_ref[:end, :].astype(F32)
    came = came_ref[:end, :].astype(F32)
    for side in range(2):
        part = jnp.where(first, mine, came) if side == 0 else jnp.where(first, came, mine)
        qkv_ref[side * half_rows : (side + 1) * half_rows, :] = part[:half_rows]
        up_ref[side * up_half : (side + 1) * up_half, :] = part[tail_rows : tail_rows + up_half]
        for place in range(folds):
            low = tail_rows + up_half + place * out_rows
            columns = (side * folds + place) * width
            down_ref[:, columns : columns + width] = part[low : low + out_rows]
        out_ref[side * (out_rows // 2) : (side + 1) * (out_rows // 2), :] = part[out_low:]
    biases = mine[half_rows : half_rows + 1] + came[half_rows : half_rows + 1]
    low = 0
    for ref in (qv_bias_ref, out_bias_ref, up_bias_ref, down_bias_ref):
        ref[...] = biases[:, low : low + ref.shape[1]]
        low += ref.shape[1]
    mine = mine_ref[end:, :]
    came = came_ref[end:, :]
    columns = above(jnp.where(first, mine, came), jnp.where(first, came, mine))
    ada_ref[...] = dot_tn(columns, silu_ref[...])[:own]
    ada_bias_ref[...] = jnp.sum(columns.astype(F32), axis=0, keepdims=True)[:, :own]


def each(shape, count):
    zeros = (0,) * (len(shape) - 1)
    return pl.BlockSpec((count,) + tuple(shape[1:]), lambda step: (step,) + zeros)


def whole(shape):
    zeros = (0,) * len(shape)
    return pl.BlockSpec(tuple(shape), lambda step: zeros)


def run_kernel(kernel, count, streamed_out, fixed_out, scratch, streamed, fixed, cost, scalars=()):
    return pl.pallas_call(
        kernel,
        grid=(streamed[0].shape[0] // count,),
        in_specs=[pl.BlockSpec(memory_space=pltpu.SMEM)] * len(scalars)
        + [each(item.shape, count) for item in streamed]
        + [whole(item.shape) for item in fixed],
        out_specs=[each(item.shape, count) for item in streamed_out]
        + [whole(item.shape) for item in fixed_out],
        out_shape=list(streamed_out) + list(fixed_out),
        scratch_shapes=scratch,
        compiler_params=pltpu.CompilerParams(
            dimension_semantics=("arbitrary",), vmem_limit_bytes=VMEM_LIMIT
        ),
        cost_estimate=cost,
    )(*scalars, *streamed, *fixed)


def shape_of(dims, kind):
    return jax.ShapeDtypeStruct(tuple(dims), kind)


AXES = ("dp", "rep")


class Hops:
    def __init__(self, n_dp, n_rep):
        self.sizes = {"dp": n_dp, "rep": n_rep}
        self.place = {name: lax.axis_index(name) for name in AXES}

    def bits(self, name):
        return [1 << shift for shift in range(self.sizes[name].bit_length() - 1)]

    def mine(self, name, bit):
        return (self.place[name] // bit) % 2

    def swap(self, value, name, bit):
        n_dp, n_rep = self.sizes["dp"], self.sizes["rep"]
        flip_dp, flip_rep = (bit, 0) if name == "dp" else (0, bit)
        pairs = [
            (d * n_rep + r, (d ^ flip_dp) * n_rep + (r ^ flip_rep))
            for d in range(n_dp)
            for r in range(n_rep)
        ]
        return lax.ppermute(value, AXES, pairs)

    def both(self, kept, came, name, bit, axis):
        upper = self.mine(name, bit) == 1
        return jnp.stack(
            [jnp.where(upper, came, kept), jnp.where(upper, kept, came)], axis=axis
        )

    def cut(self, value, name, bit, axis):
        here = self.mine(name, bit)
        return (
            lax.dynamic_index_in_dim(value, here, axis, keepdims=False),
            lax.dynamic_index_in_dim(value, 1 - here, axis, keepdims=False),
        )


def pad_rows(values, count):
    return jnp.pad(values, ((0, 0),) * (values.ndim - 2) + ((0, count - values.shape[-2]), (0, 0)))


def up_to(count, multiple):
    return -(-count // multiple) * multiple


def body(
    n_dp,
    n_rep,
    tokens,
    conditioning,
    ada_weight,
    ada_bias,
    qkv_weight,
    qv_bias,
    out_weight,
    out_bias,
    up_weight,
    up_bias,
    down_weight,
    down_bias,
    cotangent,
):
    latents, length, width = tokens.shape
    hidden_width = up_weight.shape[1] * n_dp
    heads = width // HEAD_DIM
    rows = latents * length
    hops = Hops(n_dp, n_rep)
    dp_bits = hops.bits("dp")
    folds = hidden_width // width

    up_rows, out_rows = up_weight.shape[1], out_weight.shape[1]
    down_shard = down_weight.T.reshape(out_rows, folds, width).transpose(1, 0, 2)
    late_shard = jnp.concatenate(
        [up_weight.T, down_shard.reshape(folds * out_rows, width), out_weight.T]
    )
    silu_low = jax.nn.silu(conditioning).astype(BF16)
    qkv_rows = qkv_weight.shape[1]
    half_rows = qkv_rows // 2
    core = hops.mine("rep", 1)
    bias_shard = jnp.concatenate([qv_bias, out_bias, up_bias, down_bias])
    bias_rows = 2
    front = jnp.concatenate(
        [
            lax.dynamic_slice_in_dim(qkv_weight.T, core * half_rows, half_rows, axis=0),
            silu_low,
            jnp.pad(bias_shard, (0, width - bias_shard.shape[0]))[None],
            jnp.pad(ada_bias, (0, width - ada_bias.shape[0]))[None],
        ]
    )
    front = pad_rows(front, up_to(front.shape[0], 8))
    front, late_shard = lax.optimization_barrier((front, late_shard))
    late = lax.all_gather(late_shard, "dp", axis=0)
    ada_shard, _ = lax.optimization_barrier((ada_weight.T, late))
    ada_all = lax.all_gather(ada_shard, "dp", axis=0, tiled=True)
    ada_pair = hops.both(ada_weight.T, hops.swap(ada_weight.T, "dp", 1), "dp", 1, 0)
    high_bits = dp_bits[:0:-1]
    for done, bit in enumerate(high_bits):
        front = hops.both(front, hops.swap(front, "dp", bit), "dp", bit, done)

    silu_part = front[..., half_rows : half_rows + latents, :].reshape(-1, width)
    mod = dot_nt(silu_part, ada_pair.reshape(-1, width))
    mod = mod.reshape((2,) * len(high_bits) + (latents, -1))
    for done, bit in enumerate(high_bits):
        kept, sent = hops.cut(mod, "dp", bit, done)
        mod = hops.both(kept, hops.swap(sent, "dp", bit), "dp", bit, done)
    mod = mod.reshape(n_dp // 2, latents, -1).transpose(1, 0, 2).reshape(latents, -1)

    front = hops.both(front, hops.swap(front, "dp", 1), "dp", 1, len(high_bits))
    front = front.reshape(n_dp, -1, width)
    mine = front[:, : half_rows + latents]
    came = hops.swap(mine, "rep", 1)
    silu_all = hops.both(mine[:, half_rows:], came[:, half_rows:], "rep", 1, 0)
    for bit in hops.bits("rep")[1:]:
        silu_all = hops.both(silu_all, hops.swap(silu_all, "rep", bit), "rep", bit, 0)
    silu_all = silu_all.reshape(n_rep // 2, 2, n_dp * latents, width).transpose(1, 0, 2, 3)
    silu_all = silu_all.reshape(-1, width)

    bias_all = front[:, half_rows + latents].astype(F32)
    cuts = [0]
    for part in (qv_bias, out_bias, up_bias, down_bias):
        cuts.append(cuts[-1] + part.shape[0])
    bias_all = bias_all[:, : cuts[-1]]
    qv_full = bias_all[:, : cuts[1]].reshape(1, -1)
    ada_full = front[:, half_rows + latents + 1, : ada_bias.shape[0]].astype(F32).reshape(1, -1)
    qkv_bias = jnp.concatenate(
        [qv_full[:, :width], jnp.zeros((1, width), F32), qv_full[:, width:]], axis=1
    )

    modulation = (mod + ada_full).reshape(latents, 6, width)

    core_scalar = core.astype(jnp.int32).reshape(1)
    normed, qkv, lse, attended, qkv_full = run_kernel(
        attention_forward_kernel,
        4,
        [
            shape_of((latents, length, width), BF16),
            shape_of((latents, 3 * width, length), BF16),
            shape_of((latents, 8 * ((heads + 7) // 8), length), F32),
            shape_of((latents, width, length), BF16),
        ],
        [shape_of((3 * width, width), BF16)],
        [pltpu.VMEM((3 * width, 128), F32)],
        [tokens, modulation],
        [mine, came, qkv_bias],
        pl.CostEstimate(
            flops=2 * rows * width * (3 * width + 2 * length),
            bytes_accessed=rows * width * 12,
            transcendentals=rows * heads * length,
        ),
        [core_scalar],
    )

    attended, silu_all = lax.optimization_barrier((attended, silu_all))
    (
        output,
        grad_middle,
        grad_attended,
        grad_mod_two,
        late_kept,
        late_sent,
        out_bias_grad,
        up_bias_grad,
        down_bias_grad,
    ) = run_kernel(
        functools.partial(feed_kernel, chunk=768),
        4,
        [
            shape_of((latents, length, width), BF16),
            shape_of((latents, length, width), F32),
            shape_of((latents, width, length), BF16),
            shape_of((latents, 4, width), F32),
        ],
        [
            shape_of((n_dp, late.shape[1] // 2, width), BF16),
            shape_of((n_dp, late.shape[1] // 2, width), BF16),
            shape_of((1, width), F32),
            shape_of((1, hidden_width), F32),
            shape_of((1, width), F32),
        ],
        [
            pltpu.VMEM((width, width), F32),
            pltpu.VMEM((hidden_width, width + 128), F32),
            pltpu.VMEM((hidden_width, width), F32),
            pltpu.VMEM((8, width), F32),
            pltpu.VMEM((width, width), BF16),
            pltpu.VMEM((hidden_width, width), BF16),
            pltpu.VMEM((width, hidden_width), BF16),
            pltpu.VMEM((hidden_width, 128), F32),
            pltpu.VMEM((1, width), F32),
            pltpu.VMEM((1, width), F32),
            pltpu.VMEM((1, hidden_width), F32),
            pltpu.VMEM((width, width), BF16),
            pltpu.VMEM((width, hidden_width), BF16),
            pltpu.VMEM((hidden_width, width), BF16),
            pltpu.VMEM((hidden_width, 4 * length), BF16),
            pltpu.VMEM((hidden_width, 4 * length), BF16),
            pltpu.VMEM((4 * length, width), F32),
            pltpu.VMEM((4 * length, width), F32),
            pltpu.VMEM((4 * length, width), F32),
        ],
        [tokens, cotangent, attended, modulation],
        [late, bias_all],
        pl.CostEstimate(
            flops=6 * rows * width * (width + 2 * hidden_width),
            bytes_accessed=rows * width * 14,
            transcendentals=rows * hidden_width,
        ),
        [core_scalar],
    )

    late_sent, ada_all = lax.optimization_barrier((late_sent, ada_all))
    late_half = late_kept.astype(F32) + hops.swap(late_sent, "rep", 1).astype(F32)
    late_half = late_half.astype(BF16)
    late_parts = lax.all_to_all(late_half, "dp", 0, 0, tiled=True)

    normed, _ = lax.optimization_barrier((normed, late_half))
    tail_rows = up_to(half_rows + 1, 8)
    tokens_grad, grad_mod_one, qkv_kept, qkv_sent, qkv_bias_grad = run_kernel(
        attention_backward_kernel,
        2,
        [shape_of((latents, length, width), BF16), shape_of((latents, 2, width), F32)],
        [
            shape_of((n_dp, tail_rows, width), BF16),
            shape_of((n_dp, tail_rows, width), BF16),
            shape_of((1, 3 * width), F32),
        ],
        [
            pltpu.VMEM((3 * width, width + 128), F32),
            pltpu.VMEM((width, 3 * width), BF16),
            pltpu.VMEM((2, 3 * width, length), BF16),
        ],
        [qkv, lse, grad_attended, normed, tokens, grad_middle, modulation],
        [qkv_full],
        pl.CostEstimate(flops=1, bytes_accessed=1, transcendentals=0),
        [core_scalar],
    )
    qkv_sent, late_parts = lax.optimization_barrier((qkv_sent, late_parts))
    late_sum = jnp.sum(late_parts.astype(F32), axis=0).astype(BF16)
    for bit in hops.bits("rep")[1:]:
        late_sum = late_sum.astype(F32) + hops.swap(late_sum, "rep", bit).astype(F32)
        late_sum = late_sum.astype(BF16)

    qkv_columns = qkv_bias_grad[0]
    bias_blocks = jnp.concatenate(
        [
            jnp.concatenate([qkv_columns[:width], qkv_columns[2 * width :]]).reshape(n_dp, -1),
            out_bias_grad.reshape(n_dp, -1),
            up_bias_grad.reshape(n_dp, -1),
            down_bias_grad.reshape(n_dp, -1),
        ],
        axis=1,
    )
    bias_blocks = jnp.pad(
        bias_blocks[:, None],
        ((0, 0), (half_rows, tail_rows - half_rows - 1), (0, width - cuts[-1])),
    )
    total = qkv_kept.astype(F32) + hops.swap(qkv_sent, "rep", 1).astype(F32) + bias_blocks

    grad_modulation = jnp.concatenate([grad_mod_one, grad_mod_two], axis=1).reshape(
        latents, 6 * width
    )

    own = 6 * width // n_dp
    columns = grad_modulation.reshape(latents, n_dp, own).transpose(1, 0, 2).astype(BF16)
    columns = jnp.pad(columns, ((0, 0), (0, 0), (0, up_to(own, width) - own)))
    columns = columns.reshape((2,) * len(dp_bits) + (latents, width))
    total = total.reshape((2,) * len(dp_bits) + (tail_rows, width))
    axis = len(dp_bits) - 1
    for bit in dp_bits:
        kept, sent = hops.cut(total, "dp", bit, axis)
        column_kept, column_sent = hops.cut(columns, "dp", bit, axis)
        lead = sent.shape[:axis]
        sources = column_sent.shape[axis:-2]
        came = hops.swap(
            jnp.concatenate(
                [sent.astype(BF16), column_sent.reshape(lead + (-1, width))], axis=-2
            ),
            "dp",
            bit,
        )
        total = kept.astype(F32) + came[..., :tail_rows, :].astype(F32)
        column_came = came[..., tail_rows:, :].reshape(lead + sources + (latents, width))
        columns = hops.both(column_kept, column_came, "dp", bit, axis)
        axis -= 1
    columns = columns.reshape(n_dp * latents, width)

    qkv_total = total.astype(BF16)
    for bit in hops.bits("rep")[1:]:
        came = hops.swap(jnp.concatenate([qkv_total, columns]), "rep", bit)
        qkv_total = (qkv_total.astype(F32) + came[:tail_rows].astype(F32)).astype(BF16)
        columns = hops.both(columns, came[tail_rows:], "rep", bit, 0).reshape(-1, width)
    mine = jnp.concatenate([qkv_total, late_sum, columns])
    came = hops.swap(mine, "rep", 1)
    smem = pl.BlockSpec(memory_space=pltpu.SMEM)
    vmem = pl.BlockSpec(memory_space=pltpu.VMEM)
    ada_grad, ada_bias_grad, qkv_owned, up_owned, down_owned, out_owned, *bias_sums = pl.pallas_call(
        functools.partial(finish_kernel, tail_rows=tail_rows),
        in_specs=[smem, vmem, vmem, vmem],
        out_specs=[vmem] * 10,
        out_shape=[
            shape_of((own, width), F32),
            shape_of((1, own), F32),
            shape_of((qkv_rows, width), F32),
            shape_of((up_rows, width), F32),
            shape_of((out_rows, hidden_width), F32),
            shape_of((out_rows, width), F32),
        ]
        + [shape_of((1, part.shape[0]), F32) for part in (qv_bias, out_bias, up_bias, down_bias)],
        compiler_params=pltpu.CompilerParams(vmem_limit_bytes=VMEM_LIMIT),
    )(core_scalar, mine, came, silu_all)
    ada_bias_grad = ada_bias_grad.reshape(-1)

    grad_silu = lax.dot_general(
        grad_modulation,
        ada_all.astype(F32),
        (((1,), (0,)), ((), ())),
        precision=lax.Precision.HIGHEST,
    )
    _, silu_pull = jax.vjp(jax.nn.silu, conditioning)
    condition_grad = silu_pull(grad_silu)[0]

    qv_sum, out_bias_sum, up_bias_sum, down_bias_sum = (part.reshape(-1) for part in bias_sums)
    return (
        output,
        tokens_grad,
        condition_grad,
        ada_grad.T,
        ada_bias_grad,
        qkv_owned.T,
        qv_sum,
        out_owned.T,
        out_bias_sum,
        up_owned.T,
        up_bias_sum,
        down_owned.T,
        down_bias_sum,
    )


def solution(mesh):
    return jax.shard_map(
        functools.partial(body, mesh.shape["dp"], mesh.shape["rep"]),
        mesh=mesh,
        in_specs=(
            P(("dp", "rep"), None, None),
            P(("dp", "rep"), None),
            P(None, "dp"),
            P("dp"),
            P(None, "dp"),
            P("dp"),
            P(None, "dp"),
            P("dp"),
            P(None, "dp"),
            P("dp"),
            P(None, "dp"),
            P("dp"),
            P(("dp", "rep"), None, None),
        ),
        out_specs=(
            P(("dp", "rep"), None, None),
            P(("dp", "rep"), None, None),
            P(("dp", "rep"), None),
            P(None, "dp"),
            P("dp"),
            P(None, "dp"),
            P("dp"),
            P(None, "dp"),
            P("dp"),
            P(None, "dp"),
            P("dp"),
            P(None, "dp"),
            P("dp"),
        ),
        check_vma=False,
    )
```

```python
import functools

import jax
import jax.numpy as jnp
from jax import lax
from jax.experimental import pallas as pl
from jax.experimental.pallas import tpu as pltpu
from jax.sharding import PartitionSpec as P

HEAD_DIM = 64
EPS = 1e-06
GELU_C = 0.7978845608028654
VMEM_LIMIT = 56 * 1024 * 1024
F32 = jnp.float32
BF16 = jnp.bfloat16


def dot_nn(left, right):
    return lax.dot_general(left, right, (((1,), (0,)), ((), ())), preferred_element_type=F32)


def dot_nt(left, right):
    return lax.dot_general(left, right, (((1,), (1,)), ((), ())), preferred_element_type=F32)


def dot_tn(left, right):
    return lax.dot_general(left, right, (((0,), (0,)), ((), ())), preferred_element_type=F32)


def normalise(values):
    average = jnp.mean(values, axis=-1, keepdims=True)
    centred = values - average
    spread = jnp.mean(centred * centred, axis=-1, keepdims=True)
    inverse = lax.rsqrt(spread + EPS)
    return centred * inverse, inverse


def normalise_back(upstream, normal, inverse):
    first = jnp.mean(upstream, axis=-1, keepdims=True)
    second = jnp.mean(upstream * normal, axis=-1, keepdims=True)
    return inverse * (upstream - first - normal * second)


STRIP = 32
GROUP = 3


def beside(*parts):
    return jnp.concatenate(parts, axis=1)


def above(*parts):
    return jnp.concatenate(parts, axis=0)


def strips(extent, size):
    return [slice(low, low + size) for low in range(0, extent, size)]


def head_slices(head):
    low = head * HEAD_DIM
    pair = low - low % (2 * HEAD_DIM)
    return slice(low, low + HEAD_DIM), slice(pair, pair + 2 * HEAD_DIM), low == pair


def interleave(first, second):
    done = 0
    for place, call in enumerate(first):
        call()
        until = (place + 1) * len(second) // len(first)
        for other in second[done:until]:
            other()
        done = until


def in_groups(items, size):
    return [items[low : low + size] for low in range(0, len(items), size)]


def attention_forward_kernel(
    core_ref,
    tokens_ref,
    mod_ref,
    mine_ref,
    came_ref,
    bias_row_ref,
    normed_ref,
    qkv_ref,
    lse_ref,
    attended_ref,
    weight_ref,
    bias_ref,
):
    latents, length, width = tokens_ref.shape
    blank = jnp.zeros((HEAD_DIM, length), BF16)

    @pl.when(pl.program_id(0) == 0)
    def _():
        first = core_ref[0] == 0
        n_dp = mine_ref.shape[0]
        half_rows = weight_ref.shape[0] // (2 * n_dp)
        for owner in range(n_dp):
            mine = mine_ref[owner, :half_rows, :]
            came = came_ref[owner, :half_rows, :]
            low = 2 * owner * half_rows
            weight_ref[low : low + half_rows, :] = jnp.where(first, mine, came)
            weight_ref[low + half_rows : low + 2 * half_rows, :] = jnp.where(first, came, mine)
        bias_ref[...] = jnp.broadcast_to(bias_row_ref[...], (128, 3 * width)).T


    def norm(latent, rows):
        normal, _ = normalise(tokens_ref[latent, rows, :].astype(F32))
        normed = normal * (1.0 + mod_ref[latent, 1:2, :]) + mod_ref[latent, 0:1, :]
        normed_ref[latent, rows, :] = normed.astype(BF16)

    def project(batch, part):
        normed = normed_ref[batch, :, :].reshape(-1, width)
        bias = bias_ref[part, :]
        qkv = dot_nt(weight_ref[part, :], normed) + beside(*([bias] * (normed.shape[0] // 128)))
        qkv = qkv.astype(BF16)
        for place, latent in enumerate(range(batch.start, batch.stop)):
            qkv_ref[latent, part, :] = qkv[:, place * length : (place + 1) * length]

    def norms(batch):
        return [
            functools.partial(norm, latent, rows)
            for latent in range(batch.start, batch.stop)
            for rows in strips(length, STRIP)
        ]

    def projections(batch):
        return [
            functools.partial(project, batch, part) for part in strips(3 * width, width)
        ]

    batches = strips(latents, 2)
    for call in norms(batches[0]):
        call()
    for batch, later in zip(batches[:-1], batches[1:]):
        interleave(projections(batch), norms(later))
    for call in projections(batches[-1]):
        call()
    keys_all = [qkv_ref[latent, width : 2 * width, :].T for latent in range(latents)]

    def scores_of(latent, head):
        own, pair, first = head_slices(head)
        queries = qkv_ref[latent, own, :]
        queries = above(queries, blank) if first else above(blank, queries)
        return dot_nn(keys_all[latent][:, pair], queries)

    def probs_of(latent, head, scores):
        parts = []
        for columns in strips(length, 128):
            strip = scores[:, columns] * HEAD_DIM ** (-0.5)
            highest = jnp.max(strip, axis=0, keepdims=True)
            shifted = jnp.exp(strip - highest)
            total = jnp.sum(shifted, axis=0, keepdims=True)
            parts.append((shifted * (1.0 / total)).astype(BF16))
            lse_ref[latent, head : head + 1, columns] = highest + jnp.log(total)
        return beside(*parts)

    def attend(latent, head, probs):
        own, _, _ = head_slices(head)
        values_in = qkv_ref[latent, 2 * width + own.start : 2 * width + own.stop, :]
        attended_ref[latent, own, :] = dot_nn(values_in, probs).astype(BF16)

    items = [(latent, head) for latent in range(latents) for head in range(width // HEAD_DIM)]
    groups = in_groups(items, GROUP)
    scores = [scores_of(*item) for item in groups[0]]
    previous = []
    for place, group in enumerate(groups):
        later = groups[place + 1] if place + 1 < len(groups) else []
        next_scores = [scores_of(*item) for item in later]
        probs = [probs_of(*item, value) for item, value in zip(group, scores)]
        for item, value in previous:
            attend(*item, value)
        previous = list(zip(group, probs))
        scores = next_scores
    for item, value in previous:
        attend(*item, value)


def by_side(core_ref, side, kept_ref, sent_ref, write):
    @pl.when(core_ref[0] == side)
    def _():
        write(kept_ref)

    @pl.when(core_ref[0] != side)
    def _():
        write(sent_ref)


def feed_kernel(
    core_ref,
    tokens_ref,
    cotangent_ref,
    attended_ref,
    mod_ref,
    late_ref,
    biases_ref,
    output_ref,
    grad_middle_ref,
    grad_attended_ref,
    grad_mod_ref,
    late_kept_ref,
    late_sent_ref,
    out_bias_grad_ref,
    up_bias_grad_ref,
    down_bias_grad_ref,
    out_acc,
    up_acc,
    down_acc,
    bias_acc,
    out_weight_ref,
    up_weight_ref,
    down_weight_ref,
    up_bias_ref,
    out_bias_ref,
    down_bias_ref,
    up_bias_row_ref,
    out_back,
    up_back,
    down_back,
    active_all,
    grad_hidden_all,
    middle_all,
    normal_all,
    branch_all,
    *,
    chunk,
):
    step = pl.program_id(0)
    n_dp = late_ref.shape[0]
    latents, length, width = tokens_ref.shape
    hidden_width = up_weight_ref.shape[0]
    tokens_all = latents * length
    up_rows, out_rows = hidden_width // n_dp, width // n_dp
    out_low = up_rows + out_rows * (hidden_width // width)

    @pl.when(step == 0)
    def _():
        out_acc[...] = jnp.zeros_like(out_acc)
        up_acc[...] = jnp.zeros_like(up_acc)
        down_acc[...] = jnp.zeros_like(down_acc)
        bias_acc[...] = jnp.zeros_like(bias_acc)
        for owner in range(n_dp):
            up_weight_ref[owner * up_rows : (owner + 1) * up_rows, :] = late_ref[owner, :up_rows, :]
            outs = slice(owner * out_rows, (owner + 1) * out_rows)
            for fold in range(hidden_width // width):
                low = up_rows + fold * out_rows
                down_weight_ref[outs, fold * width : (fold + 1) * width] = late_ref[
                    owner, low : low + out_rows, :
                ]
            out_weight_ref[outs, :] = late_ref[owner, out_low:, :]
        out_back[...] = out_weight_ref[...].T
        up_back[...] = up_weight_ref[...].T
        down_back[...] = down_weight_ref[...].T
        low = biases_ref.shape[1] - 2 * out_rows - up_rows
        for ref, size in ((out_bias_ref, out_rows), (up_bias_row_ref, up_rows), (down_bias_ref, out_rows)):
            for owner in range(n_dp):
                ref[0:1, owner * size : (owner + 1) * size] = biases_ref[
                    owner : owner + 1, low : low + size
                ]
            low += size
        up_bias_ref[...] = jnp.broadcast_to(up_bias_row_ref[...], (128, hidden_width)).T

    attended = beside(*[attended_ref[latent] for latent in range(latents)])
    branch_wide = dot_nn(out_weight_ref[...], attended)
    normed_parts = []
    grad_feed_parts = []
    inverses = []
    down_sum = jnp.zeros((1, width), F32)
    for latent in range(latents):
        gate_one = mod_ref[latent, 2:3, :]
        shift_two = mod_ref[latent, 3:4, :]
        scale_two = 1.0 + mod_ref[latent, 4:5, :]
        gate_two = mod_ref[latent, 5:6, :]
        branch_tall = branch_wide[:, latent * length : (latent + 1) * length].T
        for rows in strips(length, STRIP):
            there = slice(latent * length + rows.start, latent * length + rows.stop)
            branch = branch_tall[rows] + out_bias_ref[...]
            branch_all[there, :] = branch
            middle = tokens_ref[latent, rows, :].astype(F32) + gate_one * branch
            middle_all[there, :] = middle
            normal, inverse = normalise(middle)
            normal_all[there, :] = normal
            inverses.append(inverse)
            normed_parts.append((normal * scale_two + shift_two).astype(BF16))
            grad_feed = (cotangent_ref[latent, rows, :].astype(F32) * gate_two).astype(BF16)
            grad_feed_parts.append(grad_feed)
            down_sum += jnp.sum(grad_feed.astype(F32), axis=0, keepdims=True)
    bias_acc[0:1, :] += down_sum
    normed_all = above(*normed_parts)
    grad_feed_all = above(*grad_feed_parts)

    def products(rows):
        return (
            dot_nt(up_weight_ref[rows, :], normed_all),
            dot_nt(down_back[rows, :], grad_feed_all),
        )

    parts = strips(hidden_width, chunk)
    ahead = products(parts[0])
    for place, part in enumerate(parts):
        hidden_wide, grad_wide = ahead
        if place + 1 < len(parts):
            ahead = products(parts[place + 1])
        for rows in strips(chunk, STRIP):
            there = slice(part.start + rows.start, part.start + rows.stop)
            bias = up_bias_ref[there, :]
            bias = beside(bias, bias)
            for columns in strips(tokens_all, 256):
                hidden = hidden_wide[rows, columns] + bias
                square = hidden * hidden
                bent = jnp.tanh(hidden * (GELU_C + (GELU_C * 0.044715) * square))
                half = 0.5 + 0.5 * bent
                active_all[there, columns] = (hidden * half).astype(BF16)
                slope = half + hidden * (0.5 - 0.5 * (bent * bent)) * (
                    GELU_C + (3.0 * GELU_C * 0.044715) * square
                )
                grad_hidden_all[there, columns] = (grad_wide[rows, columns] * slope).astype(BF16)

    feed_wide = dot_nn(down_weight_ref[...], active_all[...])
    grad_normed_wide = dot_nn(up_back[...], grad_hidden_all[...])
    ones = jnp.ones((tokens_all, 128), BF16)
    normed_ones = beside(normed_all, ones)

    def up_product(part):
        up_acc[part, :] += dot_nn(grad_hidden_all[part, :], normed_ones)

    def down_product(part):
        down_acc[part, :] += dot_nn(active_all[part, :], grad_feed_all)

    products_left = [functools.partial(up_product, part) for part in strips(hidden_width, chunk)]
    products_left += [functools.partial(down_product, part) for part in strips(hidden_width, chunk)]
    share = -(-len(products_left) // latents)
    grad_branch_parts = []
    out_sum = jnp.zeros((1, width), F32)
    for latent in range(latents):
        gate_one = mod_ref[latent, 2:3, :]
        scale_two = 1.0 + mod_ref[latent, 4:5, :]
        gate_two = mod_ref[latent, 5:6, :]
        here = slice(latent * length, (latent + 1) * length)
        feed_tall = feed_wide[:, here].T
        grad_normed_tall = grad_normed_wide[:, here].T
        sums = [jnp.zeros((1, width), F32) for _ in range(4)]
        branch_parts = []
        out_sums = []

        def finish_rows(rows):
            there = slice(here.start + rows.start, here.start + rows.stop)
            feed = feed_tall[rows] + down_bias_ref[...]
            grad_normed = grad_normed_tall[rows]
            incoming = cotangent_ref[latent, rows, :].astype(F32)
            normal = normal_all[there, :]
            output_ref[latent, rows, :] = (middle_all[there, :] + gate_two * feed).astype(BF16)
            grad_middle = incoming + normalise_back(
                grad_normed * scale_two, normal, inverses[there.start // STRIP]
            )
            grad_middle_ref[latent, rows, :] = grad_middle
            grad_branch = (grad_middle * gate_one).astype(BF16)
            branch_parts.append(grad_branch)
            terms = (
                grad_middle * branch_all[there, :],
                grad_normed,
                grad_normed * normal,
                incoming * feed,
            )
            for place, term in enumerate(terms):
                sums[place] += jnp.sum(term, axis=0, keepdims=True)
            out_sums.append(jnp.sum(grad_branch.astype(F32), axis=0, keepdims=True))

        interleave(
            [functools.partial(finish_rows, rows) for rows in strips(length, STRIP)],
            products_left[latent * share : (latent + 1) * share],
        )
        grad_branch_parts += branch_parts
        for value in out_sums:
            out_sum += value
        grad_mod_ref[latent] = above(*sums)
    bias_acc[1:2, :] += out_sum
    grad_branch_all = above(*grad_branch_parts)
    grad_attended = dot_nt(out_back[...], grad_branch_all).astype(BF16)
    for latent in range(latents):
        grad_attended_ref[latent] = grad_attended[:, latent * length : (latent + 1) * length]
    out_acc[...] += dot_nn(attended, grad_branch_all)

    @pl.when(step == pl.num_programs(0) - 1)
    def _():
        out_acc[...] = out_acc[...].T
        up_back[...] = down_acc[...].T.astype(BF16)
        folds = hidden_width // width // 2
        out_back_rows = out_rows // 2
        for side in range(2):

            def write(ref, side=side):
                for owner in range(n_dp):
                    ups = owner * up_rows + side * (up_rows // 2)
                    ref[owner, : up_rows // 2, :] = up_acc[
                        ups : ups + up_rows // 2, :width
                    ].astype(BF16)
                    outs = slice(owner * out_rows, (owner + 1) * out_rows)
                    for place in range(folds):
                        low = up_rows // 2 + place * out_rows
                        fold = side * folds + place
                        ref[owner, low : low + out_rows, :] = up_back[
                            outs, fold * width : (fold + 1) * width
                        ]
                    outs = owner * out_rows + side * out_back_rows
                    ref[owner, out_low // 2 :, :] = out_acc[
                        outs : outs + out_back_rows
                    ].astype(BF16)

            by_side(core_ref, side, late_kept_ref, late_sent_ref, write)
        up_bias_grad_ref[...] = up_acc[:, width:].T[0:1, :]
        down_bias_grad_ref[...] = bias_acc[0:1, :]
        out_bias_grad_ref[...] = bias_acc[1:2, :]


def attention_backward_kernel(
    core_ref,
    qkv_ref,
    lse_ref,
    grad_attended_ref,
    normed_ref,
    tokens_ref,
    grad_middle_ref,
    mod_ref,
    weight_ref,
    tokens_grad_ref,
    grad_mod_ref,
    kept_ref,
    sent_ref,
    bias_grad_ref,
    acc,
    weight_back,
    grad_qkv_ref,
):
    step = pl.program_id(0)
    latents, length, width = normed_ref.shape
    blank = jnp.zeros((HEAD_DIM, length), BF16)

    @pl.when(step == 0)
    def _():
        acc[...] = jnp.zeros_like(acc)
        weight_back[...] = weight_ref[...].T

    keys_all = [qkv_ref[latent, width : 2 * width, :].T for latent in range(latents)]
    values_all = [qkv_ref[latent, 2 * width : 3 * width, :].T for latent in range(latents)]

    def products(latent, head):
        own, pair, first = head_slices(head)
        queries = qkv_ref[latent, own, :]
        grad_out = grad_attended_ref[latent, own, :]
        queries = above(queries, blank) if first else above(blank, queries)
        grad_out = above(grad_out, blank) if first else above(blank, grad_out)
        return (
            dot_nn(keys_all[latent][:, pair], queries),
            dot_nn(values_all[latent][:, pair], grad_out),
        )

    def middle_of(latent, head, scores, grad_probs):
        low_parts = []
        grad_parts = []
        for columns in strips(length, 128):
            total = lse_ref[latent, head : head + 1, columns]
            probs = jnp.exp(scores[:, columns] * HEAD_DIM ** (-0.5) - total)
            terms = probs * grad_probs[:, columns]
            row_terms = jnp.sum(terms, axis=0, keepdims=True)
            grad_parts.append((probs * (grad_probs[:, columns] - row_terms)).astype(BF16))
            low_parts.append(probs.astype(BF16))
        return beside(*low_parts), beside(*grad_parts)

    def finish(latent, head, probs, grad_scores):
        own, _, _ = head_slices(head)
        low, high = own.start, own.stop
        queries = qkv_ref[latent, own, :]
        keys_in = qkv_ref[latent, width + low : width + high, :]
        grad_out = grad_attended_ref[latent, own, :]
        scale = HEAD_DIM ** (-0.5)
        grad_qkv_ref[latent, own, :] = (dot_nn(keys_in, grad_scores) * scale).astype(BF16)
        grad_qkv_ref[latent, width + low : width + high, :] = (
            dot_nt(queries, grad_scores) * scale
        ).astype(BF16)
        grad_qkv_ref[latent, 2 * width + low : 2 * width + high, :] = dot_nt(
            grad_out, probs
        ).astype(BF16)

    items = [(latent, head) for latent in range(latents) for head in range(width // HEAD_DIM)]
    groups = in_groups(items, GROUP)
    values = [products(*item) for item in groups[0]]
    previous = []
    for place, group in enumerate(groups):
        later = groups[place + 1] if place + 1 < len(groups) else []
        next_values = [products(*item) for item in later]
        middles = [middle_of(*item, *value) for item, value in zip(group, values)]
        for item, value in previous:
            finish(*item, *value)
        previous = list(zip(group, middles))
        values = next_values
    for item, value in previous:
        finish(*item, *value)

    grad_qkv = beside(*[grad_qkv_ref[latent] for latent in range(latents)])
    normed = normed_ref[...].reshape(latents * length, width)
    grad_normed_wide = dot_nn(weight_back[...], grad_qkv)
    normed_ones = beside(normed, jnp.ones((latents * length, 128), BF16))

    def product(part):
        acc[part, :] += dot_nn(grad_qkv[part, :], normed_ones)

    products_left = [functools.partial(product, part) for part in strips(3 * width, 3 * width // 2)]
    share = -(-len(products_left) // latents)
    for latent in range(latents):
        grad_normed_tall = grad_normed_wide[:, latent * length : (latent + 1) * length].T
        scale_one = 1.0 + mod_ref[latent, 1:2, :]
        sums = [jnp.zeros((1, width), F32) for _ in range(2)]

        def finish_rows(rows):
            normal, inverse = normalise(tokens_ref[latent, rows, :].astype(F32))
            grad_normed = grad_normed_tall[rows]
            sums[0] += jnp.sum(grad_normed, axis=0, keepdims=True)
            sums[1] += jnp.sum(grad_normed * normal, axis=0, keepdims=True)
            back = normalise_back(grad_normed * scale_one, normal, inverse)
            tokens_grad_ref[latent, rows, :] = (grad_middle_ref[latent, rows, :] + back).astype(
                BF16
            )

        interleave(
            [functools.partial(finish_rows, rows) for rows in strips(length, STRIP)],
            products_left[latent * share : (latent + 1) * share],
        )
        grad_mod_ref[latent] = above(*sums)

    @pl.when(step == pl.num_programs(0) - 1)
    def _():
        n_dp, tail_rows, _ = kept_ref.shape
        half_rows = 3 * width // (2 * n_dp)
        for side in range(2):

            def write(ref, side=side):
                for owner in range(n_dp):
                    low = (2 * owner + side) * half_rows
                    rows = acc[low : low + half_rows, :width]
                    rest = jnp.zeros((tail_rows - half_rows, width), F32)
                    ref[owner] = above(rows, rest).astype(BF16)

            by_side(core_ref, side, kept_ref, sent_ref, write)
        bias_grad_ref[...] = acc[:, width:].T[0:1, :]


def finish_kernel(
    core_ref,
    mine_ref,
    came_ref,
    silu_ref,
    ada_ref,
    ada_bias_ref,
    qkv_ref,
    up_ref,
    down_ref,
    out_ref,
    qv_bias_ref,
    out_bias_ref,
    up_bias_ref,
    down_bias_ref,
    *,
    tail_rows,
):
    first = core_ref[0] == 0
    own = ada_ref.shape[0]
    half_rows = qkv_ref.shape[0] // 2
    up_half, out_rows = up_ref.shape[0] // 2, out_ref.shape[0]
    width = out_ref.shape[1]
    folds = down_ref.shape[1] // width // 2
    out_low = tail_rows + up_half + folds * out_rows
    end = out_low + out_rows // 2
    mine = mine_ref[:end, :].astype(F32)
    came = came_ref[:end, :].astype(F32)
    for side in range(2):
        part = jnp.where(first, mine, came) if side == 0 else jnp.where(first, came, mine)
        qkv_ref[side * half_rows : (side + 1) * half_rows, :] = part[:half_rows]
        up_ref[side * up_half : (side + 1) * up_half, :] = part[tail_rows : tail_rows + up_half]
        for place in range(folds):
            low = tail_rows + up_half + place * out_rows
            columns = (side * folds + place) * width
            down_ref[:, columns : columns + width] = part[low : low + out_rows]
        out_ref[side * (out_rows // 2) : (side + 1) * (out_rows // 2), :] = part[out_low:]
    biases = mine[half_rows : half_rows + 1] + came[half_rows : half_rows + 1]
    low = 0
    for ref in (qv_bias_ref, out_bias_ref, up_bias_ref, down_bias_ref):
        ref[...] = biases[:, low : low + ref.shape[1]]
        low += ref.shape[1]
    mine = mine_ref[end:, :]
    came = came_ref[end:, :]
    columns = above(jnp.where(first, mine, came), jnp.where(first, came, mine))
    ada_ref[...] = dot_tn(columns, silu_ref[...])[:own]
    ada_bias_ref[...] = jnp.sum(columns.astype(F32), axis=0, keepdims=True)[:, :own]


def each(shape, count):
    zeros = (0,) * (len(shape) - 1)
    return pl.BlockSpec((count,) + tuple(shape[1:]), lambda step: (step,) + zeros)


def whole(shape):
    zeros = (0,) * len(shape)
    return pl.BlockSpec(tuple(shape), lambda step: zeros)


def run_kernel(kernel, count, streamed_out, fixed_out, scratch, streamed, fixed, cost, scalars=()):
    return pl.pallas_call(
        kernel,
        grid=(streamed[0].shape[0] // count,),
        in_specs=[pl.BlockSpec(memory_space=pltpu.SMEM)] * len(scalars)
        + [each(item.shape, count) for item in streamed]
        + [whole(item.shape) for item in fixed],
        out_specs=[each(item.shape, count) for item in streamed_out]
        + [whole(item.shape) for item in fixed_out],
        out_shape=list(streamed_out) + list(fixed_out),
        scratch_shapes=scratch,
        compiler_params=pltpu.CompilerParams(
            dimension_semantics=("arbitrary",), vmem_limit_bytes=VMEM_LIMIT
        ),
        cost_estimate=cost,
    )(*scalars, *streamed, *fixed)


def shape_of(dims, kind):
    return jax.ShapeDtypeStruct(tuple(dims), kind)


AXES = ("dp", "rep")


class Hops:
    def __init__(self, n_dp, n_rep):
        self.sizes = {"dp": n_dp, "rep": n_rep}
        self.place = {name: lax.axis_index(name) for name in AXES}

    def bits(self, name):
        return [1 << shift for shift in range(self.sizes[name].bit_length() - 1)]

    def mine(self, name, bit):
        return (self.place[name] // bit) % 2

    def swap(self, value, name, bit):
        n_dp, n_rep = self.sizes["dp"], self.sizes["rep"]
        flip_dp, flip_rep = (bit, 0) if name == "dp" else (0, bit)
        pairs = [
            (d * n_rep + r, (d ^ flip_dp) * n_rep + (r ^ flip_rep))
            for d in range(n_dp)
            for r in range(n_rep)
        ]
        return lax.ppermute(value, AXES, pairs)

    def both(self, kept, came, name, bit, axis):
        upper = self.mine(name, bit) == 1
        return jnp.stack(
            [jnp.where(upper, came, kept), jnp.where(upper, kept, came)], axis=axis
        )

    def cut(self, value, name, bit, axis):
        here = self.mine(name, bit)
        return (
            lax.dynamic_index_in_dim(value, here, axis, keepdims=False),
            lax.dynamic_index_in_dim(value, 1 - here, axis, keepdims=False),
        )


def pad_rows(values, count):
    return jnp.pad(values, ((0, 0),) * (values.ndim - 2) + ((0, count - values.shape[-2]), (0, 0)))


def up_to(count, multiple):
    return -(-count // multiple) * multiple


def body(
    n_dp,
    n_rep,
    tokens,
    conditioning,
    ada_weight,
    ada_bias,
    qkv_weight,
    qv_bias,
    out_weight,
    out_bias,
    up_weight,
    up_bias,
    down_weight,
    down_bias,
    cotangent,
):
    latents, length, width = tokens.shape
    hidden_width = up_weight.shape[1] * n_dp
    heads = width // HEAD_DIM
    rows = latents * length
    hops = Hops(n_dp, n_rep)
    dp_bits = hops.bits("dp")
    folds = hidden_width // width

    up_rows, out_rows = up_weight.shape[1], out_weight.shape[1]
    down_shard = down_weight.T.reshape(out_rows, folds, width).transpose(1, 0, 2)
    late_shard = jnp.concatenate(
        [up_weight.T, down_shard.reshape(folds * out_rows, width), out_weight.T]
    )
    silu_low = jax.nn.silu(conditioning).astype(BF16)
    qkv_rows = qkv_weight.shape[1]
    half_rows = qkv_rows // 2
    core = hops.mine("rep", 1)
    bias_shard = jnp.concatenate([qv_bias, out_bias, up_bias, down_bias])
    bias_rows = 2
    front = jnp.concatenate(
        [
            lax.dynamic_slice_in_dim(qkv_weight.T, core * half_rows, half_rows, axis=0),
            silu_low,
            jnp.pad(bias_shard, (0, width - bias_shard.shape[0]))[None],
            jnp.pad(ada_bias, (0, width - ada_bias.shape[0]))[None],
        ]
    )
    front = pad_rows(front, up_to(front.shape[0], 8))
    late = lax.all_gather(late_shard, "dp", axis=0)
    ada_shard, _ = lax.optimization_barrier((ada_weight.T, late))
    ada_all = lax.all_gather(ada_shard, "dp", axis=0, tiled=True)
    ada_pair = hops.both(ada_weight.T, hops.swap(ada_weight.T, "dp", 1), "dp", 1, 0)
    high_bits = dp_bits[:0:-1]
    for done, bit in enumerate(high_bits):
        front = hops.both(front, hops.swap(front, "dp", bit), "dp", bit, done)

    silu_part = front[..., half_rows : half_rows + latents, :].reshape(-1, width)
    mod = dot_nt(silu_part, ada_pair.reshape(-1, width))
    mod = mod.reshape((2,) * len(high_bits) + (latents, -1))
    for done, bit in enumerate(high_bits):
        kept, sent = hops.cut(mod, "dp", bit, done)
        mod = hops.both(kept, hops.swap(sent, "dp", bit), "dp", bit, done)
    mod = mod.reshape(n_dp // 2, latents, -1).transpose(1, 0, 2).reshape(latents, -1)

    front = hops.both(front, hops.swap(front, "dp", 1), "dp", 1, len(high_bits))
    front = front.reshape(n_dp, -1, width)
    mine = front[:, : half_rows + latents]
    came = hops.swap(mine, "rep", 1)
    silu_all = hops.both(mine[:, half_rows:], came[:, half_rows:], "rep", 1, 0)
    for bit in hops.bits("rep")[1:]:
        silu_all = hops.both(silu_all, hops.swap(silu_all, "rep", bit), "rep", bit, 0)
    silu_all = silu_all.reshape(n_rep // 2, 2, n_dp * latents, width).transpose(1, 0, 2, 3)
    silu_all = silu_all.reshape(-1, width)

    bias_all = front[:, half_rows + latents].astype(F32)
    cuts = [0]
    for part in (qv_bias, out_bias, up_bias, down_bias):
        cuts.append(cuts[-1] + part.shape[0])
    bias_all = bias_all[:, : cuts[-1]]
    qv_full = bias_all[:, : cuts[1]].reshape(1, -1)
    ada_full = front[:, half_rows + latents + 1, : ada_bias.shape[0]].astype(F32).reshape(1, -1)
    qkv_bias = jnp.concatenate(
        [qv_full[:, :width], jnp.zeros((1, width), F32), qv_full[:, width:]], axis=1
    )

    modulation = (mod + ada_full).reshape(latents, 6, width)

    core_scalar = core.astype(jnp.int32).reshape(1)
    normed, qkv, lse, attended, qkv_full = run_kernel(
        attention_forward_kernel,
        4,
        [
            shape_of((latents, length, width), BF16),
            shape_of((latents, 3 * width, length), BF16),
            shape_of((latents, 8 * ((heads + 7) // 8), length), F32),
            shape_of((latents, width, length), BF16),
        ],
        [shape_of((3 * width, width), BF16)],
        [pltpu.VMEM((3 * width, 128), F32)],
        [tokens, modulation],
        [mine, came, qkv_bias],
        pl.CostEstimate(
            flops=2 * rows * width * (3 * width + 2 * length),
            bytes_accessed=rows * width * 12,
            transcendentals=rows * heads * length,
        ),
        [core_scalar],
    )

    attended, silu_all = lax.optimization_barrier((attended, silu_all))
    (
        output,
        grad_middle,
        grad_attended,
        grad_mod_two,
        late_kept,
        late_sent,
        out_bias_grad,
        up_bias_grad,
        down_bias_grad,
    ) = run_kernel(
        functools.partial(feed_kernel, chunk=768),
        4,
        [
            shape_of((latents, length, width), BF16),
            shape_of((latents, length, width), F32),
            shape_of((latents, width, length), BF16),
            shape_of((latents, 4, width), F32),
        ],
        [
            shape_of((n_dp, late.shape[1] // 2, width), BF16),
            shape_of((n_dp, late.shape[1] // 2, width), BF16),
            shape_of((1, width), F32),
            shape_of((1, hidden_width), F32),
            shape_of((1, width), F32),
        ],
        [
            pltpu.VMEM((width, width), F32),
            pltpu.VMEM((hidden_width, width + 128), F32),
            pltpu.VMEM((hidden_width, width), F32),
            pltpu.VMEM((8, width), F32),
            pltpu.VMEM((width, width), BF16),
            pltpu.VMEM((hidden_width, width), BF16),
            pltpu.VMEM((width, hidden_width), BF16),
            pltpu.VMEM((hidden_width, 128), F32),
            pltpu.VMEM((1, width), F32),
            pltpu.VMEM((1, width), F32),
            pltpu.VMEM((1, hidden_width), F32),
            pltpu.VMEM((width, width), BF16),
            pltpu.VMEM((width, hidden_width), BF16),
            pltpu.VMEM((hidden_width, width), BF16),
            pltpu.VMEM((hidden_width, 4 * length), BF16),
            pltpu.VMEM((hidden_width, 4 * length), BF16),
            pltpu.VMEM((4 * length, width), F32),
            pltpu.VMEM((4 * length, width), F32),
            pltpu.VMEM((4 * length, width), F32),
        ],
        [tokens, cotangent, attended, modulation],
        [late, bias_all],
        pl.CostEstimate(
            flops=6 * rows * width * (width + 2 * hidden_width),
            bytes_accessed=rows * width * 14,
            transcendentals=rows * hidden_width,
        ),
        [core_scalar],
    )

    late_sent, ada_all = lax.optimization_barrier((late_sent, ada_all))
    late_half = late_kept.astype(F32) + hops.swap(late_sent, "rep", 1).astype(F32)
    late_half = late_half.astype(BF16)
    late_parts = lax.all_to_all(late_half, "dp", 0, 0, tiled=True)

    normed, _ = lax.optimization_barrier((normed, late_half))
    tail_rows = up_to(half_rows + 1, 8)
    tokens_grad, grad_mod_one, qkv_kept, qkv_sent, qkv_bias_grad = run_kernel(
        attention_backward_kernel,
        2,
        [shape_of((latents, length, width), BF16), shape_of((latents, 2, width), F32)],
        [
            shape_of((n_dp, tail_rows, width), BF16),
            shape_of((n_dp, tail_rows, width), BF16),
            shape_of((1, 3 * width), F32),
        ],
        [
            pltpu.VMEM((3 * width, width + 128), F32),
            pltpu.VMEM((width, 3 * width), BF16),
            pltpu.VMEM((2, 3 * width, length), BF16),
        ],
        [qkv, lse, grad_attended, normed, tokens, grad_middle, modulation],
        [qkv_full],
        pl.CostEstimate(flops=1, bytes_accessed=1, transcendentals=0),
        [core_scalar],
    )
    qkv_sent, late_parts = lax.optimization_barrier((qkv_sent, late_parts))
    late_sum = jnp.sum(late_parts.astype(F32), axis=0).astype(BF16)
    for bit in hops.bits("rep")[1:]:
        late_sum = late_sum.astype(F32) + hops.swap(late_sum, "rep", bit).astype(F32)
        late_sum = late_sum.astype(BF16)

    qkv_columns = qkv_bias_grad[0]
    bias_blocks = jnp.concatenate(
        [
            jnp.concatenate([qkv_columns[:width], qkv_columns[2 * width :]]).reshape(n_dp, -1),
            out_bias_grad.reshape(n_dp, -1),
            up_bias_grad.reshape(n_dp, -1),
            down_bias_grad.reshape(n_dp, -1),
        ],
        axis=1,
    )
    bias_blocks = jnp.pad(
        bias_blocks[:, None],
        ((0, 0), (half_rows, tail_rows - half_rows - 1), (0, width - cuts[-1])),
    )
    total = qkv_kept.astype(F32) + hops.swap(qkv_sent, "rep", 1).astype(F32) + bias_blocks

    grad_modulation = jnp.concatenate([grad_mod_one, grad_mod_two], axis=1).reshape(
        latents, 6 * width
    )

    own = 6 * width // n_dp
    columns = grad_modulation.reshape(latents, n_dp, own).transpose(1, 0, 2).astype(BF16)
    columns = jnp.pad(columns, ((0, 0), (0, 0), (0, up_to(own, width) - own)))
    columns = columns.reshape((2,) * len(dp_bits) + (latents, width))
    total = total.reshape((2,) * len(dp_bits) + (tail_rows, width))
    axis = len(dp_bits) - 1
    for bit in dp_bits:
        kept, sent = hops.cut(total, "dp", bit, axis)
        column_kept, column_sent = hops.cut(columns, "dp", bit, axis)
        lead = sent.shape[:axis]
        sources = column_sent.shape[axis:-2]
        came = hops.swap(
            jnp.concatenate(
                [sent.astype(BF16), column_sent.reshape(lead + (-1, width))], axis=-2
            ),
            "dp",
            bit,
        )
        total = kept.astype(F32) + came[..., :tail_rows, :].astype(F32)
        column_came = came[..., tail_rows:, :].reshape(lead + sources + (latents, width))
        columns = hops.both(column_kept, column_came, "dp", bit, axis)
        axis -= 1
    columns = columns.reshape(n_dp * latents, width)

    qkv_total = total.astype(BF16)
    for bit in hops.bits("rep")[1:]:
        came = hops.swap(jnp.concatenate([qkv_total, columns]), "rep", bit)
        qkv_total = (qkv_total.astype(F32) + came[:tail_rows].astype(F32)).astype(BF16)
        columns = hops.both(columns, came[tail_rows:], "rep", bit, 0).reshape(-1, width)
    mine = jnp.concatenate([qkv_total, late_sum, columns])
    came = hops.swap(mine, "rep", 1)
    smem = pl.BlockSpec(memory_space=pltpu.SMEM)
    vmem = pl.BlockSpec(memory_space=pltpu.VMEM)
    ada_grad, ada_bias_grad, qkv_owned, up_owned, down_owned, out_owned, *bias_sums = pl.pallas_call(
        functools.partial(finish_kernel, tail_rows=tail_rows),
        in_specs=[smem, vmem, vmem, vmem],
        out_specs=[vmem] * 10,
        out_shape=[
            shape_of((own, width), F32),
            shape_of((1, own), F32),
            shape_of((qkv_rows, width), F32),
            shape_of((up_rows, width), F32),
            shape_of((out_rows, hidden_width), F32),
            shape_of((out_rows, width), F32),
        ]
        + [shape_of((1, part.shape[0]), F32) for part in (qv_bias, out_bias, up_bias, down_bias)],
        compiler_params=pltpu.CompilerParams(vmem_limit_bytes=VMEM_LIMIT),
    )(core_scalar, mine, came, silu_all)
    ada_bias_grad = ada_bias_grad.reshape(-1)

    grad_silu = lax.dot_general(
        grad_modulation,
        ada_all.astype(F32),
        (((1,), (0,)), ((), ())),
        precision=lax.Precision.HIGHEST,
    )
    _, silu_pull = jax.vjp(jax.nn.silu, conditioning)
    condition_grad = silu_pull(grad_silu)[0]

    qv_sum, out_bias_sum, up_bias_sum, down_bias_sum = (part.reshape(-1) for part in bias_sums)
    return (
        output,
        tokens_grad,
        condition_grad,
        ada_grad.T,
        ada_bias_grad,
        qkv_owned.T,
        qv_sum,
        out_owned.T,
        out_bias_sum,
        up_owned.T,
        up_bias_sum,
        down_owned.T,
        down_bias_sum,
    )


def solution(mesh):
    return jax.shard_map(
        functools.partial(body, mesh.shape["dp"], mesh.shape["rep"]),
        mesh=mesh,
        in_specs=(
            P(("dp", "rep"), None, None),
            P(("dp", "rep"), None),
            P(None, "dp"),
            P("dp"),
            P(None, "dp"),
            P("dp"),
            P(None, "dp"),
            P("dp"),
            P(None, "dp"),
            P("dp"),
            P(None, "dp"),
            P("dp"),
            P(("dp", "rep"), None, None),
        ),
        out_specs=(
            P(("dp", "rep"), None, None),
            P(("dp", "rep"), None, None),
            P(("dp", "rep"), None),
            P(None, "dp"),
            P("dp"),
            P(None, "dp"),
            P("dp"),
            P(None, "dp"),
            P("dp"),
            P(None, "dp"),
            P("dp"),
            P(None, "dp"),
            P("dp"),
        ),
        check_vma=False,
    )
```
